32 devices in a mesh: replica: 2 (over core), shard: 16 (over z, y, x).
Axes of the slice: x: 2, y: 2, z: 4, core: 2. Of those that a mesh axis runs over, the one named last changes fastest.
Arguments:
- features: bfloat16 [64, 544, 512], P(('replica', 'shard')), may hold values from -20 to 20
- frame_times: int32 [64, 544], P(('replica', 'shard')), may hold values from 0 to 1692, as said below
- cotangent: bfloat16 [64, 544, 512], P(('replica', 'shard')), may hold values from -20 to 20
- vectors: bfloat16 [9, 512], P(None, 'shard'), may hold values from 0.25 to 1.75
- first_up: bfloat16 [512, 2048], P('shard'), may hold values from -0.25 to 0.25
- first_down: bfloat16 [2048, 512], P('shard'), may hold values from -0.25 to 0.25
- query_key_value: bfloat16 [512, 1536], P('shard'), may hold values from -0.25 to 0.25
- place_weight: bfloat16 [512, 512], P('shard'), may hold values from -0.25 to 0.25
- out_weight: bfloat16 [512, 512], P('shard'), may hold values from -1 to 1
- point_glu: bfloat16 [512, 1024], P('shard'), may hold values from -0.25 to 0.25
- depth_taps: bfloat16 [31, 512], P(None, 'shard'), may hold values from -1 to 1
- point_out: bfloat16 [512, 512], P('shard'), may hold values from -0.5 to 0.5
- second_up: bfloat16 [512, 2048], P('shard'), may hold values from -0.25 to 0.25
- second_down: bfloat16 [2048, 512], P('shard'), may hold values from -0.25 to 0.25
Outputs:
- output: bfloat16 [64, 544, 512], P(('replica', 'shard'))
- grad_features: bfloat16 [64, 544, 512], P(('replica', 'shard'))
- grad_vectors: float32 [9, 512], P(None, 'shard')
- grad_first_up: float32 [512, 2048], P('shard')
- grad_first_down: float32 [2048, 512], P('shard')
- grad_query_key_value: float32 [512, 1536], P('shard')
- grad_place_weight: float32 [512, 512], P('shard')
- grad_out_weight: float32 [512, 512], P('shard')
- grad_point_glu: float32 [512, 1024], P('shard')
- grad_depth_taps: float32 [31, 512], P(None, 'shard')
- grad_point_out: float32 [512, 512], P('shard')
- grad_second_up: float32 [512, 2048], P('shard')
- grad_second_down: float32 [2048, 512], P('shard')
The draws below stay inside these ranges and needn't reach their ends.
Inputs may be any that keep to these rules, and one draw needn't show every extreme that they name: `frame_times`: within a clip the frame times rise by 1 to 3 from each token to the next.
All inputs are finite; a program needn't handle non-finite values.
Results may differ from the reference program's by a relative error of at most 0.04.
Values may be sent and summed in bfloat16 or wider, within the bound.
A program may use at most 256 MiB of HBM per device.

```python
import math
import jax
import jax.numpy as jnp
from jax import lax

D = 512
HEADS = 8
HEAD_DIM = 64
FF = 2048
KERNEL = 31
NVEC = 9
CLIP_LEN = 544
HALF = 256
CLIPS = 64


def drifting(key, ramp_top):
    noise_key, common_key = jax.random.split(key)
    full_shape = (CLIPS, CLIP_LEN, D)
    noise = jax.random.normal(noise_key, full_shape, jnp.float32)
    common = jax.random.normal(common_key, (D,), jnp.float32)
    top_level = ramp_top
    ramp = jnp.arange(CLIPS, dtype=jnp.float32) * (top_level / max(CLIPS - 1, 1))
    return noise + ramp[:, None, None] * common[None, None, :]


def draw_features(key, part):
    return drifting(jax.random.fold_in(key, 11), 2.0).astype(jnp.bfloat16)


def draw_cotangent(key, part):
    return drifting(jax.random.fold_in(key, 23), 2.0).astype(jnp.bfloat16)


def draw_frame_times(key, part):
    start_key, step_key = jax.random.split(jax.random.fold_in(key, 37))
    starts = jax.random.randint(start_key, (CLIPS, 1), 0, 64, dtype=jnp.int32)
    starts = starts.at[0, 0].set(0).at[CLIPS - 1, 0].set(63)
    steps_taken = jax.random.randint(step_key, (CLIPS, CLIP_LEN), 1, 4, dtype=jnp.int32)
    steps_taken = steps_taken.at[CLIPS - 1].set(3)
    return (starts + jnp.cumsum(steps_taken, axis=1) - steps_taken[:, :1]).astype(jnp.int32)


def steps_of(stream_key, dims, shards, low, largest):
    gain = 1.0
    for axis_at, shards_of in shards:
        draws = jax.random.uniform(jax.random.fold_in(jax.random.fold_in(stream_key, 6), axis_at), (shards_of,), jnp.float32, low / len(shards), largest / len(shards))
        gain = gain * jnp.repeat(jnp.exp(draws), dims[axis_at] // shards_of).reshape((-1,) + (1,) * (len(dims) - 1 - axis_at))
    return gain


def normal_values(key, shape, scale, bound, cuts=(), held_as=jnp.bfloat16):
    array = jax.random.normal(key, shape, jnp.float32) * scale
    if len(cuts) > 0:
        array = steps_of(key, shape, cuts, -0.22, 0.18) * array
    return jnp.clip(array, min=-bound, max=bound).astype(held_as)


def setup_inputs(seed: int = 0) -> dict:
    splits = jax.random.split(jax.random.key(seed), 15)
    return {
        "features": draw_features(jax.random.fold_in(splits[14], 71), 0),
        "frame_times": draw_frame_times(jax.random.fold_in(splits[14], 71), 0),
        "cotangent": draw_cotangent(jax.random.fold_in(splits[14], 71), 0),
        "vectors": jnp.clip(1.0 + 0.15 * jax.random.normal(splits[3], (NVEC, D), jnp.float32), 0.25, 1.75).astype(jnp.bfloat16),
        "first_up": normal_values(splits[4], (D, FF), D ** -0.5, 0.25, ((0, 16),)),
        "first_down": normal_values(splits[5], (FF, D), (FF // 4) ** -0.5, 0.25, ((0, 16),)),
        "query_key_value": normal_values(splits[6], (D, 3 * D), D ** -0.5, 0.25, ((0, 16),)),
        "place_weight": normal_values(splits[7], (D, D), D ** -0.5, 0.25, ((0, 16),)),
        "out_weight": normal_values(splits[8], (D, D), (D // 16) ** -0.5, 1.0, ((0, 16),)),
        "point_glu": normal_values(splits[9], (D, 2 * D), D ** -0.5, 0.25, ((0, 16),)),
        "depth_taps": normal_values(splits[10], (KERNEL, D), KERNEL ** -0.5, 1.0, ((1, 16),)),
        "point_out": normal_values(splits[11], (D, D), (D // 4) ** -0.5, 0.5, ((0, 16),)),
        "second_up": normal_values(splits[12], (D, FF), D ** -0.5, 0.25, ((0, 16),)),
        "second_down": normal_values(splits[13], (FF, D), (FF // 4) ** -0.5, 0.25, ((0, 16),)),
    }


epsilon = 1e-05
highest = lax.Precision.HIGHEST

@jax.custom_vjp
def low(v):
    return lax.optimization_barrier(v.astype(jnp.bfloat16)).astype(jnp.float32)

@jax.custom_vjp
def low_back(v):
    return v

def low_keep(v):
    return (low(v), None)

def low_pass(kept, grad):
    return (grad,)

def back_keep(v):
    return (v, None)

def back_low(kept, grad):
    return (low(grad),)
low.defvjp(low_keep, low_pass)
low_back.defvjp(back_keep, back_low)

def normalize(values, gain_row):
    center = values - lax.optimization_barrier(jnp.mean(values, axis=-1, keepdims=True))
    spread = lax.optimization_barrier(jnp.mean(center * center, axis=-1, keepdims=True))
    return center * lax.rsqrt(spread + epsilon) * gain_row

def swish_act(values):
    return values * jax.nn.sigmoid(values)

def wave_table(frame_pos):
    half_width = D // 2
    frequency = jnp.exp(jnp.arange(half_width, dtype=jnp.float32) * (-math.log(10000.0) / half_width))
    angles = frame_pos.astype(jnp.float32)[:, None] * frequency[None, :]
    return (jnp.sin(angles), jnp.cos(angles))

def depthwise(gated_rows, tap_weights):
    tap_count = tap_weights.shape[0]
    reach_left = tap_count // 2
    clip_length = gated_rows.shape[1]
    padded = jnp.pad(gated_rows, ((0, 0), (reach_left, tap_count - 1 - reach_left), (0, 0)))
    running_sum = jnp.zeros_like(gated_rows)
    for offset in range(tap_count):
        running_sum = running_sum + tap_weights[offset] * padded[:, offset:offset + clip_length]
    return running_sum

def gated_conv(mixed_rows, tap_weights):
    half_width = mixed_rows.shape[-1] // 2
    gated_rows = mixed_rows[..., :half_width] * jax.nn.sigmoid(mixed_rows[..., half_width:])
    return depthwise(gated_rows, tap_weights)

def project(values, weight):
    return low_back(jnp.dot(low(values), weight, precision=highest))

def feed_forward(values, gain_row, up_weight, down_weight):
    return project(swish_act(project(normalize(values, gain_row), up_weight)), down_weight)

def attend_clip(joint_rows, frame_pos, u_bias, v_bias, place3):
    clip_length = joint_rows.shape[0]
    head_shape = (clip_length, HEADS, HEAD_DIM)
    query = joint_rows[:, :D]
    query_u = low((query + u_bias).reshape(head_shape))
    query_v = low((query + v_bias).reshape(head_shape))
    key_low = low(joint_rows[:, D:2 * D].reshape(head_shape))
    value_low = low(joint_rows[:, 2 * D:].reshape(head_shape))
    sine_rows, cosines = wave_table(frame_pos)
    raw_place = low_back(jnp.einsum('ihd,ehd->hie', query_v, place3, precision=highest))
    part_sin = raw_place[..., :HALF]
    part_cos = raw_place[..., HALF:]
    coeff = low(jnp.concatenate([part_sin * sine_rows + part_cos * cosines, part_cos * sine_rows - part_sin * cosines], axis=-1))
    basis = low(jnp.concatenate([cosines, sine_rows], axis=-1))
    content = jnp.einsum('ihd,jhd->hij', query_u, key_low, precision=highest)
    placed = jnp.einsum('hie,je->hij', coeff, basis, precision=highest)
    scores = low_back((content + placed) * (1.0 / math.sqrt(HEAD_DIM)))
    prob_values = low(jax.nn.softmax(scores, axis=-1))
    context = low_back(jnp.einsum('hij,jhd->ihd', prob_values, value_low, precision=highest))
    return context.reshape(clip_length, D)

def reference(features, frame_times, cotangent, vectors, first_up, first_down, query_key_value, place_weight, out_weight, point_glu, depth_taps, point_out, second_up, second_down):

    def forward(inputs, gain_rows, up_one, down_one, joint_weight, place_full, out_full, glu_full, tap_weights, point_full, up_two, down_two):
        after_first = inputs + 0.5 * feed_forward(inputs, gain_rows[0], up_one, down_one)
        joint_rows = project(normalize(after_first, gain_rows[1]), joint_weight)
        place3 = place_full.reshape(D, HEADS, HEAD_DIM)

        def one_clip(clip_item):
            return attend_clip(clip_item[0], clip_item[1], gain_rows[2], gain_rows[3], place3)
        context = lax.map(jax.checkpoint(one_clip), (joint_rows, frame_times))
        after_attend = after_first + project(context, out_full)
        mixed_rows = project(normalize(after_attend, gain_rows[4]), glu_full)
        conv_rows = gated_conv(mixed_rows, tap_weights)
        channel_mean = lax.optimization_barrier(jnp.mean(conv_rows, axis=(0, 1)))
        centered = conv_rows - channel_mean
        variance = lax.optimization_barrier(jnp.mean(centered * centered, axis=(0, 1)))
        shaped = centered * lax.rsqrt(variance + epsilon) * gain_rows[5] + gain_rows[6]
        after_conv = after_attend + project(swish_act(shaped), point_full)
        after_second = after_conv + 0.5 * feed_forward(after_conv, gain_rows[7], up_two, down_two)
        return normalize(after_second, gain_rows[8])
    output, pull = jax.vjp(forward, features.astype(jnp.float32), vectors.astype(jnp.float32), first_up.astype(jnp.float32), first_down.astype(jnp.float32), query_key_value.astype(jnp.float32), place_weight.astype(jnp.float32), out_weight.astype(jnp.float32), point_glu.astype(jnp.float32), depth_taps.astype(jnp.float32), point_out.astype(jnp.float32), second_up.astype(jnp.float32), second_down.astype(jnp.float32))
    grads = pull(cotangent.astype(jnp.float32))
    return (output.astype(jnp.bfloat16), grads[0].astype(jnp.bfloat16), grads[1], grads[2], grads[3], grads[4], grads[5], grads[6], grads[7], grads[8], grads[9], grads[10], grads[11])
```

```python
import functools
import math

import jax
import jax.numpy as jnp
from jax import lax
from jax.experimental import pallas as pl
from jax.experimental.pallas import tpu as pltpu
from jax.sharding import PartitionSpec as P

HEADS = 8
HEAD_DIM = 64


epsilon = 1e-05


def normalize(values, gain_row):
    center = values - jnp.mean(values, axis=-1, keepdims=True)
    spread = jnp.mean(center * center, axis=-1, keepdims=True)
    return center * lax.rsqrt(spread + epsilon) * gain_row


def normalize_back(values, gain_row, grad_normed):
    pull = jax.vjp(normalize, values, gain_row)[1]
    return pull(grad_normed)


def swish_act(values):
    return values * jax.nn.sigmoid(values)


def swish_slope(values):
    sigmoid = jax.nn.sigmoid(values)
    return sigmoid * (1.0 + values * (1.0 - sigmoid))


def wave_table(frame_pos, model_width):
    half_width = model_width // 2
    frequency = jnp.exp(
        jnp.arange(half_width, dtype=jnp.float32) * (-math.log(10000.0) / half_width)
    )
    angles = frame_pos.astype(jnp.float32)[:, None] * frequency[None, :]
    return (jnp.sin(angles), jnp.cos(angles))


def product(left_side, right_side):
    return jnp.dot(left_side, right_side, preferred_element_type=jnp.float32)


def product_left(left_side, right_side):
    return lax.dot_general(
        left_side, right_side, (((0,), (0,)), ((), ())), preferred_element_type=jnp.float32
    )


def product_right(left_side, right_side):
    return lax.dot_general(
        left_side, right_side, (((1,), (1,)), ((), ())), preferred_element_type=jnp.float32
    )


def feed_forward(inputs, gain_row, up_full, down_full):
    normed_low = normalize(inputs, gain_row).astype(jnp.bfloat16)
    hidden = product(normed_low, up_full)
    active_low = swish_act(hidden).astype(jnp.bfloat16)
    return (product(active_low, down_full), (normed_low, hidden, active_low))


def feed_back(grad_stream, inputs, gain_row, up_full, down_full, kept_values):
    normed_low, hidden, active_low = kept_values
    grad_low = (0.5 * grad_stream).astype(jnp.bfloat16)
    grad_down = product_left(active_low, grad_low)
    grad_hidden = (product_right(grad_low, down_full) * swish_slope(hidden)).astype(jnp.bfloat16)
    grad_up = product_left(normed_low, grad_hidden)
    grad_normed = product_right(grad_hidden, up_full)
    grad_extra, grad_gain = normalize_back(inputs, gain_row, grad_normed)
    return (grad_stream + grad_extra, grad_gain, grad_up, grad_down)


def head_probs(query_u, query_v, key_low, place_head, sine_rows, cosines, basis_low):
    raw_place = product_right(query_v, place_head)
    half_width = raw_place.shape[-1] // 2
    part_sin = raw_place[:, :half_width]
    part_cos = raw_place[:, half_width:]
    coeff_low = jnp.concatenate(
        [part_sin * sine_rows + part_cos * cosines, part_cos * sine_rows - part_sin * cosines],
        axis=-1,
    ).astype(jnp.bfloat16)
    scores = product_right(query_u, key_low) + product_right(coeff_low, basis_low)
    scores = scores * (1.0 / math.sqrt(HEAD_DIM))
    row_peak = jnp.max(scores, axis=-1, keepdims=True)
    raised = jnp.exp(scores - row_peak)
    return raised * (1.0 / jnp.sum(raised, axis=-1, keepdims=True))


def forward_kernel(qu_ref, qv_ref, key_ref, value_ref, place_ref, sine_ref, cos_ref, out_ref):
    sine_rows = sine_ref[0]
    cosines = cos_ref[0]
    basis_low = jnp.concatenate([cosines, sine_rows], axis=-1).astype(jnp.bfloat16)
    merged = []
    for at in range(0, out_ref.shape[-1], HEAD_DIM):
        cols = slice(at, at + HEAD_DIM)
        probs = head_probs(
            qu_ref[0][:, cols],
            qv_ref[0][:, cols],
            key_ref[0][:, cols],
            place_ref[:, cols],
            sine_rows,
            cosines,
            basis_low,
        )
        merged.append(product(probs.astype(jnp.bfloat16), value_ref[0][:, cols]))
    out_ref[0] = jnp.concatenate(merged, axis=-1).astype(jnp.bfloat16)


def backward_kernel(
    qu_ref,
    qv_ref,
    key_ref,
    value_ref,
    grad_ref,
    place_ref,
    sine_ref,
    cos_ref,
    grad_query_ref,
    grad_key_ref,
    grad_value_ref,
    grad_bias_ref,
    grad_place_ref,
):
    sine_rows = sine_ref[0]
    cosines = cos_ref[0]
    basis_low = jnp.concatenate([cosines, sine_rows], axis=-1).astype(jnp.bfloat16)
    half_width = sine_rows.shape[-1]
    queries, keys, values, sums_u, sums_v, places = ([], [], [], [], [], [])
    for at in range(0, grad_query_ref.shape[-1], HEAD_DIM):
        cols = slice(at, at + HEAD_DIM)
        query_u = qu_ref[0][:, cols]
        query_v = qv_ref[0][:, cols]
        key_low = key_ref[0][:, cols]
        place_head = place_ref[:, cols]
        grad_head = grad_ref[0][:, cols]
        probs = head_probs(query_u, query_v, key_low, place_head, sine_rows, cosines, basis_low)
        values.append(product_left(probs.astype(jnp.bfloat16), grad_head))
        grad_probs = product_right(grad_head, value_ref[0][:, cols])
        inner_sum = jnp.sum(grad_probs * probs, axis=-1, keepdims=True)
        grad_scores = (probs * (grad_probs - inner_sum) * (1.0 / math.sqrt(HEAD_DIM))).astype(
            jnp.bfloat16
        )
        grad_u = product(grad_scores, key_low)
        keys.append(product_left(grad_scores, query_u))
        grad_coeff = product(grad_scores, basis_low)
        grad_a = grad_coeff[:, :half_width]
        grad_b = grad_coeff[:, half_width:]
        grad_raw = jnp.concatenate(
            [grad_a * sine_rows - grad_b * cosines, grad_a * cosines + grad_b * sine_rows],
            axis=-1,
        ).astype(jnp.bfloat16)
        grad_v = product(grad_raw, place_head)
        places.append(product_left(grad_raw, query_v))
        queries.append(grad_u + grad_v)
        sums_u.append(jnp.sum(grad_u, axis=0, keepdims=True))
        sums_v.append(jnp.sum(grad_v, axis=0, keepdims=True))
    grad_query_ref[0] = jnp.concatenate(queries, axis=-1).astype(jnp.bfloat16)
    grad_key_ref[0] = jnp.concatenate(keys, axis=-1).astype(jnp.bfloat16)
    grad_value_ref[0] = jnp.concatenate(values, axis=-1).astype(jnp.bfloat16)
    row_u = jnp.concatenate(sums_u, axis=-1)
    row_v = jnp.concatenate(sums_v, axis=-1)
    at_row = lax.broadcasted_iota(jnp.int32, grad_bias_ref.shape[1:], 0)
    grad_bias_ref[0] = jnp.where(at_row == 0, row_u, jnp.where(at_row == 1, row_v, 0.0))
    grad_place_ref[0] = jnp.concatenate(places, axis=-1)


def attention_specs(clip_length, model_width):
    rows = pl.BlockSpec((1, clip_length, 128), lambda i, j: (i, 0, j))
    place = pl.BlockSpec((model_width, 128), lambda i, j: (0, j))
    wave = pl.BlockSpec((1, clip_length, model_width // 2), lambda i, j: (i, 0, 0))
    return (rows, place, wave)


def attention_inputs(joint_clips, gains, model_width):
    query = joint_clips[..., :model_width]
    return (
        (query + gains[2]).astype(jnp.bfloat16),
        (query + gains[3]).astype(jnp.bfloat16),
        joint_clips[..., model_width : 2 * model_width].astype(jnp.bfloat16),
        joint_clips[..., 2 * model_width :].astype(jnp.bfloat16),
    )


def attention_forward(parts, place_full, sine_rows, cosines):
    clip_count, clip_length, model_width = parts[0].shape
    rows, place, wave = attention_specs(clip_length, model_width)
    return pl.pallas_call(
        forward_kernel,
        grid=(clip_count, model_width // 128),
        in_specs=[rows, rows, rows, rows, place, wave, wave],
        out_specs=rows,
        out_shape=jax.ShapeDtypeStruct(parts[0].shape, jnp.bfloat16),
        compiler_params=pltpu.CompilerParams(vmem_limit_bytes=48 * 1024 * 1024),
        cost_estimate=pl.CostEstimate(
            flops=16000000000, bytes_accessed=12000000, transcendentals=5000000
        ),
    )(*parts, place_full, sine_rows, cosines)


def attention_backward(parts, grad_context, place_full, sine_rows, cosines):
    clip_count, clip_length, model_width = parts[0].shape
    rows, place, wave = attention_specs(clip_length, model_width)
    like = jax.ShapeDtypeStruct(parts[0].shape, jnp.bfloat16)
    return pl.pallas_call(
        backward_kernel,
        grid=(clip_count, model_width // 128),
        in_specs=[rows, rows, rows, rows, rows, place, wave, wave],
        out_specs=[
            rows,
            rows,
            rows,
            pl.BlockSpec((1, 8, 128), lambda i, j: (i, 0, j)),
            pl.BlockSpec((1, model_width, 128), lambda i, j: (i, 0, j)),
        ],
        out_shape=[
            like,
            like,
            like,
            jax.ShapeDtypeStruct((clip_count, 8, model_width), jnp.float32),
            jax.ShapeDtypeStruct((clip_count, model_width, model_width), jnp.float32),
        ],
        compiler_params=pltpu.CompilerParams(vmem_limit_bytes=48 * 1024 * 1024),
        cost_estimate=pl.CostEstimate(
            flops=80000000000, bytes_accessed=20000000, transcendentals=5000000
        ),
    )(*parts, grad_context, place_full, sine_rows, cosines)


def pack_small(columns):
    joined = jnp.concatenate(columns, axis=1)
    return jnp.pad(joined, ((0, 0), (0, -joined.shape[1] % 128)))


MESH = pl.DeviceIdType.MESH
BF16 = jnp.bfloat16
F32 = jnp.float32


def bit_of(index, bit):
    return lax.rem(lax.div(index, 1 << bit), 2)


def flip_bit(index, bit):
    return index + (1 - 2 * bit_of(index, bit)) * (1 << bit)


def link_orders(bit_count):
    far = list(range(bit_count - 1, 2, -1))
    if bit_count < 3:
        return [list(range(bit_count))] * 3
    return [far + [1, 2, 0], far + [2, 0, 1], far + [0, 1, 2]]


def greet(bit_count):
    shard = lax.axis_index("shard")
    replica = lax.axis_index("replica")
    barrier = pltpu.get_barrier_semaphore()
    for bit in range(bit_count):
        pl.semaphore_signal(
            barrier, inc=1, device_id={"shard": flip_bit(shard, bit)}, device_id_type=MESH
        )
    pl.semaphore_signal(
        barrier, inc=1, device_id={"replica": flip_bit(replica, 0)}, device_id_type=MESH
    )
    pl.semaphore_wait(barrier, bit_count + 1)


def block_index(bit_count, free_bits, values):
    return tuple(
        slice(None) if bit in free_bits else values[bit] for bit in range(bit_count - 1, -1, -1)
    )


class Piece:
    def __init__(self, array, color, rows, cols):
        self.array, self.color, self.rows, self.cols = array, color, rows, cols

    @property
    def tail(self):
        return (pl.ds(*self.rows), pl.ds(*self.cols))

    @property
    def shape(self):
        return (self.rows[1], self.cols[1])


def plan_pieces(shapes, wanted):
    pieces = []
    for array, color, low, high in wanted:
        rows, cols = shapes[array]
        if cols >= 2048 or cols % (16 * 128) == 0 or rows < 32:
            unit = cols // 128
            a, b = unit * low // 16 * 128, unit * high // 16 * 128
            wide = ((0, rows), (a, b - a))
        else:
            unit = rows // 16
            a, b = unit * low // 16 * 16, unit * high // 16 * 16
            wide = ((a, b - a), (0, cols))
        if b > a:
            pieces.append(Piece(array, color, *wide))
    return pieces


class Gather:
    def __init__(self, bit_count, pieces, ins, outs, sems):
        self.bits, self.pieces, self.ins, self.outs = bit_count, pieces, ins, outs
        self.send, self.recv, self.core_send, self.core_recv, self.local = sems
        shard = lax.axis_index("shard")
        replica = lax.axis_index("replica")
        self.shard, self.half = shard, lax.rem(replica, 2)
        self.core = {"replica": flip_bit(replica, 0)}
        self.own = [bit_of(shard, bit) for bit in range(bit_count)]
        self.orders = link_orders(bit_count)

    @staticmethod
    def scratch(bit_count, pieces, array_count):
        grid = (len(pieces), bit_count)
        return [pltpu.SemaphoreType.DMA(grid)] * 4 + [pltpu.SemaphoreType.DMA((array_count,))]

    def local_copies(self):
        index = block_index(self.bits, (), self.own)
        return [
            pltpu.make_async_copy(self.ins[a], self.outs[a].at[index], self.local.at[a])
            for a in range(len(self.ins))
        ]

    def hop(self, p, step):
        piece = self.pieces[p]
        order = self.orders[piece.color]
        out = self.outs[piece.array]
        index = block_index(self.bits, order[:step], self.own)
        region = out.at[index + (self.half,) + piece.tail]
        if step == 0:
            source = self.ins[piece.array].at[(self.half,) + piece.tail]
        else:
            source = region
        return pltpu.make_async_remote_copy(
            source,
            region,
            self.send.at[p, step],
            self.recv.at[p, step],
            device_id={"shard": flip_bit(self.shard, order[step])},
            device_id_type=MESH,
        )

    def cross(self, p, step):
        piece = self.pieces[p]
        order = self.orders[piece.color]
        values = list(self.own)
        values[order[step]] = 1 - values[order[step]]
        index = block_index(self.bits, order[:step], values)
        region = self.outs[piece.array].at[index + (self.half,) + piece.tail]
        return pltpu.make_async_remote_copy(
            region,
            region,
            self.core_send.at[p, step],
            self.core_recv.at[p, step],
            device_id=self.core,
            device_id_type=MESH,
        )

    def start(self):
        for p in range(len(self.pieces)):
            self.hop(p, 0).start()
        for copy in self.local_copies():
            copy.start()

    def advance(self, step, which=None):
        if step == 0:
            for copy in self.local_copies():
                copy.wait()
        for p in range(len(self.pieces)):
            self.hop(p, step).wait_recv()
            if step + 1 < self.bits:
                self.hop(p, step + 1).start()
            self.cross(p, step).start()

    def finish(self):
        for p in range(len(self.pieces)):
            for step in range(self.bits):
                self.hop(p, step).wait_send()
                self.cross(p, step).wait()


class Scatter:
    def __init__(self, bit_count, pieces, ins, outs, refs):
        self.bits, self.pieces, self.ins, self.outs = bit_count, pieces, ins, outs
        count = len(pieces)
        self.first = refs[:count]
        self.total = refs[count : 2 * count]
        self.last = refs[2 * count : 3 * count]
        self.send, self.recv = refs[3 * count : 3 * count + 2]
        land = refs[3 * count + 2 :]
        self.land = [land[p * bit_count : (p + 1) * bit_count] for p in range(count)]
        shard = lax.axis_index("shard")
        replica = lax.axis_index("replica")
        self.shard, self.half = shard, lax.rem(replica, 2)
        self.core = {"replica": flip_bit(replica, 0)}
        self.own = [bit_of(shard, bit) for bit in range(bit_count)]
        self.orders = [order[::-1] for order in link_orders(bit_count)]

    @staticmethod
    def scratch(bit_count, pieces):
        lead = (2,) * bit_count
        return (
            [pltpu.VMEM(lead + piece.shape, BF16) for piece in pieces]
            + [pltpu.VMEM(lead + piece.shape, BF16) for piece in pieces]
            + [pltpu.VMEM(piece.shape, BF16) for piece in pieces]
            + [pltpu.SemaphoreType.DMA((len(pieces), bit_count + 2))] * 2
            + [
                pltpu.VMEM((2,) * (bit_count - step - 1) + piece.shape, BF16)
                for piece in pieces
                for step in range(bit_count)
            ]
        )

    def copy(self, p, step, source, target, device):
        return pltpu.make_async_remote_copy(
            source,
            target,
            self.send.at[p, step],
            self.recv.at[p, step],
            device_id=device,
            device_id_type=MESH,
        )

    def pair(self, p):
        piece = self.pieces[p]
        lead = (slice(None),) * self.bits
        source = self.ins[piece.array].at[lead + (1 - self.half,) + piece.tail]
        return self.copy(p, 0, source, self.first[p], self.core)

    def hop(self, p, step):
        order = self.orders[self.pieces[p].color]
        bit = order[step]
        values = list(self.own)
        values[bit] = 1 - values[bit]
        index = block_index(self.bits, order[step + 1 :], values)
        return self.copy(
            p,
            step + 1,
            self.total[p].at[index],
            self.land[p][step],
            {"shard": flip_bit(self.shard, bit)},
        )

    def final(self, p):
        index = block_index(self.bits, (), self.own)
        return self.copy(p, self.bits + 1, self.total[p].at[index], self.last[p], self.core)

    def spread(self, number, free_bits):
        values = list(self.own)
        place = 0
        for bit in sorted(free_bits):
            values[bit] = bit_of(number, place)
            place += 1
        return block_index(self.bits, (), values)

    def start(self, which=None):
        for p in range(len(self.pieces)):
            self.pair(p).start()

    def add_pair(self):
        for p, piece in enumerate(self.pieces):
            self.pair(p).wait_recv()
            every = range(self.bits)

            def add(number, carry):
                index = self.spread(number, every)
                mine = self.ins[piece.array][index + (self.half,) + piece.tail]
                theirs = self.first[p][index]
                self.total[p][index] = (mine.astype(F32) + theirs.astype(F32)).astype(BF16)
                return carry

            lax.fori_loop(0, 1 << self.bits, add, 0)
            self.hop(p, 0).start()

    def advance(self, step):
        for p, piece in enumerate(self.pieces):
            order = self.orders[piece.color]
            self.hop(p, step).wait_recv()
            count = 1 << (self.bits - step - 1)
            left = order[step + 1 :]

            def add(number, carry):
                index = self.spread(number, left)
                mine = self.total[p][index]
                free = sorted(left, reverse=True)
                at = tuple(bit_of(number, len(free) - 1 - n) for n in range(len(free)))
                theirs = self.land[p][step][at] if at else self.land[p][step][...]
                self.total[p][index] = (mine.astype(F32) + theirs.astype(F32)).astype(BF16)
                return carry

            lax.fori_loop(0, count, add, 0)
            if step + 1 < self.bits:
                self.hop(p, step + 1).start()
            else:
                self.final(p).start()

    def finish(self):
        index = block_index(self.bits, (), self.own)
        for p, piece in enumerate(self.pieces):
            self.outs[piece.array][(self.half,) + piece.tail] = self.total[p][index].astype(F32)
            self.final(p).wait_recv()
            self.outs[piece.array][(1 - self.half,) + piece.tail] = self.last[p][...].astype(F32)
        for p in range(len(self.pieces)):
            self.pair(p).wait_send()
            for step in range(self.bits):
                self.hop(p, step).wait_send()
            self.final(p).wait_send()


def gather_kernel(bit_count, pieces, array_count, *refs):
    ins, outs = refs[:array_count], refs[array_count : 2 * array_count]
    greet(bit_count)
    work = Gather(bit_count, pieces, ins, outs, refs[2 * array_count :])
    work.start()
    for step in range(bit_count):
        work.advance(step)
    work.finish()


def halves(array):
    return array.reshape(2, array.shape[0] // 2, array.shape[1])


def gather_arrays(arrays, wanted, collective_id):
    bit_count = (lax.axis_size("shard") - 1).bit_length()
    ins = [halves(array) for array in arrays]
    pieces = plan_pieces([array.shape[1:] for array in ins], wanted)
    lead = (2,) * bit_count
    outs = pl.pallas_call(
        functools.partial(gather_kernel, bit_count, pieces, len(ins)),
        in_specs=[pl.BlockSpec(memory_space=pl.ANY)] * len(ins),
        out_specs=[pl.BlockSpec(memory_space=pl.ANY)] * len(ins),
        out_shape=[jax.ShapeDtypeStruct(lead + array.shape, BF16) for array in ins],
        scratch_shapes=Gather.scratch(bit_count, pieces, len(ins)),
        compiler_params=pltpu.CompilerParams(collective_id=collective_id, has_side_effects=True),
    )(*ins)
    return [
        out.reshape(-1, array.shape[1]) for out, array in zip(outs, arrays)
    ]


def scatter_kernel(bit_count, pieces, array_count, *refs):
    ins, outs = refs[:array_count], refs[array_count : 2 * array_count]
    greet(bit_count)
    work = Scatter(bit_count, pieces, ins, outs, refs[2 * array_count :])
    work.start()
    work.add_pair()
    for step in range(bit_count):
        work.advance(step)
    work.finish()


def scatter_arrays(arrays, wanted, collective_id):
    shards = lax.axis_size("shard")
    bit_count = (shards - 1).bit_length()
    lead = (2,) * bit_count
    ins = [
        array.reshape(lead + (2, array.shape[0] // (2 * shards), array.shape[1]))
        for array in arrays
    ]
    pieces = plan_pieces([array.shape[-2:] for array in ins], wanted)
    outs = pl.pallas_call(
        functools.partial(scatter_kernel, bit_count, pieces, len(ins)),
        in_specs=[pl.BlockSpec(memory_space=pltpu.VMEM)] * len(ins),
        out_specs=[pl.BlockSpec(memory_space=pltpu.VMEM)] * len(ins),
        out_shape=[jax.ShapeDtypeStruct((2,) + array.shape[-2:], F32) for array in ins],
        scratch_shapes=Scatter.scratch(bit_count, pieces),
        compiler_params=pltpu.CompilerParams(
            collective_id=collective_id,
            has_side_effects=True,
            vmem_limit_bytes=48 * 1024 * 1024,
        ),
    )(*ins)
    outs = [out.reshape(-1, out.shape[-1]) for out in outs]
    replicas = lax.axis_size("replica")
    if replicas > 2:
        groups = [list(range(core, replicas, 2)) for core in range(2)]
        outs = [lax.psum(out, "replica", axis_index_groups=groups) for out in outs]
    return outs


def everyone(combine, count, in_ref, out_ref, held, send_sem, recv_sem):
    shards = lax.axis_size("shard")
    me = lax.axis_index("replica") * shards + lax.axis_index("shard")
    barrier = pltpu.get_barrier_semaphore()

    def place(device):
        return (lax.div(device, shards), lax.rem(device, shards))

    def hello(far, carry):
        pl.semaphore_signal(
            barrier, inc=1, device_id=place(lax.rem(me + far, count)), device_id_type=MESH
        )
        return carry

    lax.fori_loop(1, count, hello, 0)
    pl.semaphore_wait(barrier, count - 1)

    def copy(far, slot):
        return pltpu.make_async_remote_copy(
            in_ref,
            held.at[slot],
            send_sem.at[far],
            recv_sem.at[far],
            device_id=place(lax.rem(me + far, count)),
            device_id_type=MESH,
        )

    def go(far, carry):
        copy(far, me).start()
        return carry

    def arrive(far, carry):
        copy(far, lax.rem(me + count - far, count)).wait_recv()
        return carry

    def sent(far, carry):
        copy(far, me).wait_send()
        return carry

    lax.fori_loop(1, count, go, 0)
    held[me] = in_ref[...]
    lax.fori_loop(1, count, arrive, 0)
    out_ref[...] = combine(held[...])
    lax.fori_loop(1, count, sent, 0)


def combine_sums(tiles):
    return jnp.sum(tiles, axis=0)


def combine_stats(local_count, tiles):
    half = tiles.shape[1] // 2
    means = tiles[:, :half]
    mean = jnp.sum(means, axis=0) * (1.0 / tiles.shape[0])
    apart = means - mean
    total = jnp.sum(tiles[:, half:] + local_count * (apart * apart), axis=0)
    return jnp.concatenate([mean, total * (1.0 / (local_count * tiles.shape[0]))], axis=0)


def exchange_rows(upper, lower, combine, collective_id):
    width = upper.shape[0]
    tile = jnp.concatenate([upper.reshape(-1, 128), lower.reshape(-1, 128)], axis=0)
    count = lax.axis_size("replica") * lax.axis_size("shard")
    out = pl.pallas_call(
        functools.partial(everyone, combine, count),
        in_specs=[pl.BlockSpec(memory_space=pltpu.VMEM)],
        out_specs=pl.BlockSpec(memory_space=pltpu.VMEM),
        out_shape=jax.ShapeDtypeStruct(tile.shape, F32),
        scratch_shapes=[
            pltpu.VMEM((count,) + tile.shape, F32),
            pltpu.SemaphoreType.DMA((count,)),
            pltpu.SemaphoreType.DMA((count,)),
        ],
        compiler_params=pltpu.CompilerParams(collective_id=collective_id, has_side_effects=True),
    )(tile)
    return out[: width // 128].reshape(width), out[width // 128 :].reshape(width)


def tap_windows(padded_ref, start, rows, visit):
    for shift in range(8):
        window = padded_ref[start + shift : start + shift + rows + 24, :]
        for lift in range(4):
            offset = 8 * lift + shift
            if offset > 0:
                visit(offset, window[8 * lift : 8 * lift + rows])


def fill_padded(padded_ref, values):
    length = values.shape[0]
    edge = jnp.zeros((16, values.shape[1]), F32)
    padded_ref[0:16, :] = edge
    padded_ref[16 : 16 + length, :] = values
    padded_ref[16 + length : 32 + length, :] = edge


def tile_rows(length):
    for rows in (136, 128, 120, 112, 104, 96, 88, 80, 72, 64, 56, 48, 40, 32, 24, 16, 8):
        if length % rows == 0:
            return rows
    return length


def conv_forward_kernel(linear_ref, gate_ref, taps_ref, out_ref, stats_ref, padded_ref):
    length = out_ref.shape[1]
    rows = tile_rows(length)
    fill_padded(padded_ref, linear_ref[0] * jax.nn.sigmoid(gate_ref[0]))
    for start in range(0, length, rows):
        total = [jnp.zeros((rows, out_ref.shape[2]), F32)]

        def visit(offset, window):
            total[0] = total[0] + taps_ref[offset - 1 : offset, :] * window

        tap_windows(padded_ref, start, rows, visit)
        out_ref[0, start : start + rows, :] = total[0]
    values = out_ref[0]
    mean = jnp.sum(values, axis=0, keepdims=True) * (1.0 / length)
    apart = values - mean
    squares = jnp.sum(apart * apart, axis=0, keepdims=True)
    at_row = lax.broadcasted_iota(jnp.int32, stats_ref.shape[1:], 0)
    stats_ref[0] = jnp.where(at_row == 0, mean, jnp.where(at_row == 1, squares, 0.0))


def conv_forward(mixed_clips, taps):
    clip_count, clip_length, width = mixed_clips.shape
    channels = width // 2
    blocks = channels // 128
    piece = pl.BlockSpec((1, clip_length, 128), lambda i, j: (i, 0, j))
    return pl.pallas_call(
        conv_forward_kernel,
        grid=(clip_count, blocks),
        in_specs=[
            piece,
            pl.BlockSpec((1, clip_length, 128), lambda i, j: (i, 0, blocks + j)),
            pl.BlockSpec((taps.shape[0], 128), lambda i, j: (0, j)),
        ],
        out_specs=[piece, pl.BlockSpec((1, 8, 128), lambda i, j: (i, 0, j))],
        out_shape=[
            jax.ShapeDtypeStruct((clip_count, clip_length, channels), F32),
            jax.ShapeDtypeStruct((clip_count, 8, channels), F32),
        ],
        scratch_shapes=[pltpu.VMEM((clip_length + 32, 128), F32)],
        compiler_params=pltpu.CompilerParams(vmem_limit_bytes=32 * 1024 * 1024),
        cost_estimate=pl.CostEstimate(
            flops=80000000, bytes_accessed=8000000, transcendentals=600000
        ),
    )(mixed_clips, mixed_clips, taps)


def conv_backward_kernel(
    linear_ref, gate_ref, grad_ref, conv_ref, rows_ref, taps_ref,
    out_ref, grad_taps_ref, padded_ref, grad_padded_ref, tap_sums_ref,
):
    length = grad_ref.shape[1]
    rows = tile_rows(length)
    block = pl.program_id(1)
    channels = out_ref.shape[2] // 2
    mean, inverse, scale = rows_ref[0:1, :], rows_ref[1:2, :], rows_ref[2:3, :]
    shift_mean, gain_mean = rows_ref[3:4, :], rows_ref[4:5, :]
    unit = (conv_ref[0] - mean) * inverse
    grad_conv = scale * (grad_ref[0] - shift_mean - unit * gain_mean)
    fill_padded(grad_padded_ref, grad_conv)
    fill_padded(padded_ref, linear_ref[0] * jax.nn.sigmoid(gate_ref[0]))
    tap_sums_ref[...] = jnp.zeros_like(tap_sums_ref)
    first = pl.multiple_of(block * 128, 128)
    second = pl.multiple_of(channels + block * 128, 128)
    for start in range(0, length, rows):
        grad_rows = grad_padded_ref[16 + start : 16 + start + rows, :]

        def visit(offset, window):
            product_rows = (grad_rows * window).reshape(rows // 8, 8, window.shape[1])
            tap_sums_ref[offset - 1] = tap_sums_ref[offset - 1] + jnp.sum(product_rows, axis=0)

        tap_windows(padded_ref, start, rows, visit)
        total = [jnp.zeros((rows, 128), F32)]

        def visit_back(offset, window):
            total[0] = total[0] + taps_ref[31 - offset : 32 - offset, :] * window

        tap_windows(grad_padded_ref, start, rows, visit_back)
        grad_gated = total[0]
        gate = jax.nn.sigmoid(gate_ref[0, start : start + rows, :])
        grad_linear = grad_gated * gate
        linear = linear_ref[0, start : start + rows, :]
        out_ref[0, start : start + rows, pl.ds(first, 128)] = grad_linear.astype(BF16)
        out_ref[0, start : start + rows, pl.ds(second, 128)] = (
            grad_linear * linear * (1.0 - gate)
        ).astype(BF16)
    grad_taps_ref[0] = jnp.sum(tap_sums_ref[...], axis=1)


def conv_backward(mixed_clips, grad_clips, conv_clips, rows, taps):
    clip_count, clip_length, width = mixed_clips.shape
    channels = width // 2
    blocks = channels // 128
    piece = pl.BlockSpec((1, clip_length, 128), lambda i, j: (i, 0, j))
    return pl.pallas_call(
        conv_backward_kernel,
        grid=(clip_count, blocks),
        in_specs=[
            piece,
            pl.BlockSpec((1, clip_length, 128), lambda i, j: (i, 0, blocks + j)),
            piece,
            piece,
            pl.BlockSpec((8, 128), lambda i, j: (0, j)),
            pl.BlockSpec((taps.shape[0], 128), lambda i, j: (0, j)),
        ],
        out_specs=[
            pl.BlockSpec((1, clip_length, width), lambda i, j: (i, 0, 0)),
            pl.BlockSpec((1, 32, 128), lambda i, j: (i, 0, j)),
        ],
        out_shape=[
            jax.ShapeDtypeStruct((clip_count, clip_length, width), BF16),
            jax.ShapeDtypeStruct((clip_count, 32, channels), F32),
        ],
        scratch_shapes=[
            pltpu.VMEM((clip_length + 32, 128), F32),
            pltpu.VMEM((clip_length + 32, 128), F32),
            pltpu.VMEM((32, 8, 128), F32),
        ],
        compiler_params=pltpu.CompilerParams(vmem_limit_bytes=32 * 1024 * 1024),
        cost_estimate=pl.CostEstimate(
            flops=160000000, bytes_accessed=14000000, transcendentals=1200000
        ),
    )(mixed_clips, mixed_clips, grad_clips, conv_clips, rows, taps)


EARLY_PLAN = [(0, 0, 0, 10), (0, 1, 10, 16), (1, 1, 0, 4), (1, 2, 4, 16), (2, 0, 0, 16)]
LATE_PLAN = [
    (0, 0, 0, 8),
    (0, 1, 8, 16),
    (1, 1, 0, 16),
    (2, 2, 0, 16),
    (3, 1, 0, 16),
    (4, 2, 0, 16),
    (5, 0, 0, 16),
    (6, 2, 0, 16),
]
ALL_PLAN = [
    (0, 0, 0, 10),
    (0, 1, 10, 16),
    (1, 1, 0, 4),
    (1, 2, 4, 16),
    (2, 0, 0, 8),
    (2, 1, 8, 16),
    (3, 1, 0, 16),
    (4, 2, 0, 16),
    (5, 1, 0, 16),
    (6, 2, 0, 16),
    (7, 0, 0, 16),
    (8, 2, 0, 16),
    (9, 0, 0, 16),
]


def body(
    features,
    frame_times,
    cotangent,
    vectors,
    first_up,
    first_down,
    query_key_value,
    place_weight,
    out_weight,
    point_glu,
    depth_taps,
    point_out,
    second_up,
    second_down,
):
    clip_count, clip_length, model_width = features.shape
    row_count = clip_count * clip_length
    token_count = row_count * lax.axis_size("replica") * lax.axis_size("shard")

    shards = lax.axis_size("shard")
    depth = first_up.shape[0]
    hidden_width = first_up.shape[1]
    row_total = vectors.shape[0]
    tap_total = depth_taps.shape[0]

    small_shard = pack_small([vectors.T, depth_taps.T])
    up_one, down_one, small_full = gather_arrays(
        [first_up, first_down, small_shard], EARLY_PLAN, 1
    )
    gathered = gather_arrays(
        [query_key_value, place_weight, out_weight, point_glu, point_out, second_up, second_down],
        LATE_PLAN,
        2,
    )
    small = small_full.T
    first_full = (small[:row_total], up_one, down_one)
    attend_full = gathered[:3]
    conv_full = (gathered[3], small[row_total : row_total + tap_total], gathered[4])
    second_full = gathered[5:]
    gains = first_full[0].astype(jnp.float32)
    inputs = features.reshape(row_count, model_width).astype(jnp.float32)
    first_out, first_kept = feed_forward(inputs, gains[0], first_full[1], first_full[2])
    after_first = inputs + 0.5 * first_out
    normed_attend = normalize(after_first, gains[1]).astype(jnp.bfloat16)
    joint_rows = product(normed_attend, attend_full[0])
    joint_clips = joint_rows.reshape(clip_count, clip_length, 3 * model_width)
    attend_parts = attention_inputs(joint_clips, gains, model_width)
    sine_flat, cos_flat = wave_table(frame_times.reshape(row_count), model_width)
    sine_rows = sine_flat.reshape(clip_count, clip_length, -1)
    cosines = cos_flat.reshape(clip_count, clip_length, -1)
    context_clips = attention_forward(attend_parts, attend_full[1], sine_rows, cosines)
    context_low = context_clips.reshape(row_count, model_width)
    after_attend = after_first + product(context_low, attend_full[2])
    normed_conv = normalize(after_attend, gains[4]).astype(jnp.bfloat16)
    mixed_rows = product(normed_conv, conv_full[0]).reshape(
        clip_count, clip_length, 2 * model_width
    )
    taps = jnp.pad(conv_full[1].astype(jnp.float32), ((0, 32 - tap_total), (0, 0)))
    conv_clips, clip_stats = conv_forward(mixed_rows, taps)
    conv_flat = conv_clips.reshape(row_count, model_width)
    clip_means = clip_stats[:, 0]
    local_mean = jnp.mean(clip_means, axis=0)
    apart = clip_means - local_mean
    local_squares = jnp.sum(clip_stats[:, 1] + clip_length * (apart * apart), axis=0)
    channel_mean, variance = exchange_rows(
        local_mean,
        local_squares,
        functools.partial(combine_stats, row_count),
        3,
    )
    centered = conv_flat - channel_mean
    inverse = lax.rsqrt(variance + epsilon)
    unit_values = centered * inverse
    shaped = unit_values * gains[5] + gains[6]
    active_conv = swish_act(shaped).astype(jnp.bfloat16)
    after_conv = after_attend + product(active_conv, conv_full[2])
    second_out, second_kept = feed_forward(after_conv, gains[7], second_full[0], second_full[1])
    after_second = after_conv + 0.5 * second_out
    output = normalize(after_second, gains[8])
    grad_last, grad_final_gain = normalize_back(
        after_second, gains[8], cotangent.reshape(row_count, model_width).astype(jnp.float32)
    )
    second_back = second_full
    grad_conv_out, grad_second_gain, grad_second_up, grad_second_down = feed_back(
        grad_last, after_conv, gains[7], second_back[0], second_back[1], second_kept
    )
    conv_back = conv_full
    grad_low = grad_conv_out.astype(jnp.bfloat16)
    grad_point_out = product_left(active_conv, grad_low)
    grad_shaped = product_right(grad_low, conv_back[2]) * swish_slope(shaped)
    shift_total, gain_total = exchange_rows(
        jnp.sum(grad_shaped, axis=0), jnp.sum(grad_shaped * unit_values, axis=0), combine_sums, 4
    )
    zero_row = jnp.zeros_like(inverse)
    batch_rows = jnp.stack(
        [
            channel_mean,
            inverse,
            gains[5] * inverse,
            shift_total / token_count,
            gain_total / token_count,
            zero_row,
            zero_row,
            zero_row,
        ]
    )
    grad_mixed_clips, clip_taps = conv_backward(
        mixed_rows,
        grad_shaped.reshape(clip_count, clip_length, model_width),
        conv_clips,
        batch_rows,
        taps,
    )
    grad_taps = jnp.sum(clip_taps, axis=0)[:tap_total]
    grad_mixed_low = grad_mixed_clips.reshape(row_count, 2 * model_width)
    grad_point_glu = product_left(normed_conv, grad_mixed_low)
    grad_extra, grad_conv_gain = normalize_back(
        after_attend, gains[4], product_right(grad_mixed_low, conv_back[0])
    )
    grad_attend_out = grad_conv_out + grad_extra
    attend_back = attend_full
    grad_low = grad_attend_out.astype(jnp.bfloat16)
    grad_out_weight = product_left(context_low, grad_low)
    grad_context = (
        product_right(grad_low, attend_back[2])
        .astype(jnp.bfloat16)
        .reshape(clip_count, clip_length, model_width)
    )
    grad_query, grad_key, grad_value, grad_bias, grad_place = attention_backward(
        attend_parts, grad_context, attend_back[1], sine_rows, cosines
    )
    bias_rows = jnp.sum(grad_bias, axis=0)
    bias_sums = (bias_rows[0], bias_rows[1])
    grad_joint_low = jnp.concatenate([grad_query, grad_key, grad_value], axis=-1).reshape(
        row_count, 3 * model_width
    )
    grad_qkv = product_left(normed_attend, grad_joint_low)
    grad_extra, grad_attend_gain = normalize_back(
        after_first, gains[1], product_right(grad_joint_low, attend_back[0])
    )
    grad_first_out = grad_attend_out + grad_extra
    grad_place_full = jnp.sum(grad_place, axis=0)
    first_back = first_full
    first_gains = first_back[0].astype(jnp.float32)
    grad_inputs, grad_first_gain, grad_first_up, grad_first_down = feed_back(
        grad_first_out, inputs, first_gains[0], first_back[1], first_back[2], first_kept
    )
    grad_rows = jnp.stack(
        [
            grad_first_gain,
            grad_attend_gain,
            bias_sums[0],
            bias_sums[1],
            grad_conv_gain,
            zero_row,
            zero_row,
            grad_second_gain,
            grad_final_gain,
        ]
    )
    partial = [
        grad_first_up,
        grad_first_down,
        grad_qkv,
        grad_place_full,
        grad_out_weight,
        grad_point_glu,
        grad_point_out,
        grad_second_up,
        grad_second_down,
        pack_small([grad_rows.T, grad_taps.T]),
    ]
    sums = scatter_arrays([array.astype(BF16) for array in partial], ALL_PLAN, 5)
    small_sums = sums[9].T
    summed = (
        small_sums[:row_total],
        sums[0],
        sums[1],
        sums[2],
        sums[3],
        sums[4],
        sums[5],
        small_sums[row_total : row_total + tap_total],
        sums[6],
        sums[7],
        sums[8],
    )
    shard_cols = summed[0].shape[1]
    first_col = lax.axis_index("shard") * shard_cols
    gain_part = lax.dynamic_slice_in_dim(gain_total, first_col, shard_cols)
    shift_part = lax.dynamic_slice_in_dim(shift_total, first_col, shard_cols)
    grad_vectors = summed[0].at[5].add(gain_part).at[6].add(shift_part)
    return (
        output.astype(jnp.bfloat16).reshape(clip_count, clip_length, model_width),
        grad_inputs.astype(jnp.bfloat16).reshape(clip_count, clip_length, model_width),
        grad_vectors,
        summed[1],
        summed[2],
        summed[3],
        summed[4],
        summed[5],
        summed[6],
        summed[7],
        summed[8],
        summed[9],
        summed[10],
    )


def solution(mesh):
    return jax.shard_map(
        body,
        mesh=mesh,
        in_specs=(
            P(("replica", "shard"), None, None),
            P(("replica", "shard"), None),
            P(("replica", "shard"), None, None),
            P(None, "shard"),
            P("shard", None),
            P("shard", None),
            P("shard", None),
            P("shard", None),
            P("shard", None),
            P("shard", None),
            P(None, "shard"),
            P("shard", None),
            P("shard", None),
            P("shard", None),
        ),
        out_specs=(
            P(("replica", "shard"), None, None),
            P(("replica", "shard"), None, None),
            P(None, "shard"),
            P("shard", None),
            P("shard", None),
            P("shard", None),
            P("shard", None),
            P("shard", None),
            P("shard", None),
            P(None, "shard"),
            P("shard", None),
            P("shard", None),
            P("shard", None),
        ),
        check_vma=False,
    )
```

```python
import functools
import math

import jax
import jax.numpy as jnp
from jax import lax
from jax.experimental import pallas as pl
from jax.experimental.pallas import tpu as pltpu
from jax.sharding import PartitionSpec as P

HEADS = 8
HEAD_DIM = 64


epsilon = 1e-05


def normalize(values, gain_row):
    center = values - jnp.mean(values, axis=-1, keepdims=True)
    spread = jnp.mean(center * center, axis=-1, keepdims=True)
    return center * lax.rsqrt(spread + epsilon) * gain_row


def normalize_back(values, gain_row, grad_normed):
    pull = jax.vjp(normalize, values, gain_row)[1]
    return pull(grad_normed)


def swish_act(values):
    return values * jax.nn.sigmoid(values)


def swish_slope(values):
    sigmoid = jax.nn.sigmoid(values)
    return sigmoid * (1.0 + values * (1.0 - sigmoid))


def wave_table(frame_pos, model_width):
    half_width = model_width // 2
    frequency = jnp.exp(
        jnp.arange(half_width, dtype=jnp.float32) * (-math.log(10000.0) / half_width)
    )
    angles = frame_pos.astype(jnp.float32)[:, None] * frequency[None, :]
    return (jnp.sin(angles), jnp.cos(angles))


def product(left_side, right_side):
    return jnp.dot(left_side, right_side, preferred_element_type=jnp.float32)


def product_left(left_side, right_side):
    return lax.dot_general(
        left_side, right_side, (((0,), (0,)), ((), ())), preferred_element_type=jnp.float32
    )


def product_right(left_side, right_side):
    return lax.dot_general(
        left_side, right_side, (((1,), (1,)), ((), ())), preferred_element_type=jnp.float32
    )


def feed_forward(inputs, gain_row, up_full, down_full):
    normed_low = normalize(inputs, gain_row).astype(jnp.bfloat16)
    hidden = product(normed_low, up_full)
    active_low = swish_act(hidden).astype(jnp.bfloat16)
    return (product(active_low, down_full), (normed_low, hidden, active_low))


def feed_back(grad_stream, inputs, gain_row, up_full, down_full, kept_values):
    normed_low, hidden, active_low = kept_values
    grad_low = (0.5 * grad_stream).astype(jnp.bfloat16)
    grad_down = product_left(active_low, grad_low)
    grad_hidden = (product_right(grad_low, down_full) * swish_slope(hidden)).astype(jnp.bfloat16)
    grad_up = product_left(normed_low, grad_hidden)
    grad_normed = product_right(grad_hidden, up_full)
    grad_extra, grad_gain = normalize_back(inputs, gain_row, grad_normed)
    return (grad_stream + grad_extra, grad_gain, grad_up, grad_down)


def head_probs(query_u, query_v, key_low, place_head, sine_rows, cosines, basis_low):
    raw_place = product_right(query_v, place_head)
    half_width = raw_place.shape[-1] // 2
    part_sin = raw_place[:, :half_width]
    part_cos = raw_place[:, half_width:]
    coeff_low = jnp.concatenate(
        [part_sin * sine_rows + part_cos * cosines, part_cos * sine_rows - part_sin * cosines],
        axis=-1,
    ).astype(jnp.bfloat16)
    scores = product_right(query_u, key_low) + product_right(coeff_low, basis_low)
    scores = scores * (1.0 / math.sqrt(HEAD_DIM))
    row_peak = jnp.max(scores, axis=-1, keepdims=True)
    raised = jnp.exp(scores - row_peak)
    return raised * (1.0 / jnp.sum(raised, axis=-1, keepdims=True))


def forward_kernel(bit_count, pieces, array_count, *refs):
    qu_ref, qv_ref, key_ref, value_ref, place_ref, sine_ref, cos_ref = refs[:7]
    shards = refs[7 : 7 + array_count]
    out_ref, probs_ref = refs[7 + array_count : 9 + array_count]
    fulls = refs[9 + array_count : 9 + 2 * array_count]
    gather = Gather(bit_count, pieces, shards, fulls, refs[9 + 2 * array_count :])
    step = pl.program_id(0) * pl.num_programs(1) + pl.program_id(1)
    steps = pl.num_programs(0) * pl.num_programs(1)

    @pl.when(step == 0)
    def begin():
        greet(bit_count)
        gather.start()

    sine_rows = sine_ref[0]
    cosines = cos_ref[0]
    basis_low = jnp.concatenate([cosines, sine_rows], axis=-1).astype(jnp.bfloat16)
    merged = []
    for head, at in enumerate(range(0, out_ref.shape[-1], HEAD_DIM)):
        cols = slice(at, at + HEAD_DIM)
        probs = head_probs(
            qu_ref[0][:, cols],
            qv_ref[0][:, cols],
            key_ref[0][:, cols],
            place_ref[:, cols],
            sine_rows,
            cosines,
            basis_low,
        ).astype(jnp.bfloat16)
        probs_ref[0, head] = probs
        merged.append(product(probs, value_ref[0][:, cols]))
    out_ref[0] = jnp.concatenate(merged, axis=-1).astype(jnp.bfloat16)

    for phase in range(bit_count):
        when = (2, 3, 5)[phase] if phase < min(3, bit_count - 1) else steps - 1

        @pl.when(step == when)
        def go(phase=phase):
            gather.advance(phase)

    @pl.when(step == steps - 1)
    def end():
        gather.finish()


def backward_kernel(bit_count, pieces, array_count, *refs):
    qu_ref, qv_ref, key_ref, value_ref, grad_ref, place_ref, sine_ref, cos_ref, probs_ref = refs[:9]
    partials = refs[9 : 9 + array_count]
    refs = refs[9 + array_count :]
    grad_query_ref, grad_key_ref, grad_value_ref, grad_bias_ref, grad_place_ref = refs[:5]
    owned = refs[5 : 5 + array_count]
    scatter = Scatter(bit_count, pieces, partials, owned, refs[5 + array_count :])
    step = pl.program_id(0) * pl.num_programs(1) + pl.program_id(1)
    steps = pl.num_programs(0) * pl.num_programs(1)

    @pl.when(step == 0)
    def begin():
        greet(bit_count)
        scatter.start()

    sine_rows = sine_ref[0]
    cosines = cos_ref[0]
    basis_low = jnp.concatenate([cosines, sine_rows], axis=-1).astype(jnp.bfloat16)
    half_width = sine_rows.shape[-1]
    queries, keys, values, sums_u, sums_v, places = ([], [], [], [], [], [])
    for head, at in enumerate(range(0, grad_query_ref.shape[-1], HEAD_DIM)):
        cols = slice(at, at + HEAD_DIM)
        query_u = qu_ref[0][:, cols]
        query_v = qv_ref[0][:, cols]
        key_low = key_ref[0][:, cols]
        place_head = place_ref[:, cols]
        grad_head = grad_ref[0][:, cols]
        probs_low = probs_ref[0, head]
        values.append(product_left(probs_low, grad_head))
        probs = probs_low.astype(jnp.float32)
        grad_probs = product_right(grad_head, value_ref[0][:, cols])
        inner_sum = jnp.sum(grad_probs * probs, axis=-1, keepdims=True)
        grad_scores = (probs * (grad_probs - inner_sum) * (1.0 / math.sqrt(HEAD_DIM))).astype(
            jnp.bfloat16
        )
        grad_u = product(grad_scores, key_low)
        keys.append(product_left(grad_scores, query_u))
        grad_coeff = product(grad_scores, basis_low)
        grad_a = grad_coeff[:, :half_width]
        grad_b = grad_coeff[:, half_width:]
        grad_raw = jnp.concatenate(
            [grad_a * sine_rows - grad_b * cosines, grad_a * cosines + grad_b * sine_rows],
            axis=-1,
        ).astype(jnp.bfloat16)
        grad_v = product(grad_raw, place_head)
        places.append(product_left(grad_raw, query_v))
        queries.append(grad_u + grad_v)
        sums_u.append(jnp.sum(grad_u, axis=0, keepdims=True))
        sums_v.append(jnp.sum(grad_v, axis=0, keepdims=True))
    grad_query_ref[0] = jnp.concatenate(queries, axis=-1).astype(jnp.bfloat16)
    grad_key_ref[0] = jnp.concatenate(keys, axis=-1).astype(jnp.bfloat16)
    grad_value_ref[0] = jnp.concatenate(values, axis=-1).astype(jnp.bfloat16)
    row_u = jnp.concatenate(sums_u, axis=-1)
    row_v = jnp.concatenate(sums_v, axis=-1)
    at_row = lax.broadcasted_iota(jnp.int32, grad_bias_ref.shape[1:], 0)
    grad_bias_ref[0] = jnp.where(at_row == 0, row_u, jnp.where(at_row == 1, row_v, 0.0))
    grad_place_ref[0] = jnp.concatenate(places, axis=-1)

    @pl.when(step == 0)
    def pair():
        scatter.add_pair()

    for phase in range(bit_count):
        when = (2, 4, 5)[phase] if phase < min(3, bit_count - 1) else steps - 1

        @pl.when(step == when)
        def go(phase=phase):
            scatter.advance(phase)

    @pl.when(step == steps - 1)
    def end():
        scatter.finish()


def attention_specs(clip_length, model_width):
    rows = pl.BlockSpec((1, clip_length, 128), lambda i, j: (i, 0, j))
    place = pl.BlockSpec((model_width, 128), lambda i, j: (0, j))
    wave = pl.BlockSpec((1, clip_length, model_width // 2), lambda i, j: (i, 0, 0))
    return (rows, place, wave)


def attention_inputs(joint_clips, gains, model_width):
    query = joint_clips[..., :model_width]
    return (
        (query + gains[2]).astype(jnp.bfloat16),
        (query + gains[3]).astype(jnp.bfloat16),
        joint_clips[..., model_width : 2 * model_width].astype(jnp.bfloat16),
        joint_clips[..., 2 * model_width :].astype(jnp.bfloat16),
    )


def attention_forward(parts, place_full, sine_rows, cosines, shards, wanted, collective_id):
    clip_count, clip_length, model_width = parts[0].shape
    rows, place, wave = attention_specs(clip_length, model_width)
    bit_count = (lax.axis_size("shard") - 1).bit_length()
    ins = [halves(array) for array in shards]
    pieces = plan_pieces([array.shape[1:] for array in ins], wanted)
    lead = (2,) * bit_count
    whole = pl.BlockSpec(memory_space=pl.ANY)
    heads = model_width // HEAD_DIM
    outs = pl.pallas_call(
        functools.partial(forward_kernel, bit_count, pieces, len(ins)),
        grid=(clip_count, model_width // 128),
        in_specs=[rows, rows, rows, rows, place, wave, wave] + [whole] * len(ins),
        out_specs=[
            rows,
            pl.BlockSpec((1, 2, clip_length, clip_length), lambda i, j: (i, j, 0, 0)),
        ]
        + [whole] * len(ins),
        out_shape=[
            jax.ShapeDtypeStruct(parts[0].shape, jnp.bfloat16),
            jax.ShapeDtypeStruct((clip_count, heads, clip_length, clip_length), jnp.bfloat16),
        ]
        + [jax.ShapeDtypeStruct(lead + array.shape, BF16) for array in ins],
        scratch_shapes=Gather.scratch(bit_count, pieces, len(ins)),
        compiler_params=pltpu.CompilerParams(
            vmem_limit_bytes=48 * 1024 * 1024, collective_id=collective_id, has_side_effects=True
        ),
        cost_estimate=pl.CostEstimate(
            flops=16000000000, bytes_accessed=12000000, transcendentals=5000000
        ),
    )(*parts, place_full, sine_rows, cosines, *ins)
    fulls = [out.reshape(-1, array.shape[1]) for out, array in zip(outs[2:], shards)]
    return outs[0], outs[1], fulls


def attention_backward(
    parts, grad_context, place_full, sine_rows, cosines, probs, partials, wanted, collective_id
):
    clip_count, clip_length, model_width = parts[0].shape
    rows, place, wave = attention_specs(clip_length, model_width)
    like = jax.ShapeDtypeStruct(parts[0].shape, jnp.bfloat16)
    bit_count, ins, pieces, shapes = scatter_plan(partials, wanted)
    outs = pl.pallas_call(
        functools.partial(backward_kernel, bit_count, pieces, len(ins)),
        grid=(clip_count, model_width // 128),
        in_specs=[
            rows,
            rows,
            rows,
            rows,
            rows,
            place,
            wave,
            wave,
            pl.BlockSpec((1, 2, clip_length, clip_length), lambda i, j: (i, j, 0, 0)),
        ]
        + [pl.BlockSpec(memory_space=pl.ANY)] * len(ins),
        out_specs=[
            rows,
            rows,
            rows,
            pl.BlockSpec((1, 8, 128), lambda i, j: (i, 0, j)),
            pl.BlockSpec((1, model_width, 128), lambda i, j: (i, 0, j)),
        ]
        + [pl.BlockSpec(shape.shape, lambda i, j: (0, 0, 0)) for shape in shapes],
        out_shape=[
            like,
            like,
            like,
            jax.ShapeDtypeStruct((clip_count, 8, model_width), jnp.float32),
            jax.ShapeDtypeStruct((clip_count, model_width, model_width), jnp.float32),
        ]
        + shapes,
        scratch_shapes=Scatter.scratch(bit_count, pieces),
        compiler_params=pltpu.CompilerParams(
            vmem_limit_bytes=56 * 1024 * 1024, collective_id=collective_id, has_side_effects=True
        ),
        cost_estimate=pl.CostEstimate(
            flops=80000000000, bytes_accessed=20000000, transcendentals=5000000
        ),
    )(*parts, grad_context, place_full, sine_rows, cosines, probs, *ins)
    return outs[:5], outs[5:]


def pack_small(columns):
    joined = jnp.concatenate(columns, axis=1)
    return jnp.pad(joined, ((0, 0), (0, -joined.shape[1] % 128)))


MESH = pl.DeviceIdType.MESH
BF16 = jnp.bfloat16
F32 = jnp.float32


def bit_of(index, bit):
    return lax.rem(lax.div(index, 1 << bit), 2)


def flip_bit(index, bit):
    return index + (1 - 2 * bit_of(index, bit)) * (1 << bit)


def link_orders(bit_count):
    far = list(range(bit_count - 1, 2, -1))
    if bit_count < 3:
        return [list(range(bit_count))] * 3
    return [far + [1, 2, 0], far + [2, 0, 1], far + [0, 1, 2]]


def greet(bit_count):
    shard = lax.axis_index("shard")
    replica = lax.axis_index("replica")
    barrier = pltpu.get_barrier_semaphore()
    for bit in range(bit_count):
        pl.semaphore_signal(
            barrier, inc=1, device_id={"shard": flip_bit(shard, bit)}, device_id_type=MESH
        )
    pl.semaphore_signal(
        barrier, inc=1, device_id={"replica": flip_bit(replica, 0)}, device_id_type=MESH
    )
    pl.semaphore_wait(barrier, bit_count + 1)


def block_index(bit_count, free_bits, values):
    return tuple(
        slice(None) if bit in free_bits else values[bit] for bit in range(bit_count - 1, -1, -1)
    )


class Piece:
    def __init__(self, array, color, rows, cols):
        self.array, self.color, self.rows, self.cols = array, color, rows, cols

    @property
    def tail(self):
        return (pl.ds(*self.rows), pl.ds(*self.cols))

    @property
    def shape(self):
        return (self.rows[1], self.cols[1])


def plan_pieces(shapes, wanted):
    pieces = []
    for array, color, low, high in wanted:
        rows, cols = shapes[array]
        if cols >= 2048 or cols % (16 * 128) == 0 or rows < 32:
            unit = cols // 128
            a, b = unit * low // 16 * 128, unit * high // 16 * 128
            wide = ((0, rows), (a, b - a))
        else:
            unit = rows // 16
            a, b = unit * low // 16 * 16, unit * high // 16 * 16
            wide = ((a, b - a), (0, cols))
        if b > a:
            pieces.append(Piece(array, color, *wide))
    return pieces


class Gather:
    def __init__(self, bit_count, pieces, ins, outs, sems):
        self.bits, self.pieces, self.ins, self.outs = bit_count, pieces, ins, outs
        self.send, self.recv, self.core_send, self.core_recv, self.local = sems
        shard = lax.axis_index("shard")
        replica = lax.axis_index("replica")
        self.shard, self.half = shard, lax.rem(replica, 2)
        self.core = {"replica": flip_bit(replica, 0)}
        self.own = [bit_of(shard, bit) for bit in range(bit_count)]
        self.orders = link_orders(bit_count)

    @staticmethod
    def scratch(bit_count, pieces, array_count):
        grid = (len(pieces), bit_count)
        return [pltpu.SemaphoreType.DMA(grid)] * 4 + [pltpu.SemaphoreType.DMA((array_count,))]

    def local_copies(self):
        index = block_index(self.bits, (), self.own)
        return [
            pltpu.make_async_copy(self.ins[a], self.outs[a].at[index], self.local.at[a])
            for a in range(len(self.ins))
        ]

    def hop(self, p, step):
        piece = self.pieces[p]
        order = self.orders[piece.color]
        out = self.outs[piece.array]
        index = block_index(self.bits, order[:step], self.own)
        region = out.at[index + (self.half,) + piece.tail]
        if step == 0:
            source = self.ins[piece.array].at[(self.half,) + piece.tail]
        else:
            source = region
        return pltpu.make_async_remote_copy(
            source,
            region,
            self.send.at[p, step],
            self.recv.at[p, step],
            device_id={"shard": flip_bit(self.shard, order[step])},
            device_id_type=MESH,
        )

    def cross(self, p, step):
        piece = self.pieces[p]
        order = self.orders[piece.color]
        values = list(self.own)
        values[order[step]] = 1 - values[order[step]]
        index = block_index(self.bits, order[:step], values)
        region = self.outs[piece.array].at[index + (self.half,) + piece.tail]
        return pltpu.make_async_remote_copy(
            region,
            region,
            self.core_send.at[p, step],
            self.core_recv.at[p, step],
            device_id=self.core,
            device_id_type=MESH,
        )

    def start(self):
        for p in range(len(self.pieces)):
            self.hop(p, 0).start()
        for copy in self.local_copies():
            copy.start()

    def advance(self, step, which=None):
        if step == 0:
            for copy in self.local_copies():
                copy.wait()
        for p in range(len(self.pieces)):
            self.hop(p, step).wait_recv()
            if step + 1 < self.bits:
                self.hop(p, step + 1).start()
            self.cross(p, step).start()

    def finish(self):
        for p in range(len(self.pieces)):
            for step in range(self.bits):
                self.hop(p, step).wait_send()
                self.cross(p, step).wait()


class Scatter:
    def __init__(self, bit_count, pieces, ins, outs, refs):
        self.bits, self.pieces, self.ins, self.outs = bit_count, pieces, ins, outs
        count = len(pieces)
        self.first = refs[:count]
        self.total = refs[count : 2 * count]
        self.last = refs[2 * count : 3 * count]
        self.send, self.recv, self.local = refs[3 * count : 3 * count + 3]
        land = refs[3 * count + 3 :]
        self.land = [land[p * bit_count : (p + 1) * bit_count] for p in range(count)]
        shard = lax.axis_index("shard")
        replica = lax.axis_index("replica")
        self.shard, self.half = shard, lax.rem(replica, 2)
        self.core = {"replica": flip_bit(replica, 0)}
        self.own = [bit_of(shard, bit) for bit in range(bit_count)]
        self.orders = [order[::-1] for order in link_orders(bit_count)]

    @staticmethod
    def scratch(bit_count, pieces):
        lead = (2,) * bit_count
        return (
            [pltpu.VMEM(lead + piece.shape, BF16) for piece in pieces]
            + [pltpu.VMEM(lead + piece.shape, BF16) for piece in pieces]
            + [pltpu.VMEM(piece.shape, BF16) for piece in pieces]
            + [pltpu.SemaphoreType.DMA((len(pieces), bit_count + 2))] * 2
            + [pltpu.SemaphoreType.DMA((len(pieces),))]
            + [
                pltpu.VMEM((2,) * (bit_count - step - 1) + piece.shape, BF16)
                for piece in pieces
                for step in range(bit_count)
            ]
        )

    def copy(self, p, step, source, target, device):
        return pltpu.make_async_remote_copy(
            source,
            target,
            self.send.at[p, step],
            self.recv.at[p, step],
            device_id=device,
            device_id_type=MESH,
        )

    def pair(self, p):
        piece = self.pieces[p]
        lead = (slice(None),) * self.bits
        source = self.ins[piece.array].at[lead + (1 - self.half,) + piece.tail]
        return self.copy(p, 0, source, self.first[p], self.core)

    def keep(self, p):
        piece = self.pieces[p]
        lead = (slice(None),) * self.bits
        source = self.ins[piece.array].at[lead + (self.half,) + piece.tail]
        return pltpu.make_async_copy(source, self.total[p], self.local.at[p])

    def hop(self, p, step):
        order = self.orders[self.pieces[p].color]
        bit = order[step]
        values = list(self.own)
        values[bit] = 1 - values[bit]
        index = block_index(self.bits, order[step + 1 :], values)
        return self.copy(
            p,
            step + 1,
            self.total[p].at[index],
            self.land[p][step],
            {"shard": flip_bit(self.shard, bit)},
        )

    def final(self, p):
        index = block_index(self.bits, (), self.own)
        return self.copy(p, self.bits + 1, self.total[p].at[index], self.last[p], self.core)

    def spread(self, number, free_bits):
        values = list(self.own)
        place = 0
        for bit in sorted(free_bits):
            values[bit] = bit_of(number, place)
            place += 1
        return block_index(self.bits, (), values)

    def start(self, which=None):
        for p in range(len(self.pieces)):
            self.pair(p).start()
            self.keep(p).start()

    def add_pair(self):
        for p, piece in enumerate(self.pieces):
            self.pair(p).wait_recv()
            self.keep(p).wait()
            every = range(self.bits)

            def add(number, carry):
                index = self.spread(number, every)
                mine = self.total[p][index]
                theirs = self.first[p][index]
                self.total[p][index] = (mine.astype(F32) + theirs.astype(F32)).astype(BF16)
                return carry

            lax.fori_loop(0, 1 << self.bits, add, 0)
            self.hop(p, 0).start()

    def advance(self, step):
        for p, piece in enumerate(self.pieces):
            order = self.orders[piece.color]
            self.hop(p, step).wait_recv()
            count = 1 << (self.bits - step - 1)
            left = order[step + 1 :]

            def add(number, carry):
                index = self.spread(number, left)
                mine = self.total[p][index]
                free = sorted(left, reverse=True)
                at = tuple(bit_of(number, len(free) - 1 - n) for n in range(len(free)))
                theirs = self.land[p][step][at] if at else self.land[p][step][...]
                self.total[p][index] = (mine.astype(F32) + theirs.astype(F32)).astype(BF16)
                return carry

            lax.fori_loop(0, count, add, 0)
            if step + 1 < self.bits:
                self.hop(p, step + 1).start()
            else:
                self.final(p).start()

    def finish(self):
        index = block_index(self.bits, (), self.own)
        for p, piece in enumerate(self.pieces):
            self.outs[piece.array][(self.half,) + piece.tail] = self.total[p][index]
            self.final(p).wait_recv()
            self.outs[piece.array][(1 - self.half,) + piece.tail] = self.last[p][...]
        for p in range(len(self.pieces)):
            self.pair(p).wait_send()
            for step in range(self.bits):
                self.hop(p, step).wait_send()
            self.final(p).wait_send()


def gather_kernel(bit_count, pieces, array_count, *refs):
    ins, outs = refs[:array_count], refs[array_count : 2 * array_count]
    greet(bit_count)
    work = Gather(bit_count, pieces, ins, outs, refs[2 * array_count :])
    work.start()
    for step in range(bit_count):
        work.advance(step)
    work.finish()


def halves(array):
    return array.reshape(2, array.shape[0] // 2, array.shape[1])


def gather_arrays(arrays, wanted, collective_id):
    bit_count = (lax.axis_size("shard") - 1).bit_length()
    ins = [halves(array) for array in arrays]
    pieces = plan_pieces([array.shape[1:] for array in ins], wanted)
    lead = (2,) * bit_count
    outs = pl.pallas_call(
        functools.partial(gather_kernel, bit_count, pieces, len(ins)),
        in_specs=[pl.BlockSpec(memory_space=pl.ANY)] * len(ins),
        out_specs=[pl.BlockSpec(memory_space=pl.ANY)] * len(ins),
        out_shape=[jax.ShapeDtypeStruct(lead + array.shape, BF16) for array in ins],
        scratch_shapes=Gather.scratch(bit_count, pieces, len(ins)),
        compiler_params=pltpu.CompilerParams(collective_id=collective_id, has_side_effects=True),
    )(*ins)
    return [
        out.reshape(-1, array.shape[1]) for out, array in zip(outs, arrays)
    ]


def scatter_kernel(bit_count, pieces, array_count, *refs):
    ins, outs = refs[:array_count], refs[array_count : 2 * array_count]
    greet(bit_count)
    work = Scatter(bit_count, pieces, ins, outs, refs[2 * array_count :])
    work.start()
    work.add_pair()
    for step in range(bit_count):
        work.advance(step)
    work.finish()


def scatter_plan(arrays, wanted):
    shards = lax.axis_size("shard")
    bit_count = (shards - 1).bit_length()
    lead = (2,) * bit_count
    ins = [
        array.reshape(lead + (2, array.shape[0] // (2 * shards), array.shape[1]))
        for array in arrays
    ]
    pieces = plan_pieces([array.shape[-2:] for array in ins], wanted)
    shapes = [jax.ShapeDtypeStruct((2,) + array.shape[-2:], BF16) for array in ins]
    return bit_count, ins, pieces, shapes


def scatter_arrays(arrays, wanted, collective_id):
    bit_count, ins, pieces, shapes = scatter_plan(arrays, wanted)
    return pl.pallas_call(
        functools.partial(scatter_kernel, bit_count, pieces, len(ins)),
        in_specs=[pl.BlockSpec(memory_space=pl.ANY)] * len(ins),
        out_specs=[pl.BlockSpec(memory_space=pltpu.VMEM)] * len(ins),
        out_shape=shapes,
        scratch_shapes=Scatter.scratch(bit_count, pieces),
        compiler_params=pltpu.CompilerParams(
            collective_id=collective_id,
            has_side_effects=True,
            vmem_limit_bytes=48 * 1024 * 1024,
        ),
    )(*ins)


def widen_kernel(count, row_total, tap_total, *refs):
    ins, extra_ref, outs = refs[:count], refs[count], refs[count + 1 :]
    for source, target in zip(ins[:-1], outs[:-2]):
        target[...] = source[...].astype(F32)
    small = ins[-1][...].astype(F32).T
    outs[-2][...] = small[:row_total] + extra_ref[...]
    outs[-1][...] = small[row_total : row_total + tap_total]


def widen(sums, extra_rows, tap_total):
    sums = [total.reshape(-1, total.shape[-1]) for total in sums]
    replicas = lax.axis_size("replica")
    if replicas > 2:
        groups = [list(range(core, replicas, 2)) for core in range(2)]
        sums = [lax.psum(total, "replica", axis_index_groups=groups) for total in sums]
    row_total, depth = extra_rows.shape
    shapes = [total.shape for total in sums[:-1]] + [(row_total, depth), (tap_total, depth)]
    return pl.pallas_call(
        functools.partial(widen_kernel, len(sums), row_total, tap_total),
        in_specs=[pl.BlockSpec(memory_space=pltpu.VMEM)] * (len(sums) + 1),
        out_specs=[pl.BlockSpec(memory_space=pltpu.VMEM)] * len(shapes),
        out_shape=[jax.ShapeDtypeStruct(shape, F32) for shape in shapes],
        compiler_params=pltpu.CompilerParams(vmem_limit_bytes=32 * 1024 * 1024),
    )(*sums, extra_rows)


def everyone(combine, count, in_ref, out_ref, held, send_sem, recv_sem):
    shards = lax.axis_size("shard")
    me = lax.axis_index("replica") * shards + lax.axis_index("shard")
    barrier = pltpu.get_barrier_semaphore()

    def place(device):
        return (lax.div(device, shards), lax.rem(device, shards))

    def hello(far, carry):
        pl.semaphore_signal(
            barrier, inc=1, device_id=place(lax.rem(me + far, count)), device_id_type=MESH
        )
        return carry

    lax.fori_loop(1, count, hello, 0)
    pl.semaphore_wait(barrier, count - 1)

    def copy(far, slot):
        return pltpu.make_async_remote_copy(
            in_ref,
            held.at[slot],
            send_sem.at[far],
            recv_sem.at[far],
            device_id=place(lax.rem(me + far, count)),
            device_id_type=MESH,
        )

    def go(far, carry):
        copy(far, me).start()
        return carry

    def arrive(far, carry):
        copy(far, lax.rem(me + count - far, count)).wait_recv()
        return carry

    def sent(far, carry):
        copy(far, me).wait_send()
        return carry

    lax.fori_loop(1, count, go, 0)
    held[me] = in_ref[...]
    lax.fori_loop(1, count, arrive, 0)
    out_ref[...] = combine(held[...])
    lax.fori_loop(1, count, sent, 0)


def combine_sums(tiles):
    return jnp.sum(tiles, axis=0)


def combine_stats(local_count, tiles):
    half = tiles.shape[1] // 2
    means = tiles[:, :half]
    mean = jnp.sum(means, axis=0) * (1.0 / tiles.shape[0])
    apart = means - mean
    total = jnp.sum(tiles[:, half:] + local_count * (apart * apart), axis=0)
    return jnp.concatenate([mean, total * (1.0 / (local_count * tiles.shape[0]))], axis=0)


def exchange_rows(upper, lower, combine, collective_id):
    width = upper.shape[0]
    tile = jnp.concatenate([upper.reshape(-1, 128), lower.reshape(-1, 128)], axis=0)
    count = lax.axis_size("replica") * lax.axis_size("shard")
    out = pl.pallas_call(
        functools.partial(everyone, combine, count),
        in_specs=[pl.BlockSpec(memory_space=pltpu.VMEM)],
        out_specs=pl.BlockSpec(memory_space=pltpu.VMEM),
        out_shape=jax.ShapeDtypeStruct(tile.shape, F32),
        scratch_shapes=[
            pltpu.VMEM((count,) + tile.shape, F32),
            pltpu.SemaphoreType.DMA((count,)),
            pltpu.SemaphoreType.DMA((count,)),
        ],
        compiler_params=pltpu.CompilerParams(collective_id=collective_id, has_side_effects=True),
    )(tile)
    return out[: width // 128].reshape(width), out[width // 128 :].reshape(width)


def tap_windows(padded_ref, start, rows, visit):
    for shift in range(8):
        window = padded_ref[start + shift : start + shift + rows + 24, :]
        for lift in range(4):
            offset = 8 * lift + shift
            if offset > 0:
                visit(offset, window[8 * lift : 8 * lift + rows])


def fill_padded(padded_ref, values):
    length = values.shape[0]
    edge = jnp.zeros((16, values.shape[1]), F32)
    padded_ref[0:16, :] = edge
    padded_ref[16 : 16 + length, :] = values
    padded_ref[16 + length : 32 + length, :] = edge


def tile_rows(length):
    for rows in (136, 128, 120, 112, 104, 96, 88, 80, 72, 64, 56, 48, 40, 32, 24, 16, 8):
        if length % rows == 0:
            return rows
    return length


def conv_forward_kernel(linear_ref, gate_ref, taps_ref, out_ref, stats_ref, padded_ref):
    length = out_ref.shape[1]
    rows = tile_rows(length)
    fill_padded(padded_ref, linear_ref[0] * jax.nn.sigmoid(gate_ref[0]))
    for start in range(0, length, rows):
        total = [jnp.zeros((rows, out_ref.shape[2]), F32)]

        def visit(offset, window):
            total[0] = total[0] + taps_ref[offset - 1 : offset, :] * window

        tap_windows(padded_ref, start, rows, visit)
        out_ref[0, start : start + rows, :] = total[0]
    values = out_ref[0]
    mean = jnp.sum(values, axis=0, keepdims=True) * (1.0 / length)
    apart = values - mean
    squares = jnp.sum(apart * apart, axis=0, keepdims=True)
    at_row = lax.broadcasted_iota(jnp.int32, stats_ref.shape[1:], 0)
    stats_ref[0] = jnp.where(at_row == 0, mean, jnp.where(at_row == 1, squares, 0.0))


def conv_forward(mixed_clips, taps):
    clip_count, clip_length, width = mixed_clips.shape
    channels = width // 2
    blocks = channels // 128
    piece = pl.BlockSpec((1, clip_length, 128), lambda i, j: (i, 0, j))
    return pl.pallas_call(
        conv_forward_kernel,
        grid=(clip_count, blocks),
        in_specs=[
            piece,
            pl.BlockSpec((1, clip_length, 128), lambda i, j: (i, 0, blocks + j)),
            pl.BlockSpec((taps.shape[0], 128), lambda i, j: (0, j)),
        ],
        out_specs=[piece, pl.BlockSpec((1, 8, 128), lambda i, j: (i, 0, j))],
        out_shape=[
            jax.ShapeDtypeStruct((clip_count, clip_length, channels), F32),
            jax.ShapeDtypeStruct((clip_count, 8, channels), F32),
        ],
        scratch_shapes=[pltpu.VMEM((clip_length + 32, 128), F32)],
        compiler_params=pltpu.CompilerParams(vmem_limit_bytes=32 * 1024 * 1024),
        cost_estimate=pl.CostEstimate(
            flops=80000000, bytes_accessed=8000000, transcendentals=600000
        ),
    )(mixed_clips, mixed_clips, taps)


def conv_backward_kernel(
    linear_ref, gate_ref, grad_ref, conv_ref, rows_ref, taps_ref,
    out_ref, grad_taps_ref, padded_ref, grad_padded_ref, tap_sums_ref,
):
    length = grad_ref.shape[1]
    rows = tile_rows(length)
    block = pl.program_id(1)
    channels = out_ref.shape[2] // 2
    mean, inverse, scale = rows_ref[0:1, :], rows_ref[1:2, :], rows_ref[2:3, :]
    shift_mean, gain_mean = rows_ref[3:4, :], rows_ref[4:5, :]
    unit = (conv_ref[0] - mean) * inverse
    grad_conv = scale * (grad_ref[0] - shift_mean - unit * gain_mean)
    fill_padded(grad_padded_ref, grad_conv)
    fill_padded(padded_ref, linear_ref[0] * jax.nn.sigmoid(gate_ref[0]))
    tap_sums_ref[...] = jnp.zeros_like(tap_sums_ref)
    first = pl.multiple_of(block * 128, 128)
    second = pl.multiple_of(channels + block * 128, 128)
    for start in range(0, length, rows):
        grad_rows = grad_padded_ref[16 + start : 16 + start + rows, :]

        def visit(offset, window):
            product_rows = (grad_rows * window).reshape(rows // 8, 8, window.shape[1])
            tap_sums_ref[offset - 1] = tap_sums_ref[offset - 1] + jnp.sum(product_rows, axis=0)

        tap_windows(padded_ref, start, rows, visit)
        total = [jnp.zeros((rows, 128), F32)]

        def visit_back(offset, window):
            total[0] = total[0] + taps_ref[31 - offset : 32 - offset, :] * window

        tap_windows(grad_padded_ref, start, rows, visit_back)
        grad_gated = total[0]
        gate = jax.nn.sigmoid(gate_ref[0, start : start + rows, :])
        grad_linear = grad_gated * gate
        linear = linear_ref[0, start : start + rows, :]
        out_ref[0, start : start + rows, pl.ds(first, 128)] = grad_linear.astype(BF16)
        out_ref[0, start : start + rows, pl.ds(second, 128)] = (
            grad_linear * linear * (1.0 - gate)
        ).astype(BF16)
    grad_taps_ref[0] = jnp.sum(tap_sums_ref[...], axis=1)


def conv_backward(mixed_clips, grad_clips, conv_clips, rows, taps):
    clip_count, clip_length, width = mixed_clips.shape
    channels = width // 2
    blocks = channels // 128
    piece = pl.BlockSpec((1, clip_length, 128), lambda i, j: (i, 0, j))
    return pl.pallas_call(
        conv_backward_kernel,
        grid=(clip_count, blocks),
        in_specs=[
            piece,
            pl.BlockSpec((1, clip_length, 128), lambda i, j: (i, 0, blocks + j)),
            piece,
            piece,
            pl.BlockSpec((8, 128), lambda i, j: (0, j)),
            pl.BlockSpec((taps.shape[0], 128), lambda i, j: (0, j)),
        ],
        out_specs=[
            pl.BlockSpec((1, clip_length, width), lambda i, j: (i, 0, 0)),
            pl.BlockSpec((1, 32, 128), lambda i, j: (i, 0, j)),
        ],
        out_shape=[
            jax.ShapeDtypeStruct((clip_count, clip_length, width), BF16),
            jax.ShapeDtypeStruct((clip_count, 32, channels), F32),
        ],
        scratch_shapes=[
            pltpu.VMEM((clip_length + 32, 128), F32),
            pltpu.VMEM((clip_length + 32, 128), F32),
            pltpu.VMEM((32, 8, 128), F32),
        ],
        compiler_params=pltpu.CompilerParams(vmem_limit_bytes=32 * 1024 * 1024),
        cost_estimate=pl.CostEstimate(
            flops=160000000, bytes_accessed=14000000, transcendentals=1200000
        ),
    )(mixed_clips, mixed_clips, grad_clips, conv_clips, rows, taps)


EARLY_PLAN = [
    (0, 0, 0, 10),
    (0, 1, 10, 16),
    (1, 1, 0, 4),
    (1, 2, 4, 16),
    (2, 0, 0, 16),
    (3, 0, 0, 6),
    (3, 1, 6, 16),
    (4, 2, 0, 16),
]
LATE_PLAN = [(0, 1, 0, 16), (1, 1, 0, 16), (2, 1, 0, 16), (3, 0, 0, 16), (4, 2, 0, 16)]
LATE_BACK_PLAN = [(0, 1, 0, 16), (1, 1, 0, 16), (2, 0, 0, 16), (3, 2, 0, 16)]
EARLY_BACK_PLAN = [
    (0, 0, 0, 10),
    (0, 1, 10, 16),
    (1, 1, 0, 4),
    (1, 2, 4, 16),
    (2, 0, 0, 8),
    (2, 1, 8, 16),
    (3, 1, 0, 16),
    (4, 2, 0, 16),
    (5, 0, 0, 16),
]


def body(
    features,
    frame_times,
    cotangent,
    vectors,
    first_up,
    first_down,
    query_key_value,
    place_weight,
    out_weight,
    point_glu,
    depth_taps,
    point_out,
    second_up,
    second_down,
):
    clip_count, clip_length, model_width = features.shape
    row_count = clip_count * clip_length
    token_count = row_count * lax.axis_size("replica") * lax.axis_size("shard")

    shards = lax.axis_size("shard")
    depth = first_up.shape[0]
    hidden_width = first_up.shape[1]
    row_total = vectors.shape[0]
    tap_total = depth_taps.shape[0]

    small_shard = pack_small([vectors.T, depth_taps.T])
    up_one, down_one, small_full, joint_full, place_full = gather_arrays(
        [first_up, first_down, small_shard, query_key_value, place_weight], EARLY_PLAN, 1
    )
    small = small_full.T
    first_full = (small[:row_total], up_one, down_one)
    gains = first_full[0].astype(jnp.float32)
    inputs = features.reshape(row_count, model_width).astype(jnp.float32)
    first_out, first_kept = feed_forward(inputs, gains[0], first_full[1], first_full[2])
    after_first = inputs + 0.5 * first_out
    normed_attend = normalize(after_first, gains[1]).astype(jnp.bfloat16)
    joint_rows = product(normed_attend, joint_full)
    joint_clips = joint_rows.reshape(clip_count, clip_length, 3 * model_width)
    attend_parts = attention_inputs(joint_clips, gains, model_width)
    sine_flat, cos_flat = wave_table(frame_times.reshape(row_count), model_width)
    sine_rows = sine_flat.reshape(clip_count, clip_length, -1)
    cosines = cos_flat.reshape(clip_count, clip_length, -1)
    context_clips, probs, late_full = attention_forward(
        attend_parts,
        place_full,
        sine_rows,
        cosines,
        [out_weight, point_glu, point_out, second_up, second_down],
        LATE_PLAN,
        2,
    )
    out_full = late_full[0]
    conv_full = (late_full[1], small[row_total : row_total + tap_total], late_full[2])
    second_full = late_full[3:]
    context_low = context_clips.reshape(row_count, model_width)
    after_attend = after_first + product(context_low, out_full)
    normed_conv = normalize(after_attend, gains[4]).astype(jnp.bfloat16)
    mixed_rows = product(normed_conv, conv_full[0]).reshape(
        clip_count, clip_length, 2 * model_width
    )
    taps = jnp.pad(conv_full[1].astype(jnp.float32), ((0, 32 - tap_total), (0, 0)))
    conv_clips, clip_stats = conv_forward(mixed_rows, taps)
    conv_flat = conv_clips.reshape(row_count, model_width)
    clip_means = clip_stats[:, 0]
    local_mean = jnp.mean(clip_means, axis=0)
    apart = clip_means - local_mean
    local_squares = jnp.sum(clip_stats[:, 1] + clip_length * (apart * apart), axis=0)
    channel_mean, variance = exchange_rows(
        local_mean,
        local_squares,
        functools.partial(combine_stats, row_count),
        3,
    )
    centered = conv_flat - channel_mean
    inverse = lax.rsqrt(variance + epsilon)
    unit_values = centered * inverse
    shaped = unit_values * gains[5] + gains[6]
    active_conv = swish_act(shaped).astype(jnp.bfloat16)
    after_conv = after_attend + product(active_conv, conv_full[2])
    second_out, second_kept = feed_forward(after_conv, gains[7], second_full[0], second_full[1])
    after_second = after_conv + 0.5 * second_out
    output = normalize(after_second, gains[8])
    grad_last, grad_final_gain = normalize_back(
        after_second, gains[8], cotangent.reshape(row_count, model_width).astype(jnp.float32)
    )
    second_back = second_full
    grad_conv_out, grad_second_gain, grad_second_up, grad_second_down = feed_back(
        grad_last, after_conv, gains[7], second_back[0], second_back[1], second_kept
    )
    conv_back = conv_full
    grad_low = grad_conv_out.astype(jnp.bfloat16)
    grad_point_out = product_left(active_conv, grad_low)
    grad_shaped = product_right(grad_low, conv_back[2]) * swish_slope(shaped)
    shift_total, gain_total = exchange_rows(
        jnp.sum(grad_shaped, axis=0), jnp.sum(grad_shaped * unit_values, axis=0), combine_sums, 4
    )
    zero_row = jnp.zeros_like(inverse)
    batch_rows = jnp.stack(
        [
            channel_mean,
            inverse,
            gains[5] * inverse,
            shift_total / token_count,
            gain_total / token_count,
            zero_row,
            zero_row,
            zero_row,
        ]
    )
    grad_mixed_clips, clip_taps = conv_backward(
        mixed_rows,
        grad_shaped.reshape(clip_count, clip_length, model_width),
        conv_clips,
        batch_rows,
        taps,
    )
    grad_taps = jnp.sum(clip_taps, axis=0)[:tap_total]
    grad_mixed_low = grad_mixed_clips.reshape(row_count, 2 * model_width)
    grad_point_glu = product_left(normed_conv, grad_mixed_low)
    grad_extra, grad_conv_gain = normalize_back(
        after_attend, gains[4], product_right(grad_mixed_low, conv_back[0])
    )
    grad_attend_out = grad_conv_out + grad_extra
    grad_low = grad_attend_out.astype(jnp.bfloat16)
    grad_out_weight = product_left(context_low, grad_low)
    grad_context = (
        product_right(grad_low, out_full)
        .astype(jnp.bfloat16)
        .reshape(clip_count, clip_length, model_width)
    )
    attend_grads, late_sums = attention_backward(
        attend_parts,
        grad_context,
        place_full,
        sine_rows,
        cosines,
        probs,
        [
            array.astype(BF16)
            for array in (grad_point_glu, grad_point_out, grad_second_up, grad_second_down)
        ],
        LATE_BACK_PLAN,
        5,
    )
    grad_query, grad_key, grad_value, grad_bias, grad_place = attend_grads
    bias_rows = jnp.sum(grad_bias, axis=0)
    bias_sums = (bias_rows[0], bias_rows[1])
    grad_joint_low = jnp.concatenate([grad_query, grad_key, grad_value], axis=-1).reshape(
        row_count, 3 * model_width
    )
    grad_qkv = product_left(normed_attend, grad_joint_low)
    grad_extra, grad_attend_gain = normalize_back(
        after_first, gains[1], product_right(grad_joint_low, joint_full)
    )
    grad_first_out = grad_attend_out + grad_extra
    grad_place_full = jnp.sum(grad_place, axis=0)
    first_back = first_full
    first_gains = first_back[0].astype(jnp.float32)
    grad_inputs, grad_first_gain, grad_first_up, grad_first_down = feed_back(
        grad_first_out, inputs, first_gains[0], first_back[1], first_back[2], first_kept
    )
    grad_rows = jnp.stack(
        [
            grad_first_gain,
            grad_attend_gain,
            bias_sums[0],
            bias_sums[1],
            grad_conv_gain,
            zero_row,
            zero_row,
            grad_second_gain,
            grad_final_gain,
        ]
    )
    partials = [
        grad_first_up,
        grad_first_down,
        grad_qkv,
        grad_place_full,
        grad_out_weight,
        pack_small([grad_rows.T, grad_taps.T]),
    ]
    early_sums = scatter_arrays([array.astype(BF16) for array in partials], EARLY_BACK_PLAN, 6)
    shard_cols = vectors.shape[1]
    first_col = lax.axis_index("shard") * shard_cols
    batch_grads = jnp.concatenate(
        [
            jnp.zeros((5, model_width), F32),
            gain_total[None],
            shift_total[None],
            jnp.zeros((row_total - 7, model_width), F32),
        ]
    )
    batch_grads = lax.dynamic_slice_in_dim(batch_grads, first_col, shard_cols, axis=1)
    summed = widen(
        [*early_sums[:5], *late_sums, early_sums[5]], batch_grads, tap_total
    )
    return (
        output.astype(jnp.bfloat16).reshape(clip_count, clip_length, model_width),
        grad_inputs.astype(jnp.bfloat16).reshape(clip_count, clip_length, model_width),
        summed[9],
        *summed[:6],
        summed[10],
        *summed[6:9],
    )


def solution(mesh):
    return jax.shard_map(
        body,
        mesh=mesh,
        in_specs=(
            P(("replica", "shard"), None, None),
            P(("replica", "shard"), None),
            P(("replica", "shard"), None, None),
            P(None, "shard"),
            P("shard", None),
            P("shard", None),
            P("shard", None),
            P("shard", None),
            P("shard", None),
            P("shard", None),
            P(None, "shard"),
            P("shard", None),
            P("shard", None),
            P("shard", None),
        ),
        out_specs=(
            P(("replica", "shard"), None, None),
            P(("replica", "shard"), None, None),
            P(None, "shard"),
            P("shard", None),
            P("shard", None),
            P("shard", None),
            P("shard", None),
            P("shard", None),
            P("shard", None),
            P(None, "shard"),
            P("shard", None),
            P("shard", None),
            P("shard", None),
        ),
        check_vma=False,
    )
```

```python
import functools
import math

import jax
import jax.numpy as jnp
from jax import lax
from jax.experimental import pallas as pl
from jax.experimental.pallas import tpu as pltpu
from jax.sharding import PartitionSpec as P

HEADS = 8
HEAD_DIM = 64


epsilon = 1e-05


def normalize(values, gain_row):
    center = values - jnp.mean(values, axis=-1, keepdims=True)
    spread = jnp.mean(center * center, axis=-1, keepdims=True)
    return center * lax.rsqrt(spread + epsilon) * gain_row


def normalize_back(values, gain_row, grad_normed):
    pull = jax.vjp(normalize, values, gain_row)[1]
    return pull(grad_normed)


def swish_act(values):
    return values * jax.nn.sigmoid(values)


def swish_slope(values):
    sigmoid = jax.nn.sigmoid(values)
    return sigmoid * (1.0 + values * (1.0 - sigmoid))


def wave_table(frame_pos, model_width):
    half_width = model_width // 2
    frequency = jnp.exp(
        jnp.arange(half_width, dtype=jnp.float32) * (-math.log(10000.0) / half_width)
    )
    angles = frame_pos.astype(jnp.float32)[:, None] * frequency[None, :]
    return (jnp.sin(angles), jnp.cos(angles))


def product(left_side, right_side):
    return jnp.dot(left_side, right_side, preferred_element_type=jnp.float32)


def product_left(left_side, right_side):
    return lax.dot_general(
        left_side, right_side, (((0,), (0,)), ((), ())), preferred_element_type=jnp.float32
    )


def product_right(left_side, right_side):
    return lax.dot_general(
        left_side, right_side, (((1,), (1,)), ((), ())), preferred_element_type=jnp.float32
    )


def feed_forward(inputs, gain_row, up_full, down_full):
    normed_low = normalize(inputs, gain_row).astype(jnp.bfloat16)
    hidden = product(normed_low, up_full)
    active_low = swish_act(hidden).astype(jnp.bfloat16)
    return (product(active_low, down_full), (normed_low, hidden.astype(BF16), active_low))


def feed_back(grad_stream, inputs, gain_row, up_full, down_full, kept_values):
    normed_low, hidden, active_low = kept_values
    grad_low = (0.5 * grad_stream).astype(jnp.bfloat16)
    grad_down = product_left(active_low, grad_low)
    grad_hidden = (product_right(grad_low, down_full) * swish_slope(hidden.astype(F32))).astype(
        jnp.bfloat16
    )
    grad_up = product_left(normed_low, grad_hidden)
    grad_normed = product_right(grad_hidden, up_full)
    grad_extra, grad_gain = normalize_back(inputs, gain_row, grad_normed)
    return (grad_stream + grad_extra, grad_gain, grad_up, grad_down)


def head_probs(query_u, query_v, key_low, place_head, sine_rows, cosines, basis_low):
    raw_place = product_right(query_v, place_head)
    half_width = raw_place.shape[-1] // 2
    part_sin = raw_place[:, :half_width]
    part_cos = raw_place[:, half_width:]
    coeff_low = jnp.concatenate(
        [part_sin * sine_rows + part_cos * cosines, part_cos * sine_rows - part_sin * cosines],
        axis=-1,
    ).astype(jnp.bfloat16)
    scores = product_right(query_u, key_low) + product_right(coeff_low, basis_low)
    scores = scores * (1.0 / math.sqrt(HEAD_DIM))
    row_peak = jnp.max(scores, axis=-1, keepdims=True)
    raised = jnp.exp(scores - row_peak)
    return raised * (1.0 / jnp.sum(raised, axis=-1, keepdims=True))


def forward_kernel(bit_count, pieces, array_count, *refs):
    qu_ref, qv_ref, key_ref, value_ref, place_ref, sine_ref, cos_ref = refs[:7]
    shards = refs[7 : 7 + array_count]
    out_ref, probs_ref = refs[7 + array_count : 9 + array_count]
    fulls = refs[9 + array_count : 9 + 2 * array_count]
    gather = Gather(bit_count, pieces, shards, fulls, refs[9 + 2 * array_count :])
    step = pl.program_id(0) * pl.num_programs(1) + pl.program_id(1)
    steps = pl.num_programs(0) * pl.num_programs(1)

    @pl.when(step == 0)
    def begin():
        greet(bit_count)
        gather.start()

    sine_rows = sine_ref[0]
    cosines = cos_ref[0]
    basis_low = jnp.concatenate([cosines, sine_rows], axis=-1).astype(jnp.bfloat16)
    merged = []
    for head, at in enumerate(range(0, out_ref.shape[-1], HEAD_DIM)):
        cols = slice(at, at + HEAD_DIM)
        probs = head_probs(
            qu_ref[0][:, cols],
            qv_ref[0][:, cols],
            key_ref[0][:, cols],
            place_ref[:, cols],
            sine_rows,
            cosines,
            basis_low,
        ).astype(jnp.bfloat16)
        probs_ref[0, head] = probs
        merged.append(product(probs, value_ref[0][:, cols]))
    out_ref[0] = jnp.concatenate(merged, axis=-1).astype(jnp.bfloat16)

    for phase in range(bit_count):
        when = (2, 3, 5)[phase] if phase < min(3, bit_count - 1) else steps - 1

        @pl.when(step == when)
        def go(phase=phase):
            gather.advance(phase)

    @pl.when(step == steps - 1)
    def end():
        gather.finish()


def backward_kernel(bit_count, pieces, array_count, *refs):
    qu_ref, qv_ref, key_ref, value_ref, grad_ref, place_ref, sine_ref, cos_ref, probs_ref = refs[:9]
    partials = refs[9 : 9 + array_count]
    refs = refs[9 + array_count :]
    grad_query_ref, grad_key_ref, grad_value_ref, grad_bias_ref, grad_place_ref = refs[:5]
    owned = refs[5 : 5 + array_count]
    scatter = Scatter(bit_count, pieces, partials, owned, refs[5 + array_count :])
    step = pl.program_id(0) * pl.num_programs(1) + pl.program_id(1)
    steps = pl.num_programs(0) * pl.num_programs(1)

    @pl.when(step == 0)
    def begin():
        greet(bit_count)
        scatter.start()

    sine_rows = sine_ref[0]
    cosines = cos_ref[0]
    basis_low = jnp.concatenate([cosines, sine_rows], axis=-1).astype(jnp.bfloat16)
    half_width = sine_rows.shape[-1]
    queries, keys, values, sums_u, sums_v, places = ([], [], [], [], [], [])
    for head, at in enumerate(range(0, grad_query_ref.shape[-1], HEAD_DIM)):
        cols = slice(at, at + HEAD_DIM)
        query_u = qu_ref[0][:, cols]
        query_v = qv_ref[0][:, cols]
        key_low = key_ref[0][:, cols]
        place_head = place_ref[:, cols]
        grad_head = grad_ref[0][:, cols]
        probs_low = probs_ref[0, head]
        values.append(product_left(probs_low, grad_head))
        probs = probs_low.astype(jnp.float32)
        grad_probs = product_right(grad_head, value_ref[0][:, cols])
        inner_sum = jnp.sum(grad_probs * probs, axis=-1, keepdims=True)
        grad_scores = (probs * (grad_probs - inner_sum) * (1.0 / math.sqrt(HEAD_DIM))).astype(
            jnp.bfloat16
        )
        grad_u = product(grad_scores, key_low)
        keys.append(product_left(grad_scores, query_u))
        grad_coeff = product(grad_scores, basis_low)
        grad_a = grad_coeff[:, :half_width]
        grad_b = grad_coeff[:, half_width:]
        grad_raw = jnp.concatenate(
            [grad_a * sine_rows - grad_b * cosines, grad_a * cosines + grad_b * sine_rows],
            axis=-1,
        ).astype(jnp.bfloat16)
        grad_v = product(grad_raw, place_head)
        places.append(product_left(grad_raw, query_v))
        queries.append(grad_u + grad_v)
        sums_u.append(jnp.sum(grad_u, axis=0, keepdims=True))
        sums_v.append(jnp.sum(grad_v, axis=0, keepdims=True))
    grad_query_ref[0] = jnp.concatenate(queries, axis=-1).astype(jnp.bfloat16)
    grad_key_ref[0] = jnp.concatenate(keys, axis=-1).astype(jnp.bfloat16)
    grad_value_ref[0] = jnp.concatenate(values, axis=-1).astype(jnp.bfloat16)
    row_u = jnp.concatenate(sums_u, axis=-1)
    row_v = jnp.concatenate(sums_v, axis=-1)
    at_row = lax.broadcasted_iota(jnp.int32, grad_bias_ref.shape, 0)
    bias = jnp.where(at_row == 0, row_u, jnp.where(at_row == 1, row_v, 0.0))
    place_sum = jnp.concatenate(places, axis=-1)

    @pl.when(pl.program_id(1) == 0)
    def first_clip():
        grad_bias_ref[...] = bias
        grad_place_ref[...] = place_sum

    @pl.when(pl.program_id(1) > 0)
    def later_clip():
        grad_bias_ref[...] = grad_bias_ref[...] + bias
        grad_place_ref[...] = grad_place_ref[...] + place_sum

    @pl.when(step == 0)
    def pair():
        scatter.add_pair()

    for phase in range(bit_count):
        when = (2, 4, 5)[phase] if phase < min(3, bit_count - 1) else steps - 1

        @pl.when(step == when)
        def go(phase=phase):
            scatter.advance(phase)

    @pl.when(step == steps - 1)
    def end():
        scatter.finish()


def attention_specs(clip_length, model_width):
    rows = pl.BlockSpec((1, clip_length, 128), lambda i, j: (i, 0, j))
    place = pl.BlockSpec((model_width, 128), lambda i, j: (0, j))
    wave = pl.BlockSpec((1, clip_length, model_width // 2), lambda i, j: (i, 0, 0))
    return (rows, place, wave)


def attention_inputs(joint_clips, gains, model_width):
    query = joint_clips[..., :model_width]
    return (
        (query + gains[2]).astype(jnp.bfloat16),
        (query + gains[3]).astype(jnp.bfloat16),
        joint_clips[..., model_width : 2 * model_width].astype(jnp.bfloat16),
        joint_clips[..., 2 * model_width :].astype(jnp.bfloat16),
    )


def attention_forward(parts, place_full, sine_rows, cosines, shards, wanted, collective_id):
    clip_count, clip_length, model_width = parts[0].shape
    rows, place, wave = attention_specs(clip_length, model_width)
    bit_count = (lax.axis_size("shard") - 1).bit_length()
    ins = [halves(array) for array in shards]
    pieces = plan_pieces([array.shape[1:] for array in ins], wanted)
    lead = (2,) * bit_count
    whole = pl.BlockSpec(memory_space=pl.ANY)
    heads = model_width // HEAD_DIM
    outs = pl.pallas_call(
        functools.partial(forward_kernel, bit_count, pieces, len(ins)),
        grid=(clip_count, model_width // 128),
        in_specs=[rows, rows, rows, rows, place, wave, wave] + [whole] * len(ins),
        out_specs=[
            rows,
            pl.BlockSpec((1, 2, clip_length, clip_length), lambda i, j: (i, j, 0, 0)),
        ]
        + [whole] * len(ins),
        out_shape=[
            jax.ShapeDtypeStruct(parts[0].shape, jnp.bfloat16),
            jax.ShapeDtypeStruct((clip_count, heads, clip_length, clip_length), jnp.bfloat16),
        ]
        + [jax.ShapeDtypeStruct(lead + array.shape, BF16) for array in ins],
        scratch_shapes=Gather.scratch(bit_count, pieces, len(ins)),
        compiler_params=pltpu.CompilerParams(
            vmem_limit_bytes=48 * 1024 * 1024, collective_id=collective_id, has_side_effects=True
        ),
        cost_estimate=pl.CostEstimate(
            flops=16000000000, bytes_accessed=12000000, transcendentals=5000000
        ),
    )(*parts, place_full, sine_rows, cosines, *ins)
    fulls = [out.reshape(-1, array.shape[1]) for out, array in zip(outs[2:], shards)]
    return outs[0], outs[1], fulls


def attention_backward(
    parts, grad_context, place_full, sine_rows, cosines, probs, partials, wanted, collective_id
):
    clip_count, clip_length, model_width = parts[0].shape
    rows = pl.BlockSpec((1, clip_length, 128), lambda j, i: (i, 0, j))
    place = pl.BlockSpec((model_width, 128), lambda j, i: (0, j))
    wave = pl.BlockSpec((1, clip_length, model_width // 2), lambda j, i: (i, 0, 0))
    like = jax.ShapeDtypeStruct(parts[0].shape, jnp.bfloat16)
    bit_count, ins, pieces, shapes = scatter_plan(partials, wanted)
    outs = pl.pallas_call(
        functools.partial(backward_kernel, bit_count, pieces, len(ins)),
        grid=(model_width // 128, clip_count),
        in_specs=[
            rows,
            rows,
            rows,
            rows,
            rows,
            place,
            wave,
            wave,
            pl.BlockSpec((1, 2, clip_length, clip_length), lambda j, i: (i, j, 0, 0)),
        ]
        + [pl.BlockSpec(memory_space=pl.ANY)] * len(ins),
        out_specs=[
            rows,
            rows,
            rows,
            pl.BlockSpec((8, 128), lambda j, i: (0, j)),
            pl.BlockSpec((model_width, 128), lambda j, i: (0, j)),
        ]
        + [pl.BlockSpec(shape.shape, lambda i, j: (0, 0, 0)) for shape in shapes],
        out_shape=[
            like,
            like,
            like,
            jax.ShapeDtypeStruct((8, model_width), jnp.float32),
            jax.ShapeDtypeStruct((model_width, model_width), jnp.float32),
        ]
        + shapes,
        scratch_shapes=Scatter.scratch(bit_count, pieces),
        compiler_params=pltpu.CompilerParams(
            vmem_limit_bytes=56 * 1024 * 1024, collective_id=collective_id, has_side_effects=True
        ),
        cost_estimate=pl.CostEstimate(
            flops=80000000000, bytes_accessed=20000000, transcendentals=5000000
        ),
    )(*parts, grad_context, place_full, sine_rows, cosines, probs, *ins)
    return outs[:5], outs[5:]


def pack_small(columns):
    joined = jnp.concatenate(columns, axis=1)
    return jnp.pad(joined, ((0, 0), (0, -joined.shape[1] % 128)))


MESH = pl.DeviceIdType.MESH
BF16 = jnp.bfloat16
F32 = jnp.float32


def bit_of(index, bit):
    return lax.rem(lax.div(index, 1 << bit), 2)


def flip_bit(index, bit):
    return index + (1 - 2 * bit_of(index, bit)) * (1 << bit)


def link_orders(bit_count):
    far = list(range(bit_count - 1, 2, -1))
    if bit_count < 3:
        return [list(range(bit_count))] * 3
    return [far + [1, 2, 0], far + [2, 0, 1], far + [0, 1, 2]]


def greet(bit_count):
    shard = lax.axis_index("shard")
    replica = lax.axis_index("replica")
    barrier = pltpu.get_barrier_semaphore()
    for bit in range(bit_count):
        pl.semaphore_signal(
            barrier, inc=1, device_id={"shard": flip_bit(shard, bit)}, device_id_type=MESH
        )
    pl.semaphore_signal(
        barrier, inc=1, device_id={"replica": flip_bit(replica, 0)}, device_id_type=MESH
    )
    pl.semaphore_wait(barrier, bit_count + 1)


def block_index(bit_count, free_bits, values):
    return tuple(
        slice(None) if bit in free_bits else values[bit] for bit in range(bit_count - 1, -1, -1)
    )


class Piece:
    def __init__(self, array, color, rows, cols):
        self.array, self.color, self.rows, self.cols = array, color, rows, cols

    @property
    def tail(self):
        return (pl.ds(*self.rows), pl.ds(*self.cols))

    @property
    def shape(self):
        return (self.rows[1], self.cols[1])


def plan_pieces(shapes, wanted):
    pieces = []
    for array, color, low, high in wanted:
        rows, cols = shapes[array]
        if cols >= 2048 or cols % (16 * 128) == 0 or rows < 32:
            unit = cols // 128
            a, b = unit * low // 16 * 128, unit * high // 16 * 128
            wide = ((0, rows), (a, b - a))
        else:
            unit = rows // 16
            a, b = unit * low // 16 * 16, unit * high // 16 * 16
            wide = ((a, b - a), (0, cols))
        if b > a:
            pieces.append(Piece(array, color, *wide))
    return pieces


class Gather:
    def __init__(self, bit_count, pieces, ins, outs, sems):
        self.bits, self.pieces, self.ins, self.outs = bit_count, pieces, ins, outs
        self.send, self.recv, self.core_send, self.core_recv, self.local = sems
        shard = lax.axis_index("shard")
        replica = lax.axis_index("replica")
        self.shard, self.half = shard, lax.rem(replica, 2)
        self.core = {"replica": flip_bit(replica, 0)}
        self.own = [bit_of(shard, bit) for bit in range(bit_count)]
        self.orders = link_orders(bit_count)

    @staticmethod
    def scratch(bit_count, pieces, array_count):
        grid = (len(pieces), bit_count)
        return [pltpu.SemaphoreType.DMA(grid)] * 4 + [pltpu.SemaphoreType.DMA((array_count,))]

    def local_copies(self):
        index = block_index(self.bits, (), self.own)
        return [
            pltpu.make_async_copy(self.ins[a], self.outs[a].at[index], self.local.at[a])
            for a in range(len(self.ins))
        ]

    def hop(self, p, step):
        piece = self.pieces[p]
        order = self.orders[piece.color]
        out = self.outs[piece.array]
        index = block_index(self.bits, order[:step], self.own)
        region = out.at[index + (self.half,) + piece.tail]
        if step == 0:
            source = self.ins[piece.array].at[(self.half,) + piece.tail]
        else:
            source = region
        return pltpu.make_async_remote_copy(
            source,
            region,
            self.send.at[p, step],
            self.recv.at[p, step],
            device_id={"shard": flip_bit(self.shard, order[step])},
            device_id_type=MESH,
        )

    def cross(self, p, step):
        piece = self.pieces[p]
        order = self.orders[piece.color]
        values = list(self.own)
        values[order[step]] = 1 - values[order[step]]
        index = block_index(self.bits, order[:step], values)
        region = self.outs[piece.array].at[index + (self.half,) + piece.tail]
        return pltpu.make_async_remote_copy(
            region,
            region,
            self.core_send.at[p, step],
            self.core_recv.at[p, step],
            device_id=self.core,
            device_id_type=MESH,
        )

    def start(self):
        for p in range(len(self.pieces)):
            self.hop(p, 0).start()
        for copy in self.local_copies():
            copy.start()

    def advance(self, step, which=None):
        if step == 0:
            for copy in self.local_copies():
                copy.wait()
        for p in range(len(self.pieces)):
            self.hop(p, step).wait_recv()
            if step + 1 < self.bits:
                self.hop(p, step + 1).start()
            self.cross(p, step).start()

    def finish(self):
        for p in range(len(self.pieces)):
            for step in range(self.bits):
                self.hop(p, step).wait_send()
                self.cross(p, step).wait()


class Scatter:
    def __init__(self, bit_count, pieces, ins, outs, refs):
        self.bits, self.pieces, self.ins, self.outs = bit_count, pieces, ins, outs
        count = len(pieces)
        self.first = refs[:count]
        self.total = refs[count : 2 * count]
        self.last = refs[2 * count : 3 * count]
        self.send, self.recv, self.local = refs[3 * count : 3 * count + 3]
        land = refs[3 * count + 3 :]
        self.land = [land[p * bit_count : (p + 1) * bit_count] for p in range(count)]
        shard = lax.axis_index("shard")
        replica = lax.axis_index("replica")
        self.shard, self.half = shard, lax.rem(replica, 2)
        self.core = {"replica": flip_bit(replica, 0)}
        self.own = [bit_of(shard, bit) for bit in range(bit_count)]
        self.orders = [order[::-1] for order in link_orders(bit_count)]

    @staticmethod
    def scratch(bit_count, pieces):
        lead = (2,) * bit_count
        return (
            [pltpu.VMEM(lead + piece.shape, BF16) for piece in pieces]
            + [pltpu.VMEM(lead + piece.shape, BF16) for piece in pieces]
            + [pltpu.VMEM(piece.shape, BF16) for piece in pieces]
            + [pltpu.SemaphoreType.DMA((len(pieces), bit_count + 2))] * 2
            + [pltpu.SemaphoreType.DMA((len(pieces),))]
            + [
                pltpu.VMEM((2,) * (bit_count - step - 1) + piece.shape, BF16)
                for piece in pieces
                for step in range(bit_count)
            ]
        )

    def copy(self, p, step, source, target, device):
        return pltpu.make_async_remote_copy(
            source,
            target,
            self.send.at[p, step],
            self.recv.at[p, step],
            device_id=device,
            device_id_type=MESH,
        )

    def pair(self, p):
        piece = self.pieces[p]
        lead = (slice(None),) * self.bits
        source = self.ins[piece.array].at[lead + (1 - self.half,) + piece.tail]
        return self.copy(p, 0, source, self.first[p], self.core)

    def keep(self, p):
        piece = self.pieces[p]
        lead = (slice(None),) * self.bits
        source = self.ins[piece.array].at[lead + (self.half,) + piece.tail]
        return pltpu.make_async_copy(source, self.total[p], self.local.at[p])

    def hop(self, p, step):
        order = self.orders[self.pieces[p].color]
        bit = order[step]
        values = list(self.own)
        values[bit] = 1 - values[bit]
        index = block_index(self.bits, order[step + 1 :], values)
        return self.copy(
            p,
            step + 1,
            self.total[p].at[index],
            self.land[p][step],
            {"shard": flip_bit(self.shard, bit)},
        )

    def final(self, p):
        index = block_index(self.bits, (), self.own)
        return self.copy(p, self.bits + 1, self.total[p].at[index], self.last[p], self.core)

    def start(self, which=None):
        for p in range(len(self.pieces)) if which is None else which:
            self.pair(p).start()
            self.keep(p).start()

    def add_pair(self, which=None):
        for p in range(len(self.pieces)) if which is None else which:
            self.pair(p).wait_recv()
            self.keep(p).wait()
            self.total[p][...] = self.total[p][...] + self.first[p][...]
            self.hop(p, 0).start()

    def advance(self, step, which=None):
        for p in range(len(self.pieces)) if which is None else which:
            piece = self.pieces[p]
            order = self.orders[piece.color]
            self.hop(p, step).wait_recv()
            index = block_index(self.bits, order[step + 1 :], self.own)
            self.total[p][index] = self.total[p][index] + self.land[p][step][...]
            if step + 1 < self.bits:
                self.hop(p, step + 1).start()
            else:
                self.final(p).start()

    def finish(self):
        index = block_index(self.bits, (), self.own)
        for p, piece in enumerate(self.pieces):
            self.outs[piece.array][(self.half,) + piece.tail] = self.total[p][index]
            self.final(p).wait_recv()
            self.outs[piece.array][(1 - self.half,) + piece.tail] = self.last[p][...]
        for p in range(len(self.pieces)):
            self.pair(p).wait_send()
            for step in range(self.bits):
                self.hop(p, step).wait_send()
            self.final(p).wait_send()


def gather_kernel(bit_count, pieces, array_count, *refs):
    ins, outs = refs[:array_count], refs[array_count : 2 * array_count]
    greet(bit_count)
    work = Gather(bit_count, pieces, ins, outs, refs[2 * array_count :])
    work.start()
    for step in range(bit_count):
        work.advance(step)
    work.finish()


def halves(array):
    return array.reshape(2, array.shape[0] // 2, array.shape[1])


def gather_arrays(arrays, wanted, collective_id):
    bit_count = (lax.axis_size("shard") - 1).bit_length()
    ins = [halves(array) for array in arrays]
    pieces = plan_pieces([array.shape[1:] for array in ins], wanted)
    lead = (2,) * bit_count
    outs = pl.pallas_call(
        functools.partial(gather_kernel, bit_count, pieces, len(ins)),
        in_specs=[pl.BlockSpec(memory_space=pl.ANY)] * len(ins),
        out_specs=[pl.BlockSpec(memory_space=pl.ANY)] * len(ins),
        out_shape=[jax.ShapeDtypeStruct(lead + array.shape, BF16) for array in ins],
        scratch_shapes=Gather.scratch(bit_count, pieces, len(ins)),
        compiler_params=pltpu.CompilerParams(collective_id=collective_id, has_side_effects=True),
    )(*ins)
    return [
        out.reshape(-1, array.shape[1]) for out, array in zip(outs, arrays)
    ]


def scatter_plan(arrays, wanted):
    shards = lax.axis_size("shard")
    bit_count = (shards - 1).bit_length()
    lead = (2,) * bit_count
    ins = [
        array.reshape(lead + (2, array.shape[0] // (2 * shards), array.shape[1]))
        for array in arrays
    ]
    pieces = plan_pieces([array.shape[-2:] for array in ins], wanted)
    shapes = [jax.ShapeDtypeStruct((2,) + array.shape[-2:], BF16) for array in ins]
    return bit_count, ins, pieces, shapes


def row_step(count):
    for rows in (272, 256, 128, 64, 32, 16):
        if count % rows == 0:
            return rows
    return count


def loop_rows(count, visit, between=None):
    rows = row_step(count)
    steps = count // rows

    def step(number, carry):
        visit(pl.ds(pl.multiple_of(number * rows, 16), rows))
        if between is not None:
            for at in range(steps):

                @pl.when(number == at)
                def slot():
                    between()

        return carry

    lax.fori_loop(0, steps, step, ())


def standardize(values):
    center = values - jnp.mean(values, axis=-1, keepdims=True)
    spread = lax.rsqrt(jnp.mean(center * center, axis=-1, keepdims=True) + epsilon)
    return center * spread, spread


def standardize_back(grad, unit, spread):
    inner = jnp.mean(grad * unit, axis=-1, keepdims=True)
    return spread * (grad - jnp.mean(grad, axis=-1, keepdims=True) - unit * inner)


def store_blocks(ref, value, cols):
    value = value.reshape(ref.shape[:-1] + (value.shape[-1],))
    ref[(slice(None),) * (len(ref.shape) - 1) + (cols,)] = value.astype(BF16)


def tail_kernel(bit_count, pieces, groups, shapes, *refs):
    (
        gq_ref, gk_ref, gv_ref, attend_ref, after_ref, stream_ref, first_ref, features_ref,
        hidden_ref, gains_ref, joint_ref, up_ref, down_ref, bias_ref, conv_gain_ref, second_gain_ref,
        final_gain_ref, taps_ref, place_ref, out_w_ref,
    ) = refs[:20]
    grad_ref = refs[20]
    owned = refs[21:27]
    refs = refs[27:]
    (
        joint_grad, down_grad, up_grad, small_grad, stream, low, small_ref, active, normed_grad, sums,
    ) = refs[:10]
    ins = [up_grad, down_grad, joint_grad, place_ref, out_w_ref, small_grad]
    work = Scatter(bit_count, pieces, ins, owned, refs[10:])
    count, width = stream.shape
    hidden_width = hidden_ref.shape[1]
    chunk = width
    stages = {}

    def begin(name):
        work.start(groups[name])
        stages[name] = 0

    def tick(*names):
        for name in names:
            stage = stages[name]
            if stage == 0:
                work.add_pair(groups[name])
            elif stage <= bit_count:
                work.advance(stage - 1, groups[name])
            stages[name] = stage + 1

    greet(bit_count)
    for part, source in enumerate((gq_ref, gk_ref, gv_ref)):
        store_blocks(
            joint_grad,
            product_left(attend_ref[...], source[...]),
            slice(part * width, (part + 1) * width),
        )
    begin("joint")
    sums[...] = jnp.zeros_like(sums)
    gain_first, gain_attend = gains_ref[0:1, :], gains_ref[1:2, :]

    def attend_back(rows):
        unit, spread = standardize(after_ref[rows, :])
        grad = product_right(gq_ref[rows, :], joint_ref[:, :width])
        grad = grad + product_right(gk_ref[rows, :], joint_ref[:, width : 2 * width])
        grad = grad + product_right(gv_ref[rows, :], joint_ref[:, 2 * width :])
        sums[1:2, :] = sums[1:2, :] + jnp.sum(grad * unit, axis=0, keepdims=True)
        total = stream_ref[rows, :] + standardize_back(grad * gain_attend, unit, spread)
        stream[rows, :] = total
        low[rows, :] = (0.5 * total).astype(BF16)

    loop_rows(count, attend_back)
    tick("joint")
    for at in range(0, hidden_width, chunk):
        hidden = hidden_ref[:, at : at + chunk].astype(F32)
        active[...] = (hidden * jax.nn.sigmoid(hidden)).astype(BF16)
        piece = product_left(active[...], low[...])
        lead = down_grad.shape[:-2]
        blocks = chunk * (1 << bit_count) // hidden_width
        first = at * (1 << bit_count) // hidden_width
        depth = hidden_width >> (bit_count + 1)
        for n in range(blocks):
            owner = first + n
            index = tuple((owner >> bit) & 1 for bit in range(bit_count - 1, -1, -1))
            for half in range(2):
                start = (2 * n + half) * depth
                down_grad[index + (half,)] = piece[start : start + depth].astype(BF16)
    begin("down")
    tick("joint")
    for number, at in enumerate(range(0, hidden_width, chunk)):
        cols = slice(at, at + chunk)

        def hidden_back(rows):
            hidden = hidden_ref[rows, cols].astype(F32)
            grad = product_right(low[rows, :], down_ref[cols, :])
            grad_low = (grad * swish_slope(hidden)).astype(BF16)
            active[rows, :] = grad_low
            piece = product_right(grad_low, up_ref[:, cols])
            if number == 0:
                normed_grad[rows, :] = piece
            else:
                normed_grad[rows, :] = normed_grad[rows, :] + piece

        loop_rows(count, hidden_back)
        store_blocks(up_grad, product_left(first_ref[...], active[...]), cols)
        if number < 2:
            tick("joint", "down")
        elif number == 2:
            tick("down")
    begin("up")
    tick("joint", "down")

    def first_back(rows):
        unit, spread = standardize(features_ref[rows, :].astype(F32))
        grad = normed_grad[rows, :]
        sums[0:1, :] = sums[0:1, :] + jnp.sum(grad * unit, axis=0, keepdims=True)
        total = stream[rows, :] + standardize_back(grad * gain_first, unit, spread)
        grad_ref[rows, :] = total.astype(BF16)

    loop_rows(count, first_back)
    small_ref[...] = jnp.zeros_like(small_ref)
    small_ref[0:2, :] = sums[0:2, :]
    small_ref[2:4, :] = bias_ref[0:2, :]
    small_ref[4:5, :] = conv_gain_ref[...]
    small_ref[7:8, :] = second_gain_ref[...]
    small_ref[8:9, :] = final_gain_ref[...]
    small_ref[9:41, :] = jnp.sum(taps_ref[...], axis=0)
    small = small_ref[...]
    store_blocks(small_grad, small.T, slice(0, small.shape[0]))
    begin("small")
    for _ in range(bit_count + 1):
        tick("joint", "down", "up", "small")
    work.finish()


TAIL_PLAN = [
    ("joint", (3, 1, 0, 16)),
    ("joint", (4, 2, 0, 16)),
    ("joint", (2, 0, 0, 7)),
    ("joint", (2, 1, 7, 11)),
    ("joint", (2, 2, 11, 16)),
    ("down", (1, 0, 0, 4)),
    ("down", (1, 1, 4, 8)),
    ("down", (1, 2, 8, 16)),
    ("up", (0, 0, 0, 5)),
    ("up", (0, 1, 5, 10)),
    ("up", (0, 2, 10, 16)),
    ("small", (5, 0, 0, 16)),
]


def tail(
    attend_grads, normed_attend, after_first, grad_stream, normed_first, features, hidden, gains,
    joint_full, up_full, down_full, rows, taps, grad_place, grad_out, collective_id,
):
    shards = lax.axis_size("shard")
    bit_count = (shards - 1).bit_length()
    lead = (2,) * bit_count
    count, width = after_first.shape
    hidden_width = up_full.shape[1]

    def blocks(rows, cols):
        return lead + (2, rows // (2 * shards), cols)

    given = [array.reshape(blocks(*array.shape)) for array in (grad_place, grad_out)]
    shapes = [
        blocks(width, hidden_width),
        blocks(hidden_width, width),
        blocks(width, 3 * width),
        given[0].shape,
        given[1].shape,
        blocks(width, 128),
    ]
    pieces, groups = [], {}
    for name, wanted in TAIL_PLAN:
        for piece in plan_pieces([shape[-2:] for shape in shapes], [wanted]):
            groups.setdefault(name, []).append(len(pieces))
            pieces.append(piece)
    vmem = pl.BlockSpec(memory_space=pltpu.VMEM)
    outs = pl.pallas_call(
        functools.partial(tail_kernel, bit_count, pieces, groups, shapes),
        in_specs=[vmem] * 18 + [pl.BlockSpec(memory_space=pl.ANY)] * 2,
        out_specs=[vmem] * 7,
        out_shape=[jax.ShapeDtypeStruct((count, width), BF16)]
        + [jax.ShapeDtypeStruct((2,) + shape[-2:], BF16) for shape in shapes],
        scratch_shapes=[
            pltpu.VMEM(shapes[2], BF16),
            pltpu.VMEM(shapes[1], BF16),
            pltpu.VMEM(shapes[0], BF16),
            pltpu.VMEM(shapes[5], BF16),
            pltpu.VMEM((count, width), F32),
            pltpu.VMEM((count, width), BF16),
            pltpu.VMEM((128, width), F32),
            pltpu.VMEM((count, width), BF16),
            pltpu.VMEM((count, width), F32),
            pltpu.VMEM((8, width), F32),
        ]
        + Scatter.scratch(bit_count, pieces),
        compiler_params=pltpu.CompilerParams(
            collective_id=collective_id,
            has_side_effects=True,
            vmem_limit_bytes=60 * 1024 * 1024,
        ),
        cost_estimate=pl.CostEstimate(
            flops=13000000000, bytes_accessed=40000000, transcendentals=5000000
        ),
    )(
        *attend_grads, normed_attend, after_first, grad_stream, normed_first, features, hidden,
        gains, joint_full, up_full, down_full, *rows, taps, *given,
    )
    return outs[0], outs[1:]


def widen_kernel(count, row_total, tap_total, *refs):
    ins, extra_ref, grad_ref = refs[:count], refs[count], refs[count + 1]
    outs, grad_out_ref = refs[count + 2 : -1], refs[-1]
    grad_out_ref[...] = grad_ref[...]
    for source, target in zip(ins[:-1], outs[:-2]):
        target[...] = source[...].astype(F32)
    small = ins[-1][...].astype(F32).T
    outs[-2][...] = small[:row_total] + extra_ref[...]
    outs[-1][...] = small[row_total : row_total + tap_total]


def widen(sums, extra_rows, tap_total, grad_inputs):
    sums = [total.reshape(-1, total.shape[-1]) for total in sums]
    replicas = lax.axis_size("replica")
    if replicas > 2:
        groups = [list(range(core, replicas, 2)) for core in range(2)]
        sums = [lax.psum(total, "replica", axis_index_groups=groups) for total in sums]
    row_total, depth = extra_rows.shape
    shapes = [total.shape for total in sums[:-1]] + [(row_total, depth), (tap_total, depth)]

    def whole(shape):
        return pl.BlockSpec(shape, lambda i: (0,) * len(shape))

    args = (*sums, extra_rows, grad_inputs)
    return pl.pallas_call(
        functools.partial(widen_kernel, len(sums), row_total, tap_total),
        grid=(1,),
        in_specs=[whole(arg.shape) for arg in args],
        out_specs=[whole(shape) for shape in shapes] + [whole(grad_inputs.shape)],
        out_shape=[jax.ShapeDtypeStruct(shape, F32) for shape in shapes]
        + [jax.ShapeDtypeStruct(grad_inputs.shape, BF16)],
        compiler_params=pltpu.CompilerParams(vmem_limit_bytes=32 * 1024 * 1024),
    )(*args)


def everyone(combine, count, in_ref, out_ref, held, send_sem, recv_sem):
    shards = lax.axis_size("shard")
    me = lax.axis_index("replica") * shards + lax.axis_index("shard")
    barrier = pltpu.get_barrier_semaphore()

    def place(device):
        return (lax.div(device, shards), lax.rem(device, shards))

    def hello(far, carry):
        pl.semaphore_signal(
            barrier, inc=1, device_id=place(lax.rem(me + far, count)), device_id_type=MESH
        )
        return carry

    lax.fori_loop(1, count, hello, 0)
    pl.semaphore_wait(barrier, count - 1)

    def copy(far, slot):
        return pltpu.make_async_remote_copy(
            in_ref,
            held.at[slot],
            send_sem.at[far],
            recv_sem.at[far],
            device_id=place(lax.rem(me + far, count)),
            device_id_type=MESH,
        )

    def go(far, carry):
        copy(far, me).start()
        return carry

    def arrive(far, carry):
        copy(far, lax.rem(me + count - far, count)).wait_recv()
        return carry

    def sent(far, carry):
        copy(far, me).wait_send()
        return carry

    lax.fori_loop(1, count, go, 0)
    held[me] = in_ref[...]
    lax.fori_loop(1, count, arrive, 0)
    out_ref[...] = combine(held[...])
    lax.fori_loop(1, count, sent, 0)


def combine_sums(tiles):
    return jnp.sum(tiles, axis=0)


def combine_stats(local_count, tiles):
    half = tiles.shape[1] // 2
    means = tiles[:, :half]
    mean = jnp.sum(means, axis=0) * (1.0 / tiles.shape[0])
    apart = means - mean
    total = jnp.sum(tiles[:, half:] + local_count * (apart * apart), axis=0)
    return jnp.concatenate([mean, total * (1.0 / (local_count * tiles.shape[0]))], axis=0)


def exchange_rows(upper, lower, combine, collective_id):
    width = upper.shape[0]
    tile = jnp.concatenate([upper.reshape(-1, 128), lower.reshape(-1, 128)], axis=0)
    count = lax.axis_size("replica") * lax.axis_size("shard")
    out = pl.pallas_call(
        functools.partial(everyone, combine, count),
        in_specs=[pl.BlockSpec(memory_space=pltpu.VMEM)],
        out_specs=pl.BlockSpec(memory_space=pltpu.VMEM),
        out_shape=jax.ShapeDtypeStruct(tile.shape, F32),
        scratch_shapes=[
            pltpu.VMEM((count,) + tile.shape, F32),
            pltpu.SemaphoreType.DMA((count,)),
            pltpu.SemaphoreType.DMA((count,)),
        ],
        compiler_params=pltpu.CompilerParams(collective_id=collective_id, has_side_effects=True),
    )(tile)
    return out[: width // 128].reshape(width), out[width // 128 :].reshape(width)


def tap_windows(padded_ref, start, rows, visit):
    for shift in range(8):
        window = padded_ref[start + shift : start + shift + rows + 24, :]
        for lift in range(4):
            offset = 8 * lift + shift
            if offset > 0:
                visit(offset, window[8 * lift : 8 * lift + rows])


def fill_padded(padded_ref, values):
    length = values.shape[0]
    edge = jnp.zeros((16, values.shape[1]), F32)
    padded_ref[0:16, :] = edge
    padded_ref[16 : 16 + length, :] = values
    padded_ref[16 + length : 32 + length, :] = edge


def tile_rows(length):
    for rows in (136, 128, 120, 112, 104, 96, 88, 80, 72, 64, 56, 48, 40, 32, 24, 16, 8):
        if length % rows == 0:
            return rows
    return length


def conv_forward_kernel(linear_ref, gate_ref, taps_ref, out_ref, stats_ref, padded_ref):
    length = out_ref.shape[1]
    rows = tile_rows(length)
    fill_padded(padded_ref, linear_ref[0] * jax.nn.sigmoid(gate_ref[0]))
    for start in range(0, length, rows):
        total = [jnp.zeros((rows, out_ref.shape[2]), F32)]

        def visit(offset, window):
            total[0] = total[0] + taps_ref[offset - 1 : offset, :] * window

        tap_windows(padded_ref, start, rows, visit)
        out_ref[0, start : start + rows, :] = total[0]
    values = out_ref[0]
    mean = jnp.sum(values, axis=0, keepdims=True) * (1.0 / length)
    apart = values - mean
    squares = jnp.sum(apart * apart, axis=0, keepdims=True)
    at_row = lax.broadcasted_iota(jnp.int32, stats_ref.shape[1:], 0)
    stats_ref[0] = jnp.where(at_row == 0, mean, jnp.where(at_row == 1, squares, 0.0))


def conv_forward(mixed_clips, taps):
    clip_count, clip_length, width = mixed_clips.shape
    channels = width // 2
    blocks = channels // 128
    piece = pl.BlockSpec((1, clip_length, 128), lambda i, j: (i, 0, j))
    return pl.pallas_call(
        conv_forward_kernel,
        grid=(clip_count, blocks),
        in_specs=[
            piece,
            pl.BlockSpec((1, clip_length, 128), lambda i, j: (i, 0, blocks + j)),
            pl.BlockSpec((taps.shape[0], 128), lambda i, j: (0, j)),
        ],
        out_specs=[piece, pl.BlockSpec((1, 8, 128), lambda i, j: (i, 0, j))],
        out_shape=[
            jax.ShapeDtypeStruct((clip_count, clip_length, channels), F32),
            jax.ShapeDtypeStruct((clip_count, 8, channels), F32),
        ],
        scratch_shapes=[pltpu.VMEM((clip_length + 32, 128), F32)],
        compiler_params=pltpu.CompilerParams(vmem_limit_bytes=32 * 1024 * 1024),
        cost_estimate=pl.CostEstimate(
            flops=80000000, bytes_accessed=8000000, transcendentals=600000
        ),
    )(mixed_clips, mixed_clips, taps)


def conv_backward_kernel(
    linear_ref, gate_ref, grad_ref, conv_ref, rows_ref, taps_ref,
    out_ref, grad_taps_ref, padded_ref, grad_padded_ref, tap_sums_ref,
):
    length = grad_ref.shape[1]
    rows = tile_rows(length)
    block = pl.program_id(1)
    channels = out_ref.shape[2] // 2
    mean, inverse, scale = rows_ref[0:1, :], rows_ref[1:2, :], rows_ref[2:3, :]
    shift_mean, gain_mean = rows_ref[3:4, :], rows_ref[4:5, :]
    unit = (conv_ref[0] - mean) * inverse
    grad_conv = scale * (grad_ref[0] - shift_mean - unit * gain_mean)
    fill_padded(grad_padded_ref, grad_conv)
    fill_padded(padded_ref, linear_ref[0] * jax.nn.sigmoid(gate_ref[0]))
    tap_sums_ref[...] = jnp.zeros_like(tap_sums_ref)
    first = pl.multiple_of(block * 128, 128)
    second = pl.multiple_of(channels + block * 128, 128)
    for start in range(0, length, rows):
        grad_rows = grad_padded_ref[16 + start : 16 + start + rows, :]

        def visit(offset, window):
            product_rows = (grad_rows * window).reshape(rows // 8, 8, window.shape[1])
            tap_sums_ref[offset - 1] = tap_sums_ref[offset - 1] + jnp.sum(product_rows, axis=0)

        tap_windows(padded_ref, start, rows, visit)
        total = [jnp.zeros((rows, 128), F32)]

        def visit_back(offset, window):
            total[0] = total[0] + taps_ref[31 - offset : 32 - offset, :] * window

        tap_windows(grad_padded_ref, start, rows, visit_back)
        grad_gated = total[0]
        gate = jax.nn.sigmoid(gate_ref[0, start : start + rows, :])
        grad_linear = grad_gated * gate
        linear = linear_ref[0, start : start + rows, :]
        out_ref[0, start : start + rows, pl.ds(first, 128)] = grad_linear.astype(BF16)
        out_ref[0, start : start + rows, pl.ds(second, 128)] = (
            grad_linear * linear * (1.0 - gate)
        ).astype(BF16)
    grad_taps_ref[0] = jnp.sum(tap_sums_ref[...], axis=1)


def conv_backward(mixed_clips, grad_clips, conv_clips, rows, taps):
    clip_count, clip_length, width = mixed_clips.shape
    channels = width // 2
    blocks = channels // 128
    piece = pl.BlockSpec((1, clip_length, 128), lambda i, j: (i, 0, j))
    return pl.pallas_call(
        conv_backward_kernel,
        grid=(clip_count, blocks),
        in_specs=[
            piece,
            pl.BlockSpec((1, clip_length, 128), lambda i, j: (i, 0, blocks + j)),
            piece,
            piece,
            pl.BlockSpec((8, 128), lambda i, j: (0, j)),
            pl.BlockSpec((taps.shape[0], 128), lambda i, j: (0, j)),
        ],
        out_specs=[
            pl.BlockSpec((1, clip_length, width), lambda i, j: (i, 0, 0)),
            pl.BlockSpec((1, 32, 128), lambda i, j: (i, 0, j)),
        ],
        out_shape=[
            jax.ShapeDtypeStruct((clip_count, clip_length, width), BF16),
            jax.ShapeDtypeStruct((clip_count, 32, channels), F32),
        ],
        scratch_shapes=[
            pltpu.VMEM((clip_length + 32, 128), F32),
            pltpu.VMEM((clip_length + 32, 128), F32),
            pltpu.VMEM((32, 8, 128), F32),
        ],
        compiler_params=pltpu.CompilerParams(vmem_limit_bytes=32 * 1024 * 1024),
        cost_estimate=pl.CostEstimate(
            flops=160000000, bytes_accessed=14000000, transcendentals=1200000
        ),
    )(mixed_clips, mixed_clips, grad_clips, conv_clips, rows, taps)


EARLY_PLAN = [
    (0, 0, 0, 10),
    (0, 1, 10, 16),
    (1, 1, 0, 4),
    (1, 2, 4, 16),
    (2, 0, 0, 16),
    (3, 0, 0, 6),
    (3, 1, 6, 16),
    (4, 2, 0, 16),
]
LATE_PLAN = [(0, 1, 0, 16), (1, 1, 0, 16), (2, 1, 0, 16), (3, 0, 0, 16), (4, 2, 0, 16)]
LATE_BACK_PLAN = [(0, 1, 0, 16), (1, 1, 0, 16), (2, 0, 0, 16), (3, 2, 0, 16)]


def body(
    features,
    frame_times,
    cotangent,
    vectors,
    first_up,
    first_down,
    query_key_value,
    place_weight,
    out_weight,
    point_glu,
    depth_taps,
    point_out,
    second_up,
    second_down,
):
    clip_count, clip_length, model_width = features.shape
    row_count = clip_count * clip_length
    token_count = row_count * lax.axis_size("replica") * lax.axis_size("shard")

    shards = lax.axis_size("shard")
    depth = first_up.shape[0]
    hidden_width = first_up.shape[1]
    row_total = vectors.shape[0]
    tap_total = depth_taps.shape[0]

    small_shard = pack_small([vectors.T, depth_taps.T])
    up_one, down_one, small_full, joint_full, place_full = gather_arrays(
        [first_up, first_down, small_shard, query_key_value, place_weight], EARLY_PLAN, 1
    )
    small = small_full.T
    first_full = (small[:row_total], up_one, down_one)
    gains = first_full[0].astype(jnp.float32)
    inputs = features.reshape(row_count, model_width).astype(jnp.float32)
    first_out, first_kept = feed_forward(inputs, gains[0], first_full[1], first_full[2])
    after_first = inputs + 0.5 * first_out
    normed_attend = normalize(after_first, gains[1]).astype(jnp.bfloat16)
    joint_rows = product(normed_attend, joint_full)
    joint_clips = joint_rows.reshape(clip_count, clip_length, 3 * model_width)
    attend_parts = attention_inputs(joint_clips, gains, model_width)
    sine_flat, cos_flat = wave_table(frame_times.reshape(row_count), model_width)
    sine_rows = sine_flat.reshape(clip_count, clip_length, -1)
    cosines = cos_flat.reshape(clip_count, clip_length, -1)
    context_clips, probs, late_full = attention_forward(
        attend_parts,
        place_full,
        sine_rows,
        cosines,
        [out_weight, point_glu, point_out, second_up, second_down],
        LATE_PLAN,
        2,
    )
    out_full = late_full[0]
    conv_full = (late_full[1], small[row_total : row_total + tap_total], late_full[2])
    second_full = late_full[3:]
    context_low = context_clips.reshape(row_count, model_width)
    after_attend = after_first + product(context_low, out_full)
    normed_conv = normalize(after_attend, gains[4]).astype(jnp.bfloat16)
    mixed_rows = product(normed_conv, conv_full[0]).reshape(
        clip_count, clip_length, 2 * model_width
    )
    taps = jnp.pad(conv_full[1].astype(jnp.float32), ((0, 32 - tap_total), (0, 0)))
    conv_clips, clip_stats = conv_forward(mixed_rows, taps)
    conv_flat = conv_clips.reshape(row_count, model_width)
    clip_means = clip_stats[:, 0]
    local_mean = jnp.mean(clip_means, axis=0)
    apart = clip_means - local_mean
    local_squares = jnp.sum(clip_stats[:, 1] + clip_length * (apart * apart), axis=0)
    channel_mean, variance = exchange_rows(
        local_mean,
        local_squares,
        functools.partial(combine_stats, row_count),
        3,
    )
    centered = conv_flat - channel_mean
    inverse = lax.rsqrt(variance + epsilon)
    unit_values = centered * inverse
    shaped = unit_values * gains[5] + gains[6]
    active_conv = swish_act(shaped).astype(jnp.bfloat16)
    after_conv = after_attend + product(active_conv, conv_full[2])
    second_out, second_kept = feed_forward(after_conv, gains[7], second_full[0], second_full[1])
    after_second = after_conv + 0.5 * second_out
    output = normalize(after_second, gains[8])
    grad_last, grad_final_gain = normalize_back(
        after_second, gains[8], cotangent.reshape(row_count, model_width).astype(jnp.float32)
    )
    second_back = second_full
    grad_conv_out, grad_second_gain, grad_second_up, grad_second_down = feed_back(
        grad_last, after_conv, gains[7], second_back[0], second_back[1], second_kept
    )
    conv_back = conv_full
    grad_low = grad_conv_out.astype(jnp.bfloat16)
    grad_point_out = product_left(active_conv, grad_low)
    grad_shaped = product_right(grad_low, conv_back[2]) * swish_slope(shaped)
    shift_total, gain_total = exchange_rows(
        jnp.sum(grad_shaped, axis=0), jnp.sum(grad_shaped * unit_values, axis=0), combine_sums, 4
    )
    zero_row = jnp.zeros_like(inverse)
    batch_rows = jnp.stack(
        [
            channel_mean,
            inverse,
            gains[5] * inverse,
            shift_total / token_count,
            gain_total / token_count,
            zero_row,
            zero_row,
            zero_row,
        ]
    )
    grad_mixed_clips, clip_taps = conv_backward(
        mixed_rows,
        grad_shaped.reshape(clip_count, clip_length, model_width),
        conv_clips,
        batch_rows,
        taps,
    )
    grad_mixed_low = grad_mixed_clips.reshape(row_count, 2 * model_width)
    grad_point_glu = product_left(normed_conv, grad_mixed_low)
    grad_extra, grad_conv_gain = normalize_back(
        after_attend, gains[4], product_right(grad_mixed_low, conv_back[0])
    )
    grad_attend_out = grad_conv_out + grad_extra
    grad_low = grad_attend_out.astype(jnp.bfloat16)
    grad_out_weight = product_left(context_low, grad_low)
    grad_context = (
        product_right(grad_low, out_full)
        .astype(jnp.bfloat16)
        .reshape(clip_count, clip_length, model_width)
    )
    attend_grads, late_sums = attention_backward(
        attend_parts,
        grad_context,
        place_full,
        sine_rows,
        cosines,
        probs,
        [
            array.astype(BF16)
            for array in (grad_point_glu, grad_point_out, grad_second_up, grad_second_down)
        ],
        LATE_BACK_PLAN,
        5,
    )
    grad_query, grad_key, grad_value, grad_bias, grad_place = attend_grads
    attend_low = [
        array.reshape(row_count, model_width) for array in (grad_query, grad_key, grad_value)
    ]
    grad_inputs, early_sums = tail(
        attend_low,
        normed_attend,
        after_first,
        grad_attend_out,
        first_kept[0],
        features.reshape(row_count, model_width),
        first_kept[1],
        gains,
        joint_full,
        first_full[1],
        first_full[2],
        [grad_bias, grad_conv_gain[None], grad_second_gain[None], grad_final_gain[None]],
        clip_taps,
        grad_place.astype(BF16),
        grad_out_weight.astype(BF16),
        6,
    )
    shard_cols = vectors.shape[1]
    first_col = lax.axis_index("shard") * shard_cols
    batch_grads = jnp.concatenate(
        [
            jnp.zeros((5, model_width), F32),
            gain_total[None],
            shift_total[None],
            jnp.zeros((row_total - 7, model_width), F32),
        ]
    )
    batch_grads = lax.dynamic_slice_in_dim(batch_grads, first_col, shard_cols, axis=1)
    summed = widen(
        [*early_sums[:5], *late_sums, early_sums[5]], batch_grads, tap_total, grad_inputs
    )
    return (
        output.astype(jnp.bfloat16).reshape(clip_count, clip_length, model_width),
        summed[11].reshape(clip_count, clip_length, model_width),
        summed[9],
        *summed[:6],
        summed[10],
        *summed[6:9],
    )


def solution(mesh):
    return jax.shard_map(
        body,
        mesh=mesh,
        in_specs=(
            P(("replica", "shard"), None, None),
            P(("replica", "shard"), None),
            P(("replica", "shard"), None, None),
            P(None, "shard"),
            P("shard", None),
            P("shard", None),
            P("shard", None),
            P("shard", None),
            P("shard", None),
            P("shard", None),
            P(None, "shard"),
            P("shard", None),
            P("shard", None),
            P("shard", None),
        ),
        out_specs=(
            P(("replica", "shard"), None, None),
            P(("replica", "shard"), None, None),
            P(None, "shard"),
            P("shard", None),
            P("shard", None),
            P("shard", None),
            P("shard", None),
            P("shard", None),
            P("shard", None),
            P(None, "shard"),
            P("shard", None),
            P("shard", None),
            P("shard", None),
        ),
        check_vma=False,
    )
```

```python
import functools
import math

import jax
import jax.numpy as jnp
from jax import lax
from jax.experimental import pallas as pl
from jax.experimental.pallas import tpu as pltpu
from jax.sharding import PartitionSpec as P

HEADS = 8
HEAD_DIM = 64


epsilon = 1e-05


def normalize(values, gain_row):
    center = values - jnp.mean(values, axis=-1, keepdims=True)
    spread = jnp.mean(center * center, axis=-1, keepdims=True)
    return center * lax.rsqrt(spread + epsilon) * gain_row


def normalize_back(values, gain_row, grad_normed):
    pull = jax.vjp(normalize, values, gain_row)[1]
    return pull(grad_normed)


def swish_act(values):
    return values * jax.nn.sigmoid(values)


def swish_slope(values):
    sigmoid = jax.nn.sigmoid(values)
    return sigmoid * (1.0 + values * (1.0 - sigmoid))


def wave_table(frame_pos, model_width):
    half_width = model_width // 2
    frequency = jnp.exp(
        jnp.arange(half_width, dtype=jnp.float32) * (-math.log(10000.0) / half_width)
    )
    angles = frame_pos.astype(jnp.float32)[:, None] * frequency[None, :]
    return (jnp.sin(angles), jnp.cos(angles))


def product(left_side, right_side):
    return jnp.dot(left_side, right_side, preferred_element_type=jnp.float32)


def product_left(left_side, right_side):
    return lax.dot_general(
        left_side, right_side, (((0,), (0,)), ((), ())), preferred_element_type=jnp.float32
    )


def product_right(left_side, right_side):
    return lax.dot_general(
        left_side, right_side, (((1,), (1,)), ((), ())), preferred_element_type=jnp.float32
    )


def feed_forward(inputs, gain_row, up_full, down_full):
    normed_low = normalize(inputs, gain_row).astype(jnp.bfloat16)
    hidden = product(normed_low, up_full)
    active_low = swish_act(hidden).astype(jnp.bfloat16)
    return (product(active_low, down_full), (normed_low, hidden.astype(BF16), active_low))


def head_probs(query_u, query_v, key_low, place_head, sine_rows, cosines, basis_low):
    raw_place = product_right(query_v, place_head)
    half_width = raw_place.shape[-1] // 2
    part_sin = raw_place[:, :half_width]
    part_cos = raw_place[:, half_width:]
    coeff_low = jnp.concatenate(
        [part_sin * sine_rows + part_cos * cosines, part_cos * sine_rows - part_sin * cosines],
        axis=-1,
    ).astype(jnp.bfloat16)
    scores = product_right(query_u, key_low) + product_right(coeff_low, basis_low)
    scores = scores * (1.0 / math.sqrt(HEAD_DIM))
    row_peak = jnp.max(scores, axis=-1, keepdims=True)
    raised = jnp.exp(scores - row_peak)
    return raised * (1.0 / jnp.sum(raised, axis=-1, keepdims=True))


def forward_kernel(bit_count, pieces, array_count, *refs):
    qu_ref, qv_ref, key_ref, value_ref, place_ref, sine_ref, cos_ref = refs[:7]
    shards = refs[7 : 7 + array_count]
    out_ref, probs_ref = refs[7 + array_count : 9 + array_count]
    fulls = refs[9 + array_count : 9 + 2 * array_count]
    gather = Gather(bit_count, pieces, shards, fulls, refs[9 + 2 * array_count :])
    step = pl.program_id(0) * pl.num_programs(1) + pl.program_id(1)
    steps = pl.num_programs(0) * pl.num_programs(1)

    @pl.when(step == 0)
    def begin():
        greet(bit_count)
        gather.start()

    sine_rows = sine_ref[0]
    cosines = cos_ref[0]
    basis_low = jnp.concatenate([cosines, sine_rows], axis=-1).astype(jnp.bfloat16)
    merged = []
    for head, at in enumerate(range(0, out_ref.shape[-1], HEAD_DIM)):
        cols = slice(at, at + HEAD_DIM)
        probs = head_probs(
            qu_ref[0][:, cols],
            qv_ref[0][:, cols],
            key_ref[0][:, cols],
            place_ref[:, cols],
            sine_rows,
            cosines,
            basis_low,
        ).astype(jnp.bfloat16)
        probs_ref[0, head] = probs
        merged.append(product(probs, value_ref[0][:, cols]))
    out_ref[0] = jnp.concatenate(merged, axis=-1).astype(jnp.bfloat16)

    for phase in range(bit_count):
        when = (2, 3, 5)[phase] if phase < min(3, bit_count - 1) else steps - 1

        @pl.when(step == when)
        def go(phase=phase):
            gather.advance(phase)

    @pl.when(step == steps - 1)
    def end():
        gather.finish()


def backward_kernel(bit_count, pieces, array_count, *refs):
    qu_ref, qv_ref, key_ref, value_ref, grad_ref, place_ref, sine_ref, cos_ref, probs_ref = refs[:9]
    partials = refs[9 : 9 + array_count]
    refs = refs[9 + array_count :]
    grad_query_ref, grad_key_ref, grad_value_ref, grad_bias_ref, grad_place_ref = refs[:5]
    owned = refs[5 : 5 + array_count]
    scatter = Scatter(bit_count, pieces, partials, owned, refs[5 + array_count :])
    step = pl.program_id(0) * pl.num_programs(1) + pl.program_id(1)
    steps = pl.num_programs(0) * pl.num_programs(1)

    @pl.when(step == 0)
    def begin():
        greet(bit_count)
        scatter.start()

    sine_rows = sine_ref[0]
    cosines = cos_ref[0]
    basis_low = jnp.concatenate([cosines, sine_rows], axis=-1).astype(jnp.bfloat16)
    half_width = sine_rows.shape[-1]
    queries, keys, values, sums_u, sums_v, places = ([], [], [], [], [], [])
    for head, at in enumerate(range(0, grad_query_ref.shape[-1], HEAD_DIM)):
        cols = slice(at, at + HEAD_DIM)
        query_u = qu_ref[0][:, cols]
        query_v = qv_ref[0][:, cols]
        key_low = key_ref[0][:, cols]
        place_head = place_ref[:, cols]
        grad_head = grad_ref[0][:, cols]
        probs_low = probs_ref[0, head]
        values.append(product_left(probs_low, grad_head))
        probs = probs_low.astype(jnp.float32)
        grad_probs = product_right(grad_head, value_ref[0][:, cols])
        inner_sum = jnp.sum(grad_probs * probs, axis=-1, keepdims=True)
        grad_scores = (probs * (grad_probs - inner_sum) * (1.0 / math.sqrt(HEAD_DIM))).astype(
            jnp.bfloat16
        )
        grad_u = product(grad_scores, key_low)
        keys.append(product_left(grad_scores, query_u))
        grad_coeff = product(grad_scores, basis_low)
        grad_a = grad_coeff[:, :half_width]
        grad_b = grad_coeff[:, half_width:]
        grad_raw = jnp.concatenate(
            [grad_a * sine_rows - grad_b * cosines, grad_a * cosines + grad_b * sine_rows],
            axis=-1,
        ).astype(jnp.bfloat16)
        grad_v = product(grad_raw, place_head)
        places.append(product_left(grad_raw, query_v))
        queries.append(grad_u + grad_v)
        sums_u.append(jnp.sum(grad_u, axis=0, keepdims=True))
        sums_v.append(jnp.sum(grad_v, axis=0, keepdims=True))
    grad_query_ref[0] = jnp.concatenate(queries, axis=-1).astype(jnp.bfloat16)
    grad_key_ref[0] = jnp.concatenate(keys, axis=-1).astype(jnp.bfloat16)
    grad_value_ref[0] = jnp.concatenate(values, axis=-1).astype(jnp.bfloat16)
    row_u = jnp.concatenate(sums_u, axis=-1)
    row_v = jnp.concatenate(sums_v, axis=-1)
    at_row = lax.broadcasted_iota(jnp.int32, grad_bias_ref.shape, 0)
    bias = jnp.where(at_row == 0, row_u, jnp.where(at_row == 1, row_v, 0.0))
    place_sum = jnp.concatenate(places, axis=-1)

    @pl.when(pl.program_id(1) == 0)
    def first_clip():
        grad_bias_ref[...] = bias
        grad_place_ref[...] = place_sum

    @pl.when(pl.program_id(1) > 0)
    def later_clip():
        grad_bias_ref[...] = grad_bias_ref[...] + bias
        grad_place_ref[...] = grad_place_ref[...] + place_sum

    @pl.when(step == 0)
    def pair():
        scatter.add_pair()

    for phase in range(bit_count):
        when = (2, 4, 5)[phase] if phase < min(3, bit_count - 1) else steps - 1

        @pl.when(step == when)
        def go(phase=phase):
            scatter.advance(phase)

    @pl.when(step == steps - 1)
    def end():
        scatter.finish()


def attention_specs(clip_length, model_width):
    rows = pl.BlockSpec((1, clip_length, 128), lambda i, j: (i, 0, j))
    place = pl.BlockSpec((model_width, 128), lambda i, j: (0, j))
    wave = pl.BlockSpec((1, clip_length, model_width // 2), lambda i, j: (i, 0, 0))
    return (rows, place, wave)


def attention_inputs(joint_clips, gains, model_width):
    query = joint_clips[..., :model_width]
    return (
        (query + gains[2]).astype(jnp.bfloat16),
        (query + gains[3]).astype(jnp.bfloat16),
        joint_clips[..., model_width : 2 * model_width].astype(jnp.bfloat16),
        joint_clips[..., 2 * model_width :].astype(jnp.bfloat16),
    )


def attention_forward(parts, place_full, sine_rows, cosines, shards, wanted, collective_id):
    clip_count, clip_length, model_width = parts[0].shape
    rows, place, wave = attention_specs(clip_length, model_width)
    bit_count = (lax.axis_size("shard") - 1).bit_length()
    ins = [halves(array) for array in shards]
    pieces = plan_pieces([array.shape[1:] for array in ins], wanted)
    lead = (2,) * bit_count
    whole = pl.BlockSpec(memory_space=pl.ANY)
    heads = model_width // HEAD_DIM
    outs = pl.pallas_call(
        functools.partial(forward_kernel, bit_count, pieces, len(ins)),
        grid=(clip_count, model_width // 128),
        in_specs=[rows, rows, rows, rows, place, wave, wave] + [whole] * len(ins),
        out_specs=[
            rows,
            pl.BlockSpec((1, 2, clip_length, clip_length), lambda i, j: (i, j, 0, 0)),
        ]
        + [whole] * len(ins),
        out_shape=[
            jax.ShapeDtypeStruct(parts[0].shape, jnp.bfloat16),
            jax.ShapeDtypeStruct((clip_count, heads, clip_length, clip_length), jnp.bfloat16),
        ]
        + [jax.ShapeDtypeStruct(lead + array.shape, BF16) for array in ins],
        scratch_shapes=Gather.scratch(bit_count, pieces, len(ins)),
        compiler_params=pltpu.CompilerParams(
            vmem_limit_bytes=48 * 1024 * 1024, collective_id=collective_id, has_side_effects=True
        ),
        cost_estimate=pl.CostEstimate(
            flops=16000000000, bytes_accessed=12000000, transcendentals=5000000
        ),
    )(*parts, place_full, sine_rows, cosines, *ins)
    fulls = [out.reshape(-1, array.shape[1]) for out, array in zip(outs[2:], shards)]
    return outs[0], outs[1], fulls


def attention_backward(
    parts, grad_context, place_full, sine_rows, cosines, probs, partials, wanted, collective_id
):
    clip_count, clip_length, model_width = parts[0].shape
    rows = pl.BlockSpec((1, clip_length, 128), lambda j, i: (i, 0, j))
    place = pl.BlockSpec((model_width, 128), lambda j, i: (0, j))
    wave = pl.BlockSpec((1, clip_length, model_width // 2), lambda j, i: (i, 0, 0))
    like = jax.ShapeDtypeStruct(parts[0].shape, jnp.bfloat16)
    bit_count, ins, pieces, shapes = scatter_plan(partials, wanted)
    outs = pl.pallas_call(
        functools.partial(backward_kernel, bit_count, pieces, len(ins)),
        grid=(model_width // 128, clip_count),
        in_specs=[
            rows,
            rows,
            rows,
            rows,
            rows,
            place,
            wave,
            wave,
            pl.BlockSpec((1, 2, clip_length, clip_length), lambda j, i: (i, j, 0, 0)),
        ]
        + [pl.BlockSpec(memory_space=pl.ANY)] * len(ins),
        out_specs=[
            rows,
            rows,
            rows,
            pl.BlockSpec((8, 128), lambda j, i: (0, j)),
            pl.BlockSpec((model_width, 128), lambda j, i: (0, j)),
        ]
        + [pl.BlockSpec(shape.shape, lambda i, j: (0, 0, 0)) for shape in shapes],
        out_shape=[
            like,
            like,
            like,
            jax.ShapeDtypeStruct((8, model_width), jnp.float32),
            jax.ShapeDtypeStruct((model_width, model_width), jnp.float32),
        ]
        + shapes,
        scratch_shapes=Scatter.scratch(bit_count, pieces),
        compiler_params=pltpu.CompilerParams(
            vmem_limit_bytes=56 * 1024 * 1024, collective_id=collective_id, has_side_effects=True
        ),
        cost_estimate=pl.CostEstimate(
            flops=80000000000, bytes_accessed=20000000, transcendentals=5000000
        ),
    )(*parts, grad_context, place_full, sine_rows, cosines, probs, *ins)
    return outs[:5], outs[5:]


def pack_small(columns):
    joined = jnp.concatenate(columns, axis=1)
    return jnp.pad(joined, ((0, 0), (0, -joined.shape[1] % 128)))


MESH = pl.DeviceIdType.MESH
BF16 = jnp.bfloat16
F32 = jnp.float32


def bit_of(index, bit):
    return lax.rem(lax.div(index, 1 << bit), 2)


def flip_bit(index, bit):
    return index + (1 - 2 * bit_of(index, bit)) * (1 << bit)


def link_orders(bit_count):
    far = list(range(bit_count - 1, 2, -1))
    if bit_count < 3:
        return [list(range(bit_count))] * 3
    return [far + [1, 2, 0], far + [2, 0, 1], far + [0, 1, 2]]


def greet(bit_count):
    shard = lax.axis_index("shard")
    replica = lax.axis_index("replica")
    barrier = pltpu.get_barrier_semaphore()
    for bit in range(bit_count):
        pl.semaphore_signal(
            barrier, inc=1, device_id={"shard": flip_bit(shard, bit)}, device_id_type=MESH
        )
    pl.semaphore_signal(
        barrier, inc=1, device_id={"replica": flip_bit(replica, 0)}, device_id_type=MESH
    )
    pl.semaphore_wait(barrier, bit_count + 1)


def block_index(bit_count, free_bits, values):
    return tuple(
        slice(None) if bit in free_bits else values[bit] for bit in range(bit_count - 1, -1, -1)
    )


class Piece:
    def __init__(self, array, color, rows, cols):
        self.array, self.color, self.rows, self.cols = array, color, rows, cols

    @property
    def tail(self):
        return (pl.ds(*self.rows), pl.ds(*self.cols))

    @property
    def shape(self):
        return (self.rows[1], self.cols[1])


def plan_pieces(shapes, wanted):
    pieces = []
    for array, color, low, high in wanted:
        rows, cols = shapes[array]
        if cols >= 2048 or cols % (16 * 128) == 0 or rows < 32:
            unit = cols // 128
            a, b = unit * low // 16 * 128, unit * high // 16 * 128
            wide = ((0, rows), (a, b - a))
        else:
            unit = rows // 16
            a, b = unit * low // 16 * 16, unit * high // 16 * 16
            wide = ((a, b - a), (0, cols))
        if b > a:
            pieces.append(Piece(array, color, *wide))
    return pieces


class Gather:
    def __init__(self, bit_count, pieces, ins, outs, sems):
        self.bits, self.pieces, self.ins, self.outs = bit_count, pieces, ins, outs
        self.send, self.recv, self.core_send, self.core_recv, self.local = sems
        shard = lax.axis_index("shard")
        replica = lax.axis_index("replica")
        self.shard, self.half = shard, lax.rem(replica, 2)
        self.core = {"replica": flip_bit(replica, 0)}
        self.own = [bit_of(shard, bit) for bit in range(bit_count)]
        self.orders = link_orders(bit_count)

    @staticmethod
    def scratch(bit_count, pieces, array_count):
        grid = (len(pieces), bit_count)
        return [pltpu.SemaphoreType.DMA(grid)] * 4 + [pltpu.SemaphoreType.DMA((array_count,))]

    def local_copies(self):
        index = block_index(self.bits, (), self.own)
        return [
            pltpu.make_async_copy(self.ins[a], self.outs[a].at[index], self.local.at[a])
            for a in range(len(self.ins))
        ]

    def hop(self, p, step):
        piece = self.pieces[p]
        order = self.orders[piece.color]
        out = self.outs[piece.array]
        index = block_index(self.bits, order[:step], self.own)
        region = out.at[index + (self.half,) + piece.tail]
        if step == 0:
            source = self.ins[piece.array].at[(self.half,) + piece.tail]
        else:
            source = region
        return pltpu.make_async_remote_copy(
            source,
            region,
            self.send.at[p, step],
            self.recv.at[p, step],
            device_id={"shard": flip_bit(self.shard, order[step])},
            device_id_type=MESH,
        )

    def cross(self, p, step):
        piece = self.pieces[p]
        order = self.orders[piece.color]
        values = list(self.own)
        values[order[step]] = 1 - values[order[step]]
        index = block_index(self.bits, order[:step], values)
        region = self.outs[piece.array].at[index + (self.half,) + piece.tail]
        return pltpu.make_async_remote_copy(
            region,
            region,
            self.core_send.at[p, step],
            self.core_recv.at[p, step],
            device_id=self.core,
            device_id_type=MESH,
        )

    def start(self):
        for p in range(len(self.pieces)):
            self.hop(p, 0).start()
        for copy in self.local_copies():
            copy.start()

    def advance(self, step, which=None):
        if step == 0:
            for copy in self.local_copies():
                copy.wait()
        for p in range(len(self.pieces)):
            self.hop(p, step).wait_recv()
            if step + 1 < self.bits:
                self.hop(p, step + 1).start()
            self.cross(p, step).start()

    def finish(self):
        for p in range(len(self.pieces)):
            for step in range(self.bits):
                self.hop(p, step).wait_send()
                self.cross(p, step).wait()


class Scatter:
    def __init__(self, bit_count, pieces, ins, outs, refs):
        self.bits, self.pieces, self.ins, self.outs = bit_count, pieces, ins, outs
        count = len(pieces)
        self.first = refs[:count]
        self.total = refs[count : 2 * count]
        self.last = refs[2 * count : 3 * count]
        self.send, self.recv, self.local = refs[3 * count : 3 * count + 3]
        land = refs[3 * count + 3 :]
        self.land = [land[p * bit_count : (p + 1) * bit_count] for p in range(count)]
        shard = lax.axis_index("shard")
        replica = lax.axis_index("replica")
        self.shard, self.half = shard, lax.rem(replica, 2)
        self.core = {"replica": flip_bit(replica, 0)}
        self.own = [bit_of(shard, bit) for bit in range(bit_count)]
        self.orders = [order[::-1] for order in link_orders(bit_count)]

    @staticmethod
    def scratch(bit_count, pieces):
        lead = (2,) * bit_count
        return (
            [pltpu.VMEM(lead + piece.shape, BF16) for piece in pieces]
            + [pltpu.VMEM(lead + piece.shape, BF16) for piece in pieces]
            + [pltpu.VMEM(piece.shape, BF16) for piece in pieces]
            + [pltpu.SemaphoreType.DMA((len(pieces), bit_count + 2))] * 2
            + [pltpu.SemaphoreType.DMA((len(pieces),))]
            + [
                pltpu.VMEM((2,) * (bit_count - step - 1) + piece.shape, BF16)
                for piece in pieces
                for step in range(bit_count)
            ]
        )

    def copy(self, p, step, source, target, device):
        return pltpu.make_async_remote_copy(
            source,
            target,
            self.send.at[p, step],
            self.recv.at[p, step],
            device_id=device,
            device_id_type=MESH,
        )

    def pair(self, p):
        piece = self.pieces[p]
        lead = (slice(None),) * self.bits
        source = self.ins[piece.array].at[lead + (1 - self.half,) + piece.tail]
        return self.copy(p, 0, source, self.first[p], self.core)

    def keep(self, p):
        piece = self.pieces[p]
        lead = (slice(None),) * self.bits
        source = self.ins[piece.array].at[lead + (self.half,) + piece.tail]
        return pltpu.make_async_copy(source, self.total[p], self.local.at[p])

    def hop(self, p, step):
        order = self.orders[self.pieces[p].color]
        bit = order[step]
        values = list(self.own)
        values[bit] = 1 - values[bit]
        index = block_index(self.bits, order[step + 1 :], values)
        return self.copy(
            p,
            step + 1,
            self.total[p].at[index],
            self.land[p][step],
            {"shard": flip_bit(self.shard, bit)},
        )

    def final(self, p):
        index = block_index(self.bits, (), self.own)
        return self.copy(p, self.bits + 1, self.total[p].at[index], self.last[p], self.core)

    def start(self, which=None):
        for p in range(len(self.pieces)) if which is None else which:
            self.pair(p).start()
            self.keep(p).start()

    def add_pair(self, which=None):
        for p in range(len(self.pieces)) if which is None else which:
            self.pair(p).wait_recv()
            self.keep(p).wait()
            self.total[p][...] = self.total[p][...] + self.first[p][...]
            self.hop(p, 0).start()

    def advance(self, step, which=None):
        for p in range(len(self.pieces)) if which is None else which:
            piece = self.pieces[p]
            order = self.orders[piece.color]
            self.hop(p, step).wait_recv()
            index = block_index(self.bits, order[step + 1 :], self.own)
            self.total[p][index] = self.total[p][index] + self.land[p][step][...]
            if step + 1 < self.bits:
                self.hop(p, step + 1).start()
            else:
                self.final(p).start()

    def finish(self):
        index = block_index(self.bits, (), self.own)
        for p, piece in enumerate(self.pieces):
            self.outs[piece.array][(self.half,) + piece.tail] = self.total[p][index]
            self.final(p).wait_recv()
            self.outs[piece.array][(1 - self.half,) + piece.tail] = self.last[p][...]
        for p in range(len(self.pieces)):
            self.pair(p).wait_send()
            for step in range(self.bits):
                self.hop(p, step).wait_send()
            self.final(p).wait_send()


def gather_kernel(bit_count, pieces, array_count, *refs):
    ins, outs = refs[:array_count], refs[array_count : 2 * array_count]
    greet(bit_count)
    work = Gather(bit_count, pieces, ins, outs, refs[2 * array_count :])
    work.start()
    for step in range(bit_count):
        work.advance(step)
    work.finish()


def halves(array):
    return array.reshape(2, array.shape[0] // 2, array.shape[1])


def gather_arrays(arrays, wanted, collective_id):
    bit_count = (lax.axis_size("shard") - 1).bit_length()
    ins = [halves(array) for array in arrays]
    pieces = plan_pieces([array.shape[1:] for array in ins], wanted)
    lead = (2,) * bit_count
    outs = pl.pallas_call(
        functools.partial(gather_kernel, bit_count, pieces, len(ins)),
        in_specs=[pl.BlockSpec(memory_space=pl.ANY)] * len(ins),
        out_specs=[pl.BlockSpec(memory_space=pl.ANY)] * len(ins),
        out_shape=[jax.ShapeDtypeStruct(lead + array.shape, BF16) for array in ins],
        scratch_shapes=Gather.scratch(bit_count, pieces, len(ins)),
        compiler_params=pltpu.CompilerParams(collective_id=collective_id, has_side_effects=True),
    )(*ins)
    return [
        out.reshape(-1, array.shape[1]) for out, array in zip(outs, arrays)
    ]


def scatter_plan(arrays, wanted):
    shards = lax.axis_size("shard")
    bit_count = (shards - 1).bit_length()
    lead = (2,) * bit_count
    ins = [
        array.reshape(lead + (2, array.shape[0] // (2 * shards), array.shape[1]))
        for array in arrays
    ]
    pieces = plan_pieces([array.shape[-2:] for array in ins], wanted)
    shapes = [jax.ShapeDtypeStruct((2,) + array.shape[-2:], BF16) for array in ins]
    return bit_count, ins, pieces, shapes


def row_step(count):
    for rows in (272, 256, 128, 64, 32, 16):
        if count % rows == 0:
            return rows
    return count


def loop_rows(count, visit, between=None):
    rows = row_step(count)
    steps = count // rows

    def step(number, carry):
        visit(pl.ds(pl.multiple_of(number * rows, 16), rows))
        if between is not None:
            for at in range(steps):

                @pl.when(number == at)
                def slot():
                    between()

        return carry

    lax.fori_loop(0, steps, step, ())


def standardize(values):
    center = values - jnp.mean(values, axis=-1, keepdims=True)
    spread = lax.rsqrt(jnp.mean(center * center, axis=-1, keepdims=True) + epsilon)
    return center * spread, spread


def standardize_back(grad, unit, spread):
    inner = jnp.mean(grad * unit, axis=-1, keepdims=True)
    return spread * (grad - jnp.mean(grad, axis=-1, keepdims=True) - unit * inner)


def store_blocks(ref, value, cols):
    value = value.reshape(ref.shape[:-1] + (value.shape[-1],))
    ref[(slice(None),) * (len(ref.shape) - 1) + (cols,)] = value.astype(BF16)


def tail_kernel(bit_count, pieces, groups, shapes, *refs):
    (
        gq_ref, gk_ref, gv_ref, attend_ref, after_ref, stream_ref, first_ref, features_ref,
        hidden_ref, gains_ref, joint_ref, up_ref, down_ref, bias_ref, conv_gain_ref, middle_ref,
        taps_ref, place_ref, out_w_ref,
    ) = refs[:19]
    grad_ref = refs[19]
    owned = refs[20:26]
    refs = refs[26:]
    (
        joint_grad, down_grad, up_grad, small_grad, stream, low, small_ref, active, normed_grad, sums,
    ) = refs[:10]
    ins = [up_grad, down_grad, joint_grad, place_ref, out_w_ref, small_grad]
    work = Scatter(bit_count, pieces, ins, owned, refs[10:])
    count, width = stream.shape
    hidden_width = hidden_ref.shape[1]
    chunk = width
    stages = {}

    def begin(name):
        work.start(groups[name])
        stages[name] = 0

    def tick(*names):
        for name in names:
            stage = stages[name]
            if stage == 0:
                work.add_pair(groups[name])
            elif stage <= bit_count:
                work.advance(stage - 1, groups[name])
            stages[name] = stage + 1

    greet(bit_count)
    for part, source in enumerate((gq_ref, gk_ref, gv_ref)):
        store_blocks(
            joint_grad,
            product_left(attend_ref[...], source[...]),
            slice(part * width, (part + 1) * width),
        )
    begin("joint")
    sums[...] = jnp.zeros_like(sums)
    gain_first, gain_attend = gains_ref[0:1, :], gains_ref[1:2, :]

    def attend_back(rows):
        unit, spread = standardize(after_ref[rows, :])
        grad = product_right(gq_ref[rows, :], joint_ref[:, :width])
        grad = grad + product_right(gk_ref[rows, :], joint_ref[:, width : 2 * width])
        grad = grad + product_right(gv_ref[rows, :], joint_ref[:, 2 * width :])
        sums[1:2, :] = sums[1:2, :] + jnp.sum(grad * unit, axis=0, keepdims=True)
        total = stream_ref[rows, :] + standardize_back(grad * gain_attend, unit, spread)
        stream[rows, :] = total
        low[rows, :] = (0.5 * total).astype(BF16)

    loop_rows(count, attend_back)
    tick("joint")
    for at in range(0, hidden_width, chunk):
        hidden = hidden_ref[:, at : at + chunk].astype(F32)
        active[...] = (hidden * jax.nn.sigmoid(hidden)).astype(BF16)
        piece = product_left(active[...], low[...])
        lead = down_grad.shape[:-2]
        blocks = chunk * (1 << bit_count) // hidden_width
        first = at * (1 << bit_count) // hidden_width
        depth = hidden_width >> (bit_count + 1)
        for n in range(blocks):
            owner = first + n
            index = tuple((owner >> bit) & 1 for bit in range(bit_count - 1, -1, -1))
            for half in range(2):
                start = (2 * n + half) * depth
                down_grad[index + (half,)] = piece[start : start + depth].astype(BF16)
    begin("down")
    tick("joint")
    for number, at in enumerate(range(0, hidden_width, chunk)):
        cols = slice(at, at + chunk)

        def hidden_back(rows):
            hidden = hidden_ref[rows, cols].astype(F32)
            grad = product_right(low[rows, :], down_ref[cols, :])
            grad_low = (grad * swish_slope(hidden)).astype(BF16)
            active[rows, :] = grad_low
            piece = product_right(grad_low, up_ref[:, cols])
            if number == 0:
                normed_grad[rows, :] = piece
            else:
                normed_grad[rows, :] = normed_grad[rows, :] + piece

        loop_rows(count, hidden_back)
        store_blocks(up_grad, product_left(first_ref[...], active[...]), cols)
        if number < 2:
            tick("joint", "down")
        elif number == 2:
            tick("down")
    begin("up")
    tick("joint", "down")

    def first_back(rows):
        unit, spread = standardize(features_ref[rows, :].astype(F32))
        grad = normed_grad[rows, :]
        sums[0:1, :] = sums[0:1, :] + jnp.sum(grad * unit, axis=0, keepdims=True)
        total = stream[rows, :] + standardize_back(grad * gain_first, unit, spread)
        grad_ref[rows, :] = total.astype(BF16)

    loop_rows(count, first_back)
    small_ref[...] = jnp.zeros_like(small_ref)
    small_ref[0:2, :] = sums[0:2, :]
    small_ref[2:4, :] = bias_ref[0:2, :]
    small_ref[4:5, :] = conv_gain_ref[...]
    small_ref[7:9, :] = middle_ref[5:7, :]
    small_ref[9:41, :] = jnp.sum(taps_ref[...], axis=0)
    small = small_ref[...]
    store_blocks(small_grad, small.T, slice(0, small.shape[0]))
    begin("small")
    for _ in range(bit_count + 1):
        tick("joint", "down", "up", "small")
    work.finish()


TAIL_PLAN = [
    ("joint", (3, 1, 0, 16)),
    ("joint", (4, 2, 0, 16)),
    ("joint", (2, 0, 0, 7)),
    ("joint", (2, 1, 7, 11)),
    ("joint", (2, 2, 11, 16)),
    ("down", (1, 0, 0, 4)),
    ("down", (1, 1, 4, 8)),
    ("down", (1, 2, 8, 16)),
    ("up", (0, 0, 0, 5)),
    ("up", (0, 1, 5, 10)),
    ("up", (0, 2, 10, 16)),
    ("small", (5, 0, 0, 16)),
]


def tail(
    attend_grads, normed_attend, after_first, grad_stream, normed_first, features, hidden, gains,
    joint_full, up_full, down_full, rows, taps, grad_place, grad_out, collective_id,
):
    shards = lax.axis_size("shard")
    bit_count = (shards - 1).bit_length()
    lead = (2,) * bit_count
    count, width = after_first.shape
    hidden_width = up_full.shape[1]

    def blocks(rows, cols):
        return lead + (2, rows // (2 * shards), cols)

    given = [array.reshape(blocks(*array.shape)) for array in (grad_place, grad_out)]
    shapes = [
        blocks(width, hidden_width),
        blocks(hidden_width, width),
        blocks(width, 3 * width),
        given[0].shape,
        given[1].shape,
        blocks(width, 128),
    ]
    pieces, groups = [], {}
    for name, wanted in TAIL_PLAN:
        for piece in plan_pieces([shape[-2:] for shape in shapes], [wanted]):
            groups.setdefault(name, []).append(len(pieces))
            pieces.append(piece)
    vmem = pl.BlockSpec(memory_space=pltpu.VMEM)
    outs = pl.pallas_call(
        functools.partial(tail_kernel, bit_count, pieces, groups, shapes),
        in_specs=[vmem] * 17 + [pl.BlockSpec(memory_space=pl.ANY)] * 2,
        out_specs=[vmem] * 7,
        out_shape=[jax.ShapeDtypeStruct((count, width), BF16)]
        + [jax.ShapeDtypeStruct((2,) + shape[-2:], BF16) for shape in shapes],
        scratch_shapes=[
            pltpu.VMEM(shapes[2], BF16),
            pltpu.VMEM(shapes[1], BF16),
            pltpu.VMEM(shapes[0], BF16),
            pltpu.VMEM(shapes[5], BF16),
            pltpu.VMEM((count, width), F32),
            pltpu.VMEM((count, width), BF16),
            pltpu.VMEM((128, width), F32),
            pltpu.VMEM((count, width), BF16),
            pltpu.VMEM((count, width), F32),
            pltpu.VMEM((8, width), F32),
        ]
        + Scatter.scratch(bit_count, pieces),
        compiler_params=pltpu.CompilerParams(
            collective_id=collective_id,
            has_side_effects=True,
            vmem_limit_bytes=60 * 1024 * 1024,
        ),
        cost_estimate=pl.CostEstimate(
            flops=13000000000, bytes_accessed=40000000, transcendentals=5000000
        ),
    )(
        *attend_grads, normed_attend, after_first, grad_stream, normed_first, features, hidden,
        gains, joint_full, up_full, down_full, *rows, taps, *given,
    )
    return outs[0], outs[1:]


def widen_kernel(count, row_total, tap_total, *refs):
    ins, extra_ref, grad_ref = refs[:count], refs[count], refs[count + 1]
    outs, grad_out_ref = refs[count + 2 : -1], refs[-1]
    grad_out_ref[...] = grad_ref[...]
    for source, target in zip(ins[:-1], outs[:-2]):
        target[...] = source[...].astype(F32)
    small = ins[-1][...].astype(F32).T
    outs[-2][...] = small[:row_total] + extra_ref[...]
    outs[-1][...] = small[row_total : row_total + tap_total]


def widen(sums, extra_rows, tap_total, grad_inputs):
    sums = [total.reshape(-1, total.shape[-1]) for total in sums]
    replicas = lax.axis_size("replica")
    if replicas > 2:
        groups = [list(range(core, replicas, 2)) for core in range(2)]
        sums = [lax.psum(total, "replica", axis_index_groups=groups) for total in sums]
    row_total, depth = extra_rows.shape
    shapes = [total.shape for total in sums[:-1]] + [(row_total, depth), (tap_total, depth)]

    def whole(shape):
        return pl.BlockSpec(shape, lambda i: (0,) * len(shape))

    args = (*sums, extra_rows, grad_inputs)
    return pl.pallas_call(
        functools.partial(widen_kernel, len(sums), row_total, tap_total),
        grid=(1,),
        in_specs=[whole(arg.shape) for arg in args],
        out_specs=[whole(shape) for shape in shapes] + [whole(grad_inputs.shape)],
        out_shape=[jax.ShapeDtypeStruct(shape, F32) for shape in shapes]
        + [jax.ShapeDtypeStruct(grad_inputs.shape, BF16)],
        compiler_params=pltpu.CompilerParams(vmem_limit_bytes=32 * 1024 * 1024),
    )(*args)


def combine_sums(tiles):
    return jnp.sum(tiles, axis=0)


def combine_stats(local_count, tiles):
    half = tiles.shape[1] // 2
    means = tiles[:, :half]
    mean = jnp.sum(means, axis=0) * (1.0 / tiles.shape[0])
    apart = means - mean
    total = jnp.sum(tiles[:, half:] + local_count * (apart * apart), axis=0)
    return jnp.concatenate([mean, total * (1.0 / (local_count * tiles.shape[0]))], axis=0)


class Everyone:
    def __init__(self):
        self.shards = lax.axis_size("shard")
        self.count = self.shards * lax.axis_size("replica")
        self.me = lax.axis_index("replica") * self.shards + lax.axis_index("shard")

    def place(self, far):
        device = lax.rem(self.me + far, self.count)
        return (lax.div(device, self.shards), lax.rem(device, self.shards))

    def greet(self):
        barrier = pltpu.get_barrier_semaphore()

        def hello(far, carry):
            pl.semaphore_signal(barrier, inc=1, device_id=self.place(far), device_id_type=MESH)
            return carry

        lax.fori_loop(1, self.count, hello, 0)
        pl.semaphore_wait(barrier, self.count - 1)

    def copy(self, buffers, far, slot):
        tile, held, send_sem, recv_sem = buffers
        return pltpu.make_async_remote_copy(
            tile,
            held.at[slot],
            send_sem.at[far],
            recv_sem.at[far],
            device_id=self.place(far),
            device_id_type=MESH,
        )

    def send(self, buffers):
        tile, held = buffers[:2]

        def go(far, carry):
            self.copy(buffers, far, self.me).start()
            return carry

        lax.fori_loop(1, self.count, go, 0)
        held[self.me] = tile[...]

    def receive(self, buffers):
        def arrive(far, carry):
            self.copy(buffers, far, lax.rem(self.me + self.count - far, self.count)).wait_recv()
            return carry

        lax.fori_loop(1, self.count, arrive, 0)

    def close(self, buffers):
        def sent(far, carry):
            self.copy(buffers, far, self.me).wait_send()
            return carry

        lax.fori_loop(1, self.count, sent, 0)

    def scratch(self, rows):
        return [
            pltpu.VMEM((rows, 128), F32),
            pltpu.VMEM((self.count, rows, 128), F32),
            pltpu.SemaphoreType.DMA((self.count,)),
            pltpu.SemaphoreType.DMA((self.count,)),
        ]


def rows_to_tile(tile_ref, *rows):
    at = 0
    for row in rows:
        for start in range(0, row.shape[1], 128):
            tile_ref[at : at + 1, :] = row[:, start : start + 128]
            at += 1


def tile_to_row(tile, start, width):
    return jnp.concatenate(
        [tile[at : at + 1] for at in range(start, start + width // 128)], axis=1
    )


def middle_kernel(clip_length, *refs):
    (
        conv_ref, after_ref, cotangent_ref, gains_ref, stats_ref, point_ref, up_ref, down_ref,
    ) = refs[:8]
    (
        out_ref, shaped_grad_ref, stream_ref, rows_ref, totals_ref,
        point_grad_ref, up_grad_ref, down_grad_ref,
    ) = refs[8:16]
    active_conv, normed, active, back, low, low_conv, hidden, sums = refs[16:24]
    stats_buffers, sums_buffers = refs[24:28], refs[28:32]
    count, width = out_ref.shape
    hidden_width = up_ref.shape[1]
    everyone = Everyone()
    tokens = count * everyone.count

    everyone.greet()
    clips = stats_ref.shape[0]
    mean = sum(stats_ref[clip, 0:1, :] for clip in range(clips)) * (1.0 / clips)
    squares = jnp.zeros_like(mean)
    for clip in range(clips):
        apart = stats_ref[clip, 0:1, :] - mean
        squares = squares + stats_ref[clip, 1:2, :] + clip_length * (apart * apart)
    rows_to_tile(stats_buffers[0], mean, squares)
    everyone.send(stats_buffers)
    sums[...] = jnp.zeros_like(sums)
    everyone.receive(stats_buffers)
    tile = combine_stats(count, stats_buffers[1][...])
    mean = tile_to_row(tile, 0, width)
    inverse = lax.rsqrt(tile_to_row(tile, width // 128, width) + epsilon)
    scale, shift = gains_ref[5:6, :], gains_ref[6:7, :]
    gain_second, gain_final = gains_ref[7:8, :], gains_ref[8:9, :]

    def visit(rows):
        unit = (conv_ref[rows, :] - mean) * inverse
        shaped = unit * scale + shift
        active_conv[rows, :] = swish_act(shaped).astype(BF16)
        after_conv = after_ref[rows, :] + product(active_conv[rows, :], point_ref[...])
        unit_second, spread_second = standardize(after_conv)
        normed[rows, :] = (unit_second * gain_second).astype(BF16)
        total = jnp.zeros(after_conv.shape, F32)
        for at in range(0, hidden_width, width):
            cols = slice(at, at + width)
            values = product(normed[rows, :], up_ref[:, cols])
            hidden[:, cols] = values
            active[rows, cols] = swish_act(values).astype(BF16)
            total = total + product(active[rows, cols], down_ref[cols, :])
        unit_last, spread_last = standardize(after_conv + 0.5 * total)
        out_ref[rows, :] = (unit_last * gain_final).astype(BF16)
        grad = cotangent_ref[rows, :].astype(F32)
        sums[1:2, :] = sums[1:2, :] + jnp.sum(grad * unit_last, axis=0, keepdims=True)
        last = standardize_back(grad * gain_final, unit_last, spread_last)
        low[rows, :] = (0.5 * last).astype(BF16)
        total = jnp.zeros(after_conv.shape, F32)
        for at in range(0, hidden_width, width):
            cols = slice(at, at + width)
            grad = product_right(low[rows, :], down_ref[cols, :])
            back[rows, cols] = (grad * swish_slope(hidden[:, cols])).astype(BF16)
            total = total + product_right(back[rows, cols], up_ref[:, cols])
        sums[0:1, :] = sums[0:1, :] + jnp.sum(total * unit_second, axis=0, keepdims=True)
        stream = last + standardize_back(total * gain_second, unit_second, spread_second)
        stream_ref[rows, :] = stream
        low_conv[rows, :] = stream.astype(BF16)
        grad = product_right(low_conv[rows, :], point_ref[...]) * swish_slope(shaped)
        shaped_grad_ref[rows, :] = grad
        sums[2:3, :] = sums[2:3, :] + jnp.sum(grad, axis=0, keepdims=True)
        sums[3:4, :] = sums[3:4, :] + jnp.sum(grad * unit, axis=0, keepdims=True)

    loop_rows(count, visit)
    rows_to_tile(sums_buffers[0], sums[2:3, :], sums[3:4, :])
    everyone.send(sums_buffers)
    point_grad_ref[...] = product_left(active_conv[...], low_conv[...]).astype(BF16)
    for at in range(0, hidden_width, width):
        cols = slice(at, at + width)
        down_grad_ref[cols, :] = product_left(active[:, cols], low[...]).astype(BF16)
        up_grad_ref[:, cols] = product_left(normed[...], back[:, cols]).astype(BF16)
    everyone.receive(sums_buffers)
    tile = combine_sums(sums_buffers[1][...])
    shift_total = tile_to_row(tile, 0, width)
    gain_total = tile_to_row(tile, width // 128, width)
    rows_ref[0:1, :] = mean
    rows_ref[1:2, :] = inverse
    rows_ref[2:3, :] = scale * inverse
    rows_ref[3:4, :] = shift_total * (1.0 / tokens)
    rows_ref[4:5, :] = gain_total * (1.0 / tokens)
    rows_ref[5:7, :] = sums[0:2, :]
    rows_ref[7:8, :] = jnp.zeros_like(mean)
    totals_ref[...] = jnp.zeros_like(totals_ref)
    totals_ref[5:6, :] = gain_total
    totals_ref[6:7, :] = shift_total
    everyone.close(stats_buffers)
    everyone.close(sums_buffers)


def middle(
    conv_flat, after_attend, cotangent, gains, clip_stats, point_full, up_full, down_full,
    clip_length, collective_id,
):
    count, width = after_attend.shape
    hidden_width = up_full.shape[1]
    everyone = Everyone()
    vmem = pl.BlockSpec(memory_space=pltpu.VMEM)
    tile_rows_count = 2 * width // 128
    return pl.pallas_call(
        functools.partial(middle_kernel, clip_length),
        in_specs=[vmem] * 8,
        out_specs=[vmem] * 8,
        out_shape=[
            jax.ShapeDtypeStruct((count, width), BF16),
            jax.ShapeDtypeStruct((count, width), F32),
            jax.ShapeDtypeStruct((count, width), F32),
            jax.ShapeDtypeStruct((8, width), F32),
            jax.ShapeDtypeStruct((gains.shape[0], width), F32),
            jax.ShapeDtypeStruct((width, width), BF16),
            jax.ShapeDtypeStruct((width, hidden_width), BF16),
            jax.ShapeDtypeStruct((hidden_width, width), BF16),
        ],
        scratch_shapes=[
            pltpu.VMEM((count, width), BF16),
            pltpu.VMEM((count, width), BF16),
            pltpu.VMEM((count, hidden_width), BF16),
            pltpu.VMEM((count, hidden_width), BF16),
            pltpu.VMEM((count, width), BF16),
            pltpu.VMEM((count, width), BF16),
            pltpu.VMEM((row_step(count), hidden_width), F32),
            pltpu.VMEM((8, width), F32),
        ]
        + everyone.scratch(tile_rows_count)
        + everyone.scratch(tile_rows_count),
        compiler_params=pltpu.CompilerParams(
            collective_id=collective_id,
            has_side_effects=True,
            vmem_limit_bytes=60 * 1024 * 1024,
        ),
        cost_estimate=pl.CostEstimate(
            flops=15500000000, bytes_accessed=25000000, transcendentals=10000000
        ),
    )(conv_flat, after_attend, cotangent, gains, clip_stats, point_full, up_full, down_full)


def tap_windows(padded_ref, start, rows, visit):
    for shift in range(8):
        window = padded_ref[start + shift : start + shift + rows + 24, :]
        for lift in range(4):
            offset = 8 * lift + shift
            if offset > 0:
                visit(offset, window[8 * lift : 8 * lift + rows])


def fill_padded(padded_ref, values):
    length = values.shape[0]
    edge = jnp.zeros((16, values.shape[1]), F32)
    padded_ref[0:16, :] = edge
    padded_ref[16 : 16 + length, :] = values
    padded_ref[16 + length : 32 + length, :] = edge


def tile_rows(length):
    for rows in (136, 128, 120, 112, 104, 96, 88, 80, 72, 64, 56, 48, 40, 32, 24, 16, 8):
        if length % rows == 0:
            return rows
    return length


def conv_forward_kernel(linear_ref, gate_ref, taps_ref, out_ref, stats_ref, padded_ref):
    length = out_ref.shape[1]
    rows = tile_rows(length)
    fill_padded(padded_ref, linear_ref[0] * jax.nn.sigmoid(gate_ref[0]))
    for start in range(0, length, rows):
        total = [jnp.zeros((rows, out_ref.shape[2]), F32)]

        def visit(offset, window):
            total[0] = total[0] + taps_ref[offset - 1 : offset, :] * window

        tap_windows(padded_ref, start, rows, visit)
        out_ref[0, start : start + rows, :] = total[0]
    values = out_ref[0]
    mean = jnp.sum(values, axis=0, keepdims=True) * (1.0 / length)
    apart = values - mean
    squares = jnp.sum(apart * apart, axis=0, keepdims=True)
    at_row = lax.broadcasted_iota(jnp.int32, stats_ref.shape[1:], 0)
    stats_ref[0] = jnp.where(at_row == 0, mean, jnp.where(at_row == 1, squares, 0.0))


def conv_forward(mixed_clips, taps):
    clip_count, clip_length, width = mixed_clips.shape
    channels = width // 2
    blocks = channels // 128
    piece = pl.BlockSpec((1, clip_length, 128), lambda i, j: (i, 0, j))
    return pl.pallas_call(
        conv_forward_kernel,
        grid=(clip_count, blocks),
        in_specs=[
            piece,
            pl.BlockSpec((1, clip_length, 128), lambda i, j: (i, 0, blocks + j)),
            pl.BlockSpec((taps.shape[0], 128), lambda i, j: (0, j)),
        ],
        out_specs=[piece, pl.BlockSpec((1, 8, 128), lambda i, j: (i, 0, j))],
        out_shape=[
            jax.ShapeDtypeStruct((clip_count, clip_length, channels), F32),
            jax.ShapeDtypeStruct((clip_count, 8, channels), F32),
        ],
        scratch_shapes=[pltpu.VMEM((clip_length + 32, 128), F32)],
        compiler_params=pltpu.CompilerParams(vmem_limit_bytes=32 * 1024 * 1024),
        cost_estimate=pl.CostEstimate(
            flops=80000000, bytes_accessed=8000000, transcendentals=600000
        ),
    )(mixed_clips, mixed_clips, taps)


def conv_backward_kernel(
    linear_ref, gate_ref, grad_ref, conv_ref, rows_ref, taps_ref,
    out_ref, grad_taps_ref, padded_ref, grad_padded_ref, tap_sums_ref,
):
    length = grad_ref.shape[1]
    rows = tile_rows(length)
    block = pl.program_id(1)
    channels = out_ref.shape[2] // 2
    mean, inverse, scale = rows_ref[0:1, :], rows_ref[1:2, :], rows_ref[2:3, :]
    shift_mean, gain_mean = rows_ref[3:4, :], rows_ref[4:5, :]
    unit = (conv_ref[0] - mean) * inverse
    grad_conv = scale * (grad_ref[0] - shift_mean - unit * gain_mean)
    fill_padded(grad_padded_ref, grad_conv)
    fill_padded(padded_ref, linear_ref[0] * jax.nn.sigmoid(gate_ref[0]))
    tap_sums_ref[...] = jnp.zeros_like(tap_sums_ref)
    first = pl.multiple_of(block * 128, 128)
    second = pl.multiple_of(channels + block * 128, 128)
    for start in range(0, length, rows):
        grad_rows = grad_padded_ref[16 + start : 16 + start + rows, :]

        def visit(offset, window):
            product_rows = (grad_rows * window).reshape(rows // 8, 8, window.shape[1])
            tap_sums_ref[offset - 1] = tap_sums_ref[offset - 1] + jnp.sum(product_rows, axis=0)

        tap_windows(padded_ref, start, rows, visit)
        total = [jnp.zeros((rows, 128), F32)]

        def visit_back(offset, window):
            total[0] = total[0] + taps_ref[31 - offset : 32 - offset, :] * window

        tap_windows(grad_padded_ref, start, rows, visit_back)
        grad_gated = total[0]
        gate = jax.nn.sigmoid(gate_ref[0, start : start + rows, :])
        grad_linear = grad_gated * gate
        linear = linear_ref[0, start : start + rows, :]
        out_ref[0, start : start + rows, pl.ds(first, 128)] = grad_linear.astype(BF16)
        out_ref[0, start : start + rows, pl.ds(second, 128)] = (
            grad_linear * linear * (1.0 - gate)
        ).astype(BF16)
    grad_taps_ref[0] = jnp.sum(tap_sums_ref[...], axis=1)


def conv_backward(mixed_clips, grad_clips, conv_clips, rows, taps):
    clip_count, clip_length, width = mixed_clips.shape
    channels = width // 2
    blocks = channels // 128
    piece = pl.BlockSpec((1, clip_length, 128), lambda i, j: (i, 0, j))
    return pl.pallas_call(
        conv_backward_kernel,
        grid=(clip_count, blocks),
        in_specs=[
            piece,
            pl.BlockSpec((1, clip_length, 128), lambda i, j: (i, 0, blocks + j)),
            piece,
            piece,
            pl.BlockSpec((8, 128), lambda i, j: (0, j)),
            pl.BlockSpec((taps.shape[0], 128), lambda i, j: (0, j)),
        ],
        out_specs=[
            pl.BlockSpec((1, clip_length, width), lambda i, j: (i, 0, 0)),
            pl.BlockSpec((1, 32, 128), lambda i, j: (i, 0, j)),
        ],
        out_shape=[
            jax.ShapeDtypeStruct((clip_count, clip_length, width), BF16),
            jax.ShapeDtypeStruct((clip_count, 32, channels), F32),
        ],
        scratch_shapes=[
            pltpu.VMEM((clip_length + 32, 128), F32),
            pltpu.VMEM((clip_length + 32, 128), F32),
            pltpu.VMEM((32, 8, 128), F32),
        ],
        compiler_params=pltpu.CompilerParams(vmem_limit_bytes=32 * 1024 * 1024),
        cost_estimate=pl.CostEstimate(
            flops=160000000, bytes_accessed=14000000, transcendentals=1200000
        ),
    )(mixed_clips, mixed_clips, grad_clips, conv_clips, rows, taps)


EARLY_PLAN = [
    (0, 0, 0, 10),
    (0, 1, 10, 16),
    (1, 1, 0, 4),
    (1, 2, 4, 16),
    (2, 0, 0, 16),
    (3, 0, 0, 6),
    (3, 1, 6, 16),
    (4, 2, 0, 16),
]
LATE_PLAN = [(0, 1, 0, 16), (1, 1, 0, 16), (2, 1, 0, 16), (3, 0, 0, 16), (4, 2, 0, 16)]
LATE_BACK_PLAN = [(0, 1, 0, 16), (1, 1, 0, 16), (2, 0, 0, 16), (3, 2, 0, 16)]


def body(
    features,
    frame_times,
    cotangent,
    vectors,
    first_up,
    first_down,
    query_key_value,
    place_weight,
    out_weight,
    point_glu,
    depth_taps,
    point_out,
    second_up,
    second_down,
):
    clip_count, clip_length, model_width = features.shape
    row_count = clip_count * clip_length
    row_total = vectors.shape[0]
    tap_total = depth_taps.shape[0]

    small_shard = pack_small([vectors.T, depth_taps.T])
    up_one, down_one, small_full, joint_full, place_full = gather_arrays(
        [first_up, first_down, small_shard, query_key_value, place_weight], EARLY_PLAN, 1
    )
    small = small_full.T
    first_full = (small[:row_total], up_one, down_one)
    gains = first_full[0].astype(jnp.float32)
    inputs = features.reshape(row_count, model_width).astype(jnp.float32)
    first_out, first_kept = feed_forward(inputs, gains[0], first_full[1], first_full[2])
    after_first = inputs + 0.5 * first_out
    normed_attend = normalize(after_first, gains[1]).astype(jnp.bfloat16)
    joint_rows = product(normed_attend, joint_full)
    joint_clips = joint_rows.reshape(clip_count, clip_length, 3 * model_width)
    attend_parts = attention_inputs(joint_clips, gains, model_width)
    sine_flat, cos_flat = wave_table(frame_times.reshape(row_count), model_width)
    sine_rows = sine_flat.reshape(clip_count, clip_length, -1)
    cosines = cos_flat.reshape(clip_count, clip_length, -1)
    context_clips, probs, late_full = attention_forward(
        attend_parts,
        place_full,
        sine_rows,
        cosines,
        [out_weight, point_glu, point_out, second_up, second_down],
        LATE_PLAN,
        2,
    )
    out_full = late_full[0]
    conv_full = (late_full[1], late_full[2])
    tap_rows = small[row_total : row_total + tap_total]
    second_full = late_full[3:]
    context_low = context_clips.reshape(row_count, model_width)
    after_attend = after_first + product(context_low, out_full)
    normed_conv = normalize(after_attend, gains[4]).astype(jnp.bfloat16)
    mixed_rows = product(normed_conv, conv_full[0]).reshape(
        clip_count, clip_length, 2 * model_width
    )
    taps = jnp.pad(tap_rows.astype(jnp.float32), ((0, 32 - tap_total), (0, 0)))
    conv_clips, clip_stats = conv_forward(mixed_rows, taps)
    conv_flat = conv_clips.reshape(row_count, model_width)
    (
        output,
        grad_shaped,
        grad_conv_out,
        middle_rows,
        batch_grads,
        grad_point_out,
        grad_second_up,
        grad_second_down,
    ) = middle(
        conv_flat,
        after_attend,
        cotangent.reshape(row_count, model_width),
        gains,
        clip_stats,
        conv_full[1],
        second_full[0],
        second_full[1],
        clip_length,
        3,
    )
    grad_mixed_clips, clip_taps = conv_backward(
        mixed_rows,
        grad_shaped.reshape(clip_count, clip_length, model_width),
        conv_clips,
        middle_rows,
        taps,
    )
    grad_mixed_low = grad_mixed_clips.reshape(row_count, 2 * model_width)
    grad_point_glu = product_left(normed_conv, grad_mixed_low)
    grad_extra, grad_conv_gain = normalize_back(
        after_attend, gains[4], product_right(grad_mixed_low, conv_full[0])
    )
    grad_attend_out = grad_conv_out + grad_extra
    grad_low = grad_attend_out.astype(jnp.bfloat16)
    grad_out_weight = product_left(context_low, grad_low)
    grad_context = (
        product_right(grad_low, out_full)
        .astype(jnp.bfloat16)
        .reshape(clip_count, clip_length, model_width)
    )
    attend_grads, late_sums = attention_backward(
        attend_parts,
        grad_context,
        place_full,
        sine_rows,
        cosines,
        probs,
        [
            array.astype(BF16)
            for array in (grad_point_glu, grad_point_out, grad_second_up, grad_second_down)
        ],
        LATE_BACK_PLAN,
        5,
    )
    grad_query, grad_key, grad_value, grad_bias, grad_place = attend_grads
    attend_low = [
        array.reshape(row_count, model_width) for array in (grad_query, grad_key, grad_value)
    ]
    grad_inputs, early_sums = tail(
        attend_low,
        normed_attend,
        after_first,
        grad_attend_out,
        first_kept[0],
        features.reshape(row_count, model_width),
        first_kept[1],
        gains,
        joint_full,
        first_full[1],
        first_full[2],
        [grad_bias, grad_conv_gain[None], middle_rows],
        clip_taps,
        grad_place.astype(BF16),
        grad_out_weight.astype(BF16),
        6,
    )
    shard_cols = vectors.shape[1]
    first_col = lax.axis_index("shard") * shard_cols
    batch_grads = lax.dynamic_slice_in_dim(batch_grads, first_col, shard_cols, axis=1)
    summed = widen(
        [*early_sums[:5], *late_sums, early_sums[5]], batch_grads, tap_total, grad_inputs
    )
    return (
        output.reshape(clip_count, clip_length, model_width),
        summed[11].reshape(clip_count, clip_length, model_width),
        summed[9],
        *summed[:6],
        summed[10],
        *summed[6:9],
    )


def solution(mesh):
    return jax.shard_map(
        body,
        mesh=mesh,
        in_specs=(
            P(("replica", "shard"), None, None),
            P(("replica", "shard"), None),
            P(("replica", "shard"), None, None),
            P(None, "shard"),
            P("shard", None),
            P("shard", None),
            P("shard", None),
            P("shard", None),
            P("shard", None),
            P("shard", None),
            P(None, "shard"),
            P("shard", None),
            P("shard", None),
            P("shard", None),
        ),
        out_specs=(
            P(("replica", "shard"), None, None),
            P(("replica", "shard"), None, None),
            P(None, "shard"),
            P("shard", None),
            P("shard", None),
            P("shard", None),
            P("shard", None),
            P("shard", None),
            P("shard", None),
            P(None, "shard"),
            P("shard", None),
            P("shard", None),
            P("shard", None),
        ),
        check_vma=False,
    )
```

```python
import functools
import math

import jax
import jax.numpy as jnp
from jax import lax
from jax.experimental import pallas as pl
from jax.experimental.pallas import tpu as pltpu
from jax.sharding import PartitionSpec as P

HEADS = 8
HEAD_DIM = 64


epsilon = 1e-05


def normalize(values, gain_row):
    center = values - jnp.mean(values, axis=-1, keepdims=True)
    spread = jnp.mean(center * center, axis=-1, keepdims=True)
    return center * lax.rsqrt(spread + epsilon) * gain_row


def normalize_back(values, gain_row, grad_normed):
    pull = jax.vjp(normalize, values, gain_row)[1]
    return pull(grad_normed)


def swish_act(values):
    return values * jax.nn.sigmoid(values)


def swish_slope(values):
    sigmoid = jax.nn.sigmoid(values)
    return sigmoid * (1.0 + values * (1.0 - sigmoid))


def wave_table(frame_pos, model_width):
    half_width = model_width // 2
    frequency = jnp.exp(
        jnp.arange(half_width, dtype=jnp.float32) * (-math.log(10000.0) / half_width)
    )
    angles = frame_pos.astype(jnp.float32)[:, None] * frequency[None, :]
    return (jnp.sin(angles), jnp.cos(angles))


def product(left_side, right_side):
    return jnp.dot(left_side, right_side, preferred_element_type=jnp.float32)


def product_left(left_side, right_side):
    return lax.dot_general(
        left_side, right_side, (((0,), (0,)), ((), ())), preferred_element_type=jnp.float32
    )


def product_right(left_side, right_side):
    return lax.dot_general(
        left_side, right_side, (((1,), (1,)), ((), ())), preferred_element_type=jnp.float32
    )


def feed_forward(inputs, gain_row, up_full, down_full):
    normed_low = normalize(inputs, gain_row).astype(jnp.bfloat16)
    hidden = product(normed_low, up_full)
    active_low = swish_act(hidden).astype(jnp.bfloat16)
    return (product(active_low, down_full), (normed_low, hidden.astype(BF16), active_low))


def head_probs(query_u, query_v, key_low, place_head, sine_rows, cosines, basis_low):
    raw_place = product_right(query_v, place_head)
    half_width = raw_place.shape[-1] // 2
    part_sin = raw_place[:, :half_width]
    part_cos = raw_place[:, half_width:]
    coeff_low = jnp.concatenate(
        [part_sin * sine_rows + part_cos * cosines, part_cos * sine_rows - part_sin * cosines],
        axis=-1,
    ).astype(jnp.bfloat16)
    scores = product_right(query_u, key_low) + product_right(coeff_low, basis_low)
    scores = scores * (1.0 / math.sqrt(HEAD_DIM))
    row_peak = jnp.max(scores, axis=-1, keepdims=True)
    raised = jnp.exp(scores - row_peak)
    return raised * (1.0 / jnp.sum(raised, axis=-1, keepdims=True))


def forward_kernel(bit_count, pieces, array_count, *refs):
    qu_ref, qv_ref, key_ref, value_ref, place_ref, sine_ref, cos_ref = refs[:7]
    shards = refs[7 : 7 + array_count]
    out_ref, probs_ref = refs[7 + array_count : 9 + array_count]
    fulls = refs[9 + array_count : 9 + 2 * array_count]
    gather = Gather(bit_count, pieces, shards, fulls, refs[9 + 2 * array_count :])
    step = pl.program_id(0) * pl.num_programs(1) + pl.program_id(1)
    steps = pl.num_programs(0) * pl.num_programs(1)

    @pl.when(step == 0)
    def begin():
        say_hello(bit_count)

    sine_rows = sine_ref[0]
    cosines = cos_ref[0]
    basis_low = jnp.concatenate([cosines, sine_rows], axis=-1).astype(jnp.bfloat16)
    merged = []
    for head, at in enumerate(range(0, out_ref.shape[-1], HEAD_DIM)):
        cols = slice(at, at + HEAD_DIM)
        probs = head_probs(
            qu_ref[0][:, cols],
            qv_ref[0][:, cols],
            key_ref[0][:, cols],
            place_ref[:, cols],
            sine_rows,
            cosines,
            basis_low,
        ).astype(jnp.bfloat16)
        probs_ref[0, head] = probs
        merged.append(product(probs, value_ref[0][:, cols]))
    out_ref[0] = jnp.concatenate(merged, axis=-1).astype(jnp.bfloat16)

    @pl.when(step == 0)
    def depart():
        hear_all(bit_count)
        gather.start()

    for phase in range(bit_count):
        when = (2, 3, 5)[phase] if phase < min(3, bit_count - 1) else steps - 1

        @pl.when(step == when)
        def go(phase=phase):
            if phase == 0:
                gather.land()
            gather.advance(phase)

    @pl.when(step == steps - 1)
    def end():
        gather.finish()


def backward_kernel(bit_count, pieces, array_count, *refs):
    qu_ref, qv_ref, key_ref, value_ref, grad_ref, place_ref, sine_ref, cos_ref, probs_ref = refs[:9]
    partials = refs[9 : 9 + array_count]
    refs = refs[9 + array_count :]
    grad_query_ref, grad_key_ref, grad_value_ref, grad_bias_ref, grad_place_ref = refs[:5]
    owned = refs[5 : 5 + array_count]
    scatter = Scatter(bit_count, pieces, partials, owned, refs[5 + array_count :])
    step = pl.program_id(0) * pl.num_programs(1) + pl.program_id(1)
    steps = pl.num_programs(0) * pl.num_programs(1)

    @pl.when(step == 0)
    def begin():
        say_hello(bit_count)

    sine_rows = sine_ref[0]
    cosines = cos_ref[0]
    basis_low = jnp.concatenate([cosines, sine_rows], axis=-1).astype(jnp.bfloat16)
    half_width = sine_rows.shape[-1]
    queries, keys, values, sums_u, sums_v, places = ([], [], [], [], [], [])
    for head, at in enumerate(range(0, grad_query_ref.shape[-1], HEAD_DIM)):
        cols = slice(at, at + HEAD_DIM)
        query_u = qu_ref[0][:, cols]
        query_v = qv_ref[0][:, cols]
        key_low = key_ref[0][:, cols]
        place_head = place_ref[:, cols]
        grad_head = grad_ref[0][:, cols]
        probs_low = probs_ref[0, head]
        values.append(product_left(probs_low, grad_head))
        probs = probs_low.astype(jnp.float32)
        grad_probs = product_right(grad_head, value_ref[0][:, cols])
        inner_sum = jnp.sum(grad_probs * probs, axis=-1, keepdims=True)
        grad_scores = (probs * (grad_probs - inner_sum) * (1.0 / math.sqrt(HEAD_DIM))).astype(
            jnp.bfloat16
        )
        grad_u = product(grad_scores, key_low)
        keys.append(product_left(grad_scores, query_u))
        grad_coeff = product(grad_scores, basis_low)
        grad_a = grad_coeff[:, :half_width]
        grad_b = grad_coeff[:, half_width:]
        grad_raw = jnp.concatenate(
            [grad_a * sine_rows - grad_b * cosines, grad_a * cosines + grad_b * sine_rows],
            axis=-1,
        ).astype(jnp.bfloat16)
        grad_v = product(grad_raw, place_head)
        places.append(product_left(grad_raw, query_v))
        queries.append(grad_u + grad_v)
        sums_u.append(jnp.sum(grad_u, axis=0, keepdims=True))
        sums_v.append(jnp.sum(grad_v, axis=0, keepdims=True))
    grad_query_ref[0] = jnp.concatenate(queries, axis=-1).astype(jnp.bfloat16)
    grad_key_ref[0] = jnp.concatenate(keys, axis=-1).astype(jnp.bfloat16)
    grad_value_ref[0] = jnp.concatenate(values, axis=-1).astype(jnp.bfloat16)
    row_u = jnp.concatenate(sums_u, axis=-1)
    row_v = jnp.concatenate(sums_v, axis=-1)
    at_row = lax.broadcasted_iota(jnp.int32, grad_bias_ref.shape, 0)
    bias = jnp.where(at_row == 0, row_u, jnp.where(at_row == 1, row_v, 0.0))
    place_sum = jnp.concatenate(places, axis=-1)

    @pl.when(pl.program_id(1) == 0)
    def first_clip():
        grad_bias_ref[...] = bias
        grad_place_ref[...] = place_sum

    @pl.when(pl.program_id(1) > 0)
    def later_clip():
        grad_bias_ref[...] = grad_bias_ref[...] + bias
        grad_place_ref[...] = grad_place_ref[...] + place_sum

    @pl.when(step == 0)
    def depart():
        hear_all(bit_count)
        scatter.start()

    @pl.when(step == 1)
    def pair():
        scatter.add_pair()

    for phase in range(bit_count):
        when = (3, 5, 6)[phase] if phase < min(3, bit_count - 1) else steps - 1

        @pl.when(step == when)
        def go(phase=phase):
            scatter.advance(phase)

    @pl.when(step == steps - 1)
    def end():
        scatter.finish()


def attention_specs(clip_length, model_width):
    rows = pl.BlockSpec((1, clip_length, 128), lambda i, j: (i, 0, j))
    place = pl.BlockSpec((model_width, 128), lambda i, j: (0, j))
    wave = pl.BlockSpec((1, clip_length, model_width // 2), lambda i, j: (i, 0, 0))
    return (rows, place, wave)


def attention_inputs(joint_clips, gains, model_width):
    query = joint_clips[..., :model_width]
    return (
        (query + gains[2]).astype(jnp.bfloat16),
        (query + gains[3]).astype(jnp.bfloat16),
        joint_clips[..., model_width : 2 * model_width].astype(jnp.bfloat16),
        joint_clips[..., 2 * model_width :].astype(jnp.bfloat16),
    )


def attention_forward(parts, place_full, sine_rows, cosines, shards, wanted, collective_id):
    clip_count, clip_length, model_width = parts[0].shape
    rows, place, wave = attention_specs(clip_length, model_width)
    bit_count = (lax.axis_size("shard") - 1).bit_length()
    ins = [halves(array) for array in shards]
    pieces = plan_pieces([array.shape[1:] for array in ins], wanted)
    lead = (2,) * bit_count
    whole = pl.BlockSpec(memory_space=pl.ANY)
    heads = model_width // HEAD_DIM
    outs = pl.pallas_call(
        functools.partial(forward_kernel, bit_count, pieces, len(ins)),
        grid=(clip_count, model_width // 128),
        in_specs=[rows, rows, rows, rows, place, wave, wave] + [whole] * len(ins),
        out_specs=[
            rows,
            pl.BlockSpec((1, 2, clip_length, clip_length), lambda i, j: (i, j, 0, 0)),
        ]
        + [whole] * len(ins),
        out_shape=[
            jax.ShapeDtypeStruct(parts[0].shape, jnp.bfloat16),
            jax.ShapeDtypeStruct((clip_count, heads, clip_length, clip_length), jnp.bfloat16),
        ]
        + [jax.ShapeDtypeStruct(lead + array.shape, BF16) for array in ins],
        scratch_shapes=Gather.scratch(bit_count, pieces, len(ins)),
        compiler_params=pltpu.CompilerParams(
            vmem_limit_bytes=48 * 1024 * 1024, collective_id=collective_id, has_side_effects=True
        ),
        cost_estimate=pl.CostEstimate(
            flops=16000000000, bytes_accessed=12000000, transcendentals=5000000
        ),
    )(*parts, place_full, sine_rows, cosines, *ins)
    fulls = [out.reshape(-1, array.shape[1]) for out, array in zip(outs[2:], shards)]
    return outs[0], outs[1], fulls


def attention_backward(
    parts, grad_context, place_full, sine_rows, cosines, probs, partials, wanted, collective_id
):
    clip_count, clip_length, model_width = parts[0].shape
    rows = pl.BlockSpec((1, clip_length, 128), lambda j, i: (i, 0, j))
    place = pl.BlockSpec((model_width, 128), lambda j, i: (0, j))
    wave = pl.BlockSpec((1, clip_length, model_width // 2), lambda j, i: (i, 0, 0))
    like = jax.ShapeDtypeStruct(parts[0].shape, jnp.bfloat16)
    bit_count, ins, pieces, shapes = scatter_plan(partials, wanted)
    outs = pl.pallas_call(
        functools.partial(backward_kernel, bit_count, pieces, len(ins)),
        grid=(model_width // 128, clip_count),
        in_specs=[
            rows,
            rows,
            rows,
            rows,
            rows,
            place,
            wave,
            wave,
            pl.BlockSpec((1, 2, clip_length, clip_length), lambda j, i: (i, j, 0, 0)),
        ]
        + [pl.BlockSpec(memory_space=pl.ANY)] * len(ins),
        out_specs=[
            rows,
            rows,
            rows,
            pl.BlockSpec((8, 128), lambda j, i: (0, j)),
            pl.BlockSpec((model_width, 128), lambda j, i: (0, j)),
        ]
        + [pl.BlockSpec(shape.shape, lambda i, j: (0, 0, 0)) for shape in shapes],
        out_shape=[
            like,
            like,
            like,
            jax.ShapeDtypeStruct((8, model_width), jnp.float32),
            jax.ShapeDtypeStruct((model_width, model_width), jnp.float32),
        ]
        + shapes,
        scratch_shapes=Scatter.scratch(bit_count, pieces),
        compiler_params=pltpu.CompilerParams(
            vmem_limit_bytes=56 * 1024 * 1024, collective_id=collective_id, has_side_effects=True
        ),
        cost_estimate=pl.CostEstimate(
            flops=80000000000, bytes_accessed=20000000, transcendentals=5000000
        ),
    )(*parts, grad_context, place_full, sine_rows, cosines, probs, *ins)
    return outs[:5], outs[5:]


def pack_small(columns):
    joined = jnp.concatenate(columns, axis=1)
    return jnp.pad(joined, ((0, 0), (0, -joined.shape[1] % 128)))


MESH = pl.DeviceIdType.MESH
BF16 = jnp.bfloat16
F32 = jnp.float32


def bit_of(index, bit):
    return lax.rem(lax.div(index, 1 << bit), 2)


def flip_bit(index, bit):
    return index + (1 - 2 * bit_of(index, bit)) * (1 << bit)


def link_orders(bit_count):
    far = list(range(bit_count - 1, 2, -1))
    if bit_count < 3:
        return [list(range(bit_count))] * 3
    return [far + [1, 2, 0], far + [2, 0, 1], far + [0, 1, 2]]


def greet(bit_count):
    say_hello(bit_count)
    hear_all(bit_count)


def hear_all(bit_count):
    pl.semaphore_wait(pltpu.get_barrier_semaphore(), bit_count + 1)


def say_hello(bit_count):
    shard = lax.axis_index("shard")
    replica = lax.axis_index("replica")
    barrier = pltpu.get_barrier_semaphore()
    for bit in range(bit_count):
        pl.semaphore_signal(
            barrier, inc=1, device_id={"shard": flip_bit(shard, bit)}, device_id_type=MESH
        )
    pl.semaphore_signal(
        barrier, inc=1, device_id={"replica": flip_bit(replica, 0)}, device_id_type=MESH
    )


def block_index(bit_count, free_bits, values):
    return tuple(
        slice(None) if bit in free_bits else values[bit] for bit in range(bit_count - 1, -1, -1)
    )


class Piece:
    def __init__(self, array, color, rows, cols):
        self.array, self.color, self.rows, self.cols = array, color, rows, cols

    @property
    def tail(self):
        return (pl.ds(*self.rows), pl.ds(*self.cols))

    @property
    def shape(self):
        return (self.rows[1], self.cols[1])


def plan_pieces(shapes, wanted):
    pieces = []
    for array, color, low, high in wanted:
        rows, cols = shapes[array]
        if cols >= 2048 or cols % (16 * 128) == 0 or rows < 32:
            unit = cols // 128
            a, b = unit * low // 16 * 128, unit * high // 16 * 128
            wide = ((0, rows), (a, b - a))
        else:
            unit = rows // 16
            a, b = unit * low // 16 * 16, unit * high // 16 * 16
            wide = ((a, b - a), (0, cols))
        if b > a:
            pieces.append(Piece(array, color, *wide))
    return pieces


class Gather:
    def __init__(self, bit_count, pieces, ins, outs, sems):
        self.bits, self.pieces, self.ins, self.outs = bit_count, pieces, ins, outs
        self.send, self.recv, self.core_send, self.core_recv, self.local = sems
        shard = lax.axis_index("shard")
        replica = lax.axis_index("replica")
        self.shard, self.half = shard, lax.rem(replica, 2)
        self.core = {"replica": flip_bit(replica, 0)}
        self.own = [bit_of(shard, bit) for bit in range(bit_count)]
        self.orders = link_orders(bit_count)

    @staticmethod
    def scratch(bit_count, pieces, array_count):
        grid = (len(pieces), bit_count)
        return [pltpu.SemaphoreType.DMA(grid)] * 4 + [pltpu.SemaphoreType.DMA((array_count,))]

    def local_copies(self):
        index = block_index(self.bits, (), self.own)
        return [
            pltpu.make_async_copy(self.ins[a], self.outs[a].at[index], self.local.at[a])
            for a in range(len(self.ins))
        ]

    def hop(self, p, step):
        piece = self.pieces[p]
        order = self.orders[piece.color]
        out = self.outs[piece.array]
        index = block_index(self.bits, order[:step], self.own)
        region = out.at[index + (self.half,) + piece.tail]
        if step == 0:
            source = self.ins[piece.array].at[(self.half,) + piece.tail]
        else:
            source = region
        return pltpu.make_async_remote_copy(
            source,
            region,
            self.send.at[p, step],
            self.recv.at[p, step],
            device_id={"shard": flip_bit(self.shard, order[step])},
            device_id_type=MESH,
        )

    def cross(self, p, step):
        piece = self.pieces[p]
        order = self.orders[piece.color]
        values = list(self.own)
        values[order[step]] = 1 - values[order[step]]
        index = block_index(self.bits, order[:step], values)
        region = self.outs[piece.array].at[index + (self.half,) + piece.tail]
        return pltpu.make_async_remote_copy(
            region,
            region,
            self.core_send.at[p, step],
            self.core_recv.at[p, step],
            device_id=self.core,
            device_id_type=MESH,
        )

    def start(self, which=None):
        for p in range(len(self.pieces)) if which is None else which:
            self.hop(p, 0).start()
        for copy in self.local_copies():
            copy.start()

    def land(self):
        for copy in self.local_copies():
            copy.wait()

    def advance(self, step, which=None):
        for p in range(len(self.pieces)) if which is None else which:
            self.hop(p, step).wait_recv()
            if step + 1 < self.bits:
                self.hop(p, step + 1).start()
            self.cross(p, step).start()

    def finish(self, which=None):
        for p in range(len(self.pieces)) if which is None else which:
            for step in range(self.bits):
                self.hop(p, step).wait_send()
                self.cross(p, step).wait()


class Scatter:
    def __init__(self, bit_count, pieces, ins, outs, refs):
        self.bits, self.pieces, self.ins, self.outs = bit_count, pieces, ins, outs
        count = len(pieces)
        self.first = refs[:count]
        self.total = refs[count : 2 * count]
        self.last = refs[2 * count : 3 * count]
        self.send, self.recv, self.local = refs[3 * count : 3 * count + 3]
        land = refs[3 * count + 3 :]
        self.land = [land[p * bit_count : (p + 1) * bit_count] for p in range(count)]
        shard = lax.axis_index("shard")
        replica = lax.axis_index("replica")
        self.shard, self.half = shard, lax.rem(replica, 2)
        self.core = {"replica": flip_bit(replica, 0)}
        self.own = [bit_of(shard, bit) for bit in range(bit_count)]
        self.orders = [order[::-1] for order in link_orders(bit_count)]

    @staticmethod
    def scratch(bit_count, pieces):
        lead = (2,) * bit_count
        return (
            [pltpu.VMEM(lead + piece.shape, BF16) for piece in pieces]
            + [pltpu.VMEM(lead + piece.shape, BF16) for piece in pieces]
            + [pltpu.VMEM(piece.shape, BF16) for piece in pieces]
            + [pltpu.SemaphoreType.DMA((len(pieces), bit_count + 2))] * 2
            + [pltpu.SemaphoreType.DMA((len(pieces),))]
            + [
                pltpu.VMEM((2,) * (bit_count - step - 1) + piece.shape, BF16)
                for piece in pieces
                for step in range(bit_count)
            ]
        )

    def copy(self, p, step, source, target, device):
        return pltpu.make_async_remote_copy(
            source,
            target,
            self.send.at[p, step],
            self.recv.at[p, step],
            device_id=device,
            device_id_type=MESH,
        )

    def pair(self, p):
        piece = self.pieces[p]
        lead = (slice(None),) * self.bits
        source = self.ins[piece.array].at[lead + (1 - self.half,) + piece.tail]
        return self.copy(p, 0, source, self.first[p], self.core)

    def keep(self, p):
        piece = self.pieces[p]
        lead = (slice(None),) * self.bits
        source = self.ins[piece.array].at[lead + (self.half,) + piece.tail]
        return pltpu.make_async_copy(source, self.total[p], self.local.at[p])

    def hop(self, p, step):
        order = self.orders[self.pieces[p].color]
        bit = order[step]
        values = list(self.own)
        values[bit] = 1 - values[bit]
        index = block_index(self.bits, order[step + 1 :], values)
        return self.copy(
            p,
            step + 1,
            self.total[p].at[index],
            self.land[p][step],
            {"shard": flip_bit(self.shard, bit)},
        )

    def final(self, p):
        index = block_index(self.bits, (), self.own)
        return self.copy(p, self.bits + 1, self.total[p].at[index], self.last[p], self.core)

    def start(self, which=None):
        for p in range(len(self.pieces)) if which is None else which:
            self.pair(p).start()
            self.keep(p).start()

    def add_pair(self, which=None):
        for p in range(len(self.pieces)) if which is None else which:
            self.pair(p).wait_recv()
            self.keep(p).wait()
            self.total[p][...] = self.total[p][...] + self.first[p][...]
            self.hop(p, 0).start()

    def advance(self, step, which=None):
        for p in range(len(self.pieces)) if which is None else which:
            piece = self.pieces[p]
            order = self.orders[piece.color]
            self.hop(p, step).wait_recv()
            index = block_index(self.bits, order[step + 1 :], self.own)
            self.total[p][index] = self.total[p][index] + self.land[p][step][...]
            if step + 1 < self.bits:
                self.hop(p, step + 1).start()
            else:
                self.final(p).start()

    def finish(self):
        index = block_index(self.bits, (), self.own)
        for p, piece in enumerate(self.pieces):
            self.outs[piece.array][(self.half,) + piece.tail] = self.total[p][index]
            self.final(p).wait_recv()
            self.outs[piece.array][(1 - self.half,) + piece.tail] = self.last[p][...]
        for p in range(len(self.pieces)):
            self.pair(p).wait_send()
            for step in range(self.bits):
                self.hop(p, step).wait_send()
            self.final(p).wait_send()


def gather_kernel(bit_count, pieces, array_count, *refs):
    ins, outs = refs[:array_count], refs[array_count : 2 * array_count]
    greet(bit_count)
    work = Gather(bit_count, pieces, ins, outs, refs[2 * array_count :])
    work.start()
    work.land()
    for step in range(bit_count):
        work.advance(step)
    work.finish()


def halves(array):
    return array.reshape(2, array.shape[0] // 2, array.shape[1])


def gather_arrays(arrays, wanted, collective_id):
    bit_count = (lax.axis_size("shard") - 1).bit_length()
    ins = [halves(array) for array in arrays]
    pieces = plan_pieces([array.shape[1:] for array in ins], wanted)
    lead = (2,) * bit_count
    outs = pl.pallas_call(
        functools.partial(gather_kernel, bit_count, pieces, len(ins)),
        in_specs=[pl.BlockSpec(memory_space=pl.ANY)] * len(ins),
        out_specs=[pl.BlockSpec(memory_space=pl.ANY)] * len(ins),
        out_shape=[jax.ShapeDtypeStruct(lead + array.shape, BF16) for array in ins],
        scratch_shapes=Gather.scratch(bit_count, pieces, len(ins)),
        compiler_params=pltpu.CompilerParams(collective_id=collective_id, has_side_effects=True),
    )(*ins)
    return [
        out.reshape(-1, array.shape[1]) for out, array in zip(outs, arrays)
    ]


def scatter_plan(arrays, wanted):
    shards = lax.axis_size("shard")
    bit_count = (shards - 1).bit_length()
    lead = (2,) * bit_count
    ins = [
        array.reshape(lead + (2, array.shape[0] // (2 * shards), array.shape[1]))
        for array in arrays
    ]
    pieces = plan_pieces([array.shape[-2:] for array in ins], wanted)
    shapes = [jax.ShapeDtypeStruct((2,) + array.shape[-2:], BF16) for array in ins]
    return bit_count, ins, pieces, shapes


def row_step(count, largest=544):
    for rows in (544, 272, 256, 128, 64, 32, 16):
        if rows <= largest and count % rows == 0:
            return rows
    return count


def loop_rows(count, visit, between=None, largest=544):
    rows = row_step(count, largest)
    steps = count // rows

    def step(number, carry):
        visit(pl.ds(pl.multiple_of(number * rows, 16), rows))
        if between is not None:
            for at in range(steps):

                @pl.when(number == at)
                def slot():
                    between()

        return carry

    lax.fori_loop(0, steps, step, ())


def standardize(values):
    center = values - jnp.mean(values, axis=-1, keepdims=True)
    spread = lax.rsqrt(jnp.mean(center * center, axis=-1, keepdims=True) + epsilon)
    return center * spread, spread


def standardize_back(grad, unit, spread):
    inner = jnp.mean(grad * unit, axis=-1, keepdims=True)
    return spread * (grad - jnp.mean(grad, axis=-1, keepdims=True) - unit * inner)


def store_blocks(ref, value, cols):
    value = value.reshape(ref.shape[:-1] + (value.shape[-1],))
    ref[(slice(None),) * (len(ref.shape) - 1) + (cols,)] = value.astype(BF16)


def first_kernel(bit_count, pieces, groups, *refs):
    total_arrays = len(groups["arrays"])
    features_ref, times_ref, frequency_ref = refs[:3]
    ins = refs[3 : 3 + total_arrays]
    refs = refs[3 + total_arrays :]
    normed_ref, hidden_ref, after_ref, attend_ref, sine_ref, cos_ref, rows_ref = refs[:7]
    outs = refs[7 : 7 + total_arrays]
    work = Gather(bit_count, pieces, ins, outs, refs[7 + total_arrays :])
    up_ref, down_ref, small_ref = outs[:3]
    count, width = features_ref.shape
    hidden_width = up_ref.shape[-1]
    soon, later = groups["soon"], groups["later"]

    greet(bit_count)
    work.start(soon)

    def waves(rows):
        angles = times_ref[rows, :].astype(F32) * frequency_ref[...]
        sine_ref[rows, :] = jnp.sin(angles)
        cos_ref[rows, :] = jnp.cos(angles)

    loop_rows(count, waves)
    work.land()
    for step in range(bit_count):
        work.advance(step, soon)
    for p in later:
        work.hop(p, 0).start()
    work.finish(soon)
    rows_ref[...] = small_ref[...].astype(F32).reshape(width, 128).T
    gain_first, gain_attend = rows_ref[0:1, :], rows_ref[1:2, :]
    done = []

    def between():
        if len(done) < bit_count:
            work.advance(len(done), later)
            done.append(1)

    def visit(rows):
        inputs = features_ref[rows, :].astype(F32)
        unit = standardize(inputs)[0]
        normed_ref[rows, :] = (unit * gain_first).astype(BF16)
        total = jnp.zeros(inputs.shape, F32)
        for at in range(0, hidden_width, width):
            cols = slice(at, at + width)
            lead = (slice(None),) * (bit_count + 2)
            up = up_ref[lead + (cols,)].reshape(width, width)
            values = product(normed_ref[rows, :], up)
            hidden_ref[rows, cols] = values.astype(BF16)
            owners = width * (1 << bit_count) // hidden_width
            first = at * (1 << bit_count) // hidden_width
            parts = []
            for owner in range(first, first + owners):
                index = tuple((owner >> bit) & 1 for bit in range(bit_count - 1, -1, -1))
                parts.append(down_ref[index].reshape(width // owners, width))
            down = jnp.concatenate(parts, axis=0)
            total = total + product(swish_act(values).astype(BF16), down)
        after = inputs + 0.5 * total
        after_ref[rows, :] = after
        attend_ref[rows, :] = (standardize(after)[0] * gain_attend).astype(BF16)

    loop_rows(count, visit, between, 272)
    while len(done) < bit_count:
        between()
    work.finish(later)


FIRST_PLAN = [
    (2, 0, 0, 16),
    (0, 0, 0, 5),
    (0, 1, 5, 10),
    (0, 2, 10, 16),
    (1, 0, 0, 4),
    (1, 1, 4, 8),
    (1, 2, 8, 16),
    (3, 0, 0, 11),
    (3, 1, 11, 16),
    (4, 1, 0, 16),
    (5, 2, 0, 16),
    (6, 2, 0, 16),
]


def first_stage(features, frame_times, shards, collective_id):
    count, width = features.shape
    bit_count = (lax.axis_size("shard") - 1).bit_length()
    ins = [halves(array) for array in shards]
    pieces = plan_pieces([array.shape[1:] for array in ins], FIRST_PLAN)
    groups = {
        "arrays": list(range(len(ins))),
        "soon": [p for p, piece in enumerate(pieces) if piece.array < 3],
        "later": [p for p, piece in enumerate(pieces) if piece.array >= 3],
    }
    half_width = width // 2
    frequency = jnp.exp(
        jnp.arange(half_width, dtype=jnp.float32) * (-math.log(10000.0) / half_width)
    )
    lead = (2,) * bit_count
    vmem = pl.BlockSpec(memory_space=pltpu.VMEM)
    whole = pl.BlockSpec(memory_space=pl.ANY)
    hidden_width = shards[0].shape[1]
    outs = pl.pallas_call(
        functools.partial(first_kernel, bit_count, pieces, groups),
        in_specs=[vmem] * 3 + [whole] * len(ins),
        out_specs=[vmem] * 10 + [whole] * (len(ins) - 3),
        out_shape=[
            jax.ShapeDtypeStruct((count, width), BF16),
            jax.ShapeDtypeStruct((count, hidden_width), BF16),
            jax.ShapeDtypeStruct((count, width), F32),
            jax.ShapeDtypeStruct((count, width), BF16),
            jax.ShapeDtypeStruct((count, half_width), F32),
            jax.ShapeDtypeStruct((count, half_width), F32),
            jax.ShapeDtypeStruct((128, width), F32),
        ]
        + [jax.ShapeDtypeStruct(lead + array.shape, BF16) for array in ins],
        scratch_shapes=Gather.scratch(bit_count, pieces, len(ins)),
        compiler_params=pltpu.CompilerParams(
            collective_id=collective_id,
            has_side_effects=True,
            vmem_limit_bytes=56 * 1024 * 1024,
        ),
        cost_estimate=pl.CostEstimate(
            flops=5000000000, bytes_accessed=30000000, transcendentals=3000000
        ),
    )(features, frame_times.reshape(count, 1), frequency[None], *ins)
    fulls = [out.reshape(-1, array.shape[1]) for out, array in zip(outs[7:], shards)]
    return outs[:7], fulls


def first_stage_apart(features, frame_times, shards, collective_id):
    count, width = features.shape
    fulls = gather_arrays(shards, FIRST_PLAN, collective_id)
    rows = fulls[2].T.astype(F32)
    inputs = features.astype(F32)
    first_out, (normed_first, hidden, _) = feed_forward(inputs, rows[0], fulls[0], fulls[1])
    after_first = inputs + 0.5 * first_out
    normed_attend = normalize(after_first, rows[1]).astype(BF16)
    sine_flat, cos_flat = wave_table(frame_times.reshape(count), width)
    return (
        normed_first, hidden, after_first, normed_attend, sine_flat, cos_flat, rows
    ), fulls


def tail_kernel(bit_count, pieces, groups, shapes, *refs):
    (
        gq_ref, gk_ref, gv_ref, attend_ref, after_ref, stream_ref, first_ref, features_ref,
        hidden_ref, gains_ref, joint_ref, up_ref, down_ref, bias_ref, conv_gain_ref, middle_ref,
        taps_ref, place_ref, out_w_ref,
    ) = refs[:19]
    grad_ref = refs[19]
    owned = refs[20:26]
    refs = refs[26:]
    (
        joint_grad, down_grad, up_grad, small_grad, stream, low, small_ref, active, normed_grad, sums,
    ) = refs[:10]
    ins = [up_grad, down_grad, joint_grad, place_ref, out_w_ref, small_grad]
    work = Scatter(bit_count, pieces, ins, owned, refs[10:])
    count, width = stream.shape
    hidden_width = hidden_ref.shape[1]
    chunk = width
    stages = {}

    def begin(name):
        work.start(groups[name])
        stages[name] = 0

    def tick(*names):
        for name in names:
            stage = stages[name]
            if stage == 0:
                work.add_pair(groups[name])
            elif stage <= bit_count:
                work.advance(stage - 1, groups[name])
            stages[name] = stage + 1

    greet(bit_count)
    for part, source in enumerate((gq_ref, gk_ref, gv_ref)):
        store_blocks(
            joint_grad,
            product_left(attend_ref[...], source[...]),
            slice(part * width, (part + 1) * width),
        )
    begin("joint")
    sums[...] = jnp.zeros_like(sums)
    gain_first, gain_attend = gains_ref[0:1, :], gains_ref[1:2, :]

    def attend_back(rows):
        unit, spread = standardize(after_ref[rows, :])
        grad = product_right(gq_ref[rows, :], joint_ref[:, :width])
        grad = grad + product_right(gk_ref[rows, :], joint_ref[:, width : 2 * width])
        grad = grad + product_right(gv_ref[rows, :], joint_ref[:, 2 * width :])
        sums[1:2, :] = sums[1:2, :] + jnp.sum(grad * unit, axis=0, keepdims=True)
        total = stream_ref[rows, :] + standardize_back(grad * gain_attend, unit, spread)
        stream[rows, :] = total
        low[rows, :] = (0.5 * total).astype(BF16)

    loop_rows(count, attend_back)
    tick("joint")
    for at in range(0, hidden_width, chunk):
        hidden = hidden_ref[:, at : at + chunk].astype(F32)
        active[...] = (hidden * jax.nn.sigmoid(hidden)).astype(BF16)
        piece = product_left(active[...], low[...])
        lead = down_grad.shape[:-2]
        blocks = chunk * (1 << bit_count) // hidden_width
        first = at * (1 << bit_count) // hidden_width
        depth = hidden_width >> (bit_count + 1)
        for n in range(blocks):
            owner = first + n
            index = tuple((owner >> bit) & 1 for bit in range(bit_count - 1, -1, -1))
            for half in range(2):
                start = (2 * n + half) * depth
                down_grad[index + (half,)] = piece[start : start + depth].astype(BF16)
    begin("down")
    tick("joint")
    for number, at in enumerate(range(0, hidden_width, chunk)):
        cols = slice(at, at + chunk)

        def hidden_back(rows):
            hidden = hidden_ref[rows, cols].astype(F32)
            grad = product_right(low[rows, :], down_ref[cols, :])
            grad_low = (grad * swish_slope(hidden)).astype(BF16)
            active[rows, :] = grad_low
            piece = product_right(grad_low, up_ref[:, cols])
            if number == 0:
                normed_grad[rows, :] = piece
            else:
                normed_grad[rows, :] = normed_grad[rows, :] + piece

        loop_rows(count, hidden_back)
        store_blocks(up_grad, product_left(first_ref[...], active[...]), cols)
        if number < 2:
            tick("joint", "down")
        elif number == 2:
            tick("down")
    begin("up")
    tick("joint", "down")

    def first_back(rows):
        unit, spread = standardize(features_ref[rows, :].astype(F32))
        grad = normed_grad[rows, :]
        sums[0:1, :] = sums[0:1, :] + jnp.sum(grad * unit, axis=0, keepdims=True)
        total = stream[rows, :] + standardize_back(grad * gain_first, unit, spread)
        grad_ref[rows, :] = total.astype(BF16)

    loop_rows(count, first_back)
    small_ref[...] = jnp.zeros_like(small_ref)
    small_ref[0:2, :] = sums[0:2, :]
    small_ref[2:4, :] = bias_ref[0:2, :]
    small_ref[4:5, :] = conv_gain_ref[...]
    small_ref[7:9, :] = middle_ref[5:7, :]
    small_ref[9:41, :] = jnp.sum(taps_ref[...], axis=0)
    small = small_ref[...]
    store_blocks(small_grad, small.T, slice(0, small.shape[0]))
    begin("small")
    for _ in range(bit_count + 1):
        tick("joint", "down", "up", "small")
    work.finish()


TAIL_PLAN = [
    ("joint", (3, 1, 0, 16)),
    ("joint", (4, 2, 0, 16)),
    ("joint", (2, 0, 0, 7)),
    ("joint", (2, 1, 7, 11)),
    ("joint", (2, 2, 11, 16)),
    ("down", (1, 0, 0, 4)),
    ("down", (1, 1, 4, 8)),
    ("down", (1, 2, 8, 16)),
    ("up", (0, 0, 0, 5)),
    ("up", (0, 1, 5, 10)),
    ("up", (0, 2, 10, 16)),
    ("small", (5, 0, 0, 16)),
]


def tail(
    attend_grads, normed_attend, after_first, grad_stream, normed_first, features, hidden, gains,
    joint_full, up_full, down_full, rows, taps, grad_place, grad_out, collective_id,
):
    shards = lax.axis_size("shard")
    bit_count = (shards - 1).bit_length()
    lead = (2,) * bit_count
    count, width = after_first.shape
    hidden_width = up_full.shape[1]

    def blocks(rows, cols):
        return lead + (2, rows // (2 * shards), cols)

    given = [array.reshape(blocks(*array.shape)) for array in (grad_place, grad_out)]
    shapes = [
        blocks(width, hidden_width),
        blocks(hidden_width, width),
        blocks(width, 3 * width),
        given[0].shape,
        given[1].shape,
        blocks(width, 128),
    ]
    pieces, groups = [], {}
    for name, wanted in TAIL_PLAN:
        for piece in plan_pieces([shape[-2:] for shape in shapes], [wanted]):
            groups.setdefault(name, []).append(len(pieces))
            pieces.append(piece)
    vmem = pl.BlockSpec(memory_space=pltpu.VMEM)
    outs = pl.pallas_call(
        functools.partial(tail_kernel, bit_count, pieces, groups, shapes),
        in_specs=[vmem] * 17 + [pl.BlockSpec(memory_space=pl.ANY)] * 2,
        out_specs=[vmem] * 7,
        out_shape=[jax.ShapeDtypeStruct((count, width), BF16)]
        + [jax.ShapeDtypeStruct((2,) + shape[-2:], BF16) for shape in shapes],
        scratch_shapes=[
            pltpu.VMEM(shapes[2], BF16),
            pltpu.VMEM(shapes[1], BF16),
            pltpu.VMEM(shapes[0], BF16),
            pltpu.VMEM(shapes[5], BF16),
            pltpu.VMEM((count, width), F32),
            pltpu.VMEM((count, width), BF16),
            pltpu.VMEM((128, width), F32),
            pltpu.VMEM((count, width), BF16),
            pltpu.VMEM((count, width), F32),
            pltpu.VMEM((8, width), F32),
        ]
        + Scatter.scratch(bit_count, pieces),
        compiler_params=pltpu.CompilerParams(
            collective_id=collective_id,
            has_side_effects=True,
            vmem_limit_bytes=60 * 1024 * 1024,
        ),
        cost_estimate=pl.CostEstimate(
            flops=13000000000, bytes_accessed=40000000, transcendentals=5000000
        ),
    )(
        *attend_grads, normed_attend, after_first, grad_stream, normed_first, features, hidden,
        gains, joint_full, up_full, down_full, *rows, taps, *given,
    )
    return outs[0], outs[1:]


def widen_kernel(count, row_total, tap_total, *refs):
    ins, extra_ref, grad_ref = refs[:count], refs[count], refs[count + 1]
    outs, grad_out_ref = refs[count + 2 : -1], refs[-1]
    grad_out_ref[...] = grad_ref[...]
    for source, target in zip(ins[:-1], outs[:-2]):
        target[...] = source[...].astype(F32)
    small = ins[-1][...].astype(F32).T
    outs[-2][...] = small[:row_total] + extra_ref[...]
    outs[-1][...] = small[row_total : row_total + tap_total]


def widen(sums, extra_rows, tap_total, grad_inputs):
    sums = [total.reshape(-1, total.shape[-1]) for total in sums]
    replicas = lax.axis_size("replica")
    if replicas > 2:
        groups = [list(range(core, replicas, 2)) for core in range(2)]
        sums = [lax.psum(total, "replica", axis_index_groups=groups) for total in sums]
    row_total, depth = extra_rows.shape
    shapes = [total.shape for total in sums[:-1]] + [(row_total, depth), (tap_total, depth)]

    def whole(shape):
        return pl.BlockSpec(shape, lambda i: (0,) * len(shape))

    args = (*sums, extra_rows, grad_inputs)
    return pl.pallas_call(
        functools.partial(widen_kernel, len(sums), row_total, tap_total),
        grid=(1,),
        in_specs=[whole(arg.shape) for arg in args],
        out_specs=[whole(shape) for shape in shapes] + [whole(grad_inputs.shape)],
        out_shape=[jax.ShapeDtypeStruct(shape, F32) for shape in shapes]
        + [jax.ShapeDtypeStruct(grad_inputs.shape, BF16)],
        compiler_params=pltpu.CompilerParams(vmem_limit_bytes=32 * 1024 * 1024),
    )(*args)


def combine_sums(tiles):
    return jnp.sum(tiles, axis=0)


def combine_stats(local_count, tiles):
    half = tiles.shape[1] // 2
    means = tiles[:, :half]
    mean = jnp.sum(means, axis=0) * (1.0 / tiles.shape[0])
    apart = means - mean
    total = jnp.sum(tiles[:, half:] + local_count * (apart * apart), axis=0)
    return jnp.concatenate([mean, total * (1.0 / (local_count * tiles.shape[0]))], axis=0)


class Everyone:
    def __init__(self):
        self.shards = lax.axis_size("shard")
        self.count = self.shards * lax.axis_size("replica")
        self.me = lax.axis_index("replica") * self.shards + lax.axis_index("shard")

    def place(self, far):
        device = lax.rem(self.me + far, self.count)
        return (lax.div(device, self.shards), lax.rem(device, self.shards))

    def greet(self):
        barrier = pltpu.get_barrier_semaphore()

        def hello(far, carry):
            pl.semaphore_signal(barrier, inc=1, device_id=self.place(far), device_id_type=MESH)
            return carry

        lax.fori_loop(1, self.count, hello, 0)
        pl.semaphore_wait(barrier, self.count - 1)

    def copy(self, buffers, far, slot):
        tile, held, send_sem, recv_sem = buffers
        return pltpu.make_async_remote_copy(
            tile,
            held.at[slot],
            send_sem.at[far],
            recv_sem.at[far],
            device_id=self.place(far),
            device_id_type=MESH,
        )

    def send(self, buffers):
        tile, held = buffers[:2]

        def go(far, carry):
            self.copy(buffers, far, self.me).start()
            return carry

        lax.fori_loop(1, self.count, go, 0)
        held[self.me] = tile[...]

    def receive(self, buffers):
        def arrive(far, carry):
            self.copy(buffers, far, lax.rem(self.me + self.count - far, self.count)).wait_recv()
            return carry

        lax.fori_loop(1, self.count, arrive, 0)

    def close(self, buffers):
        def sent(far, carry):
            self.copy(buffers, far, self.me).wait_send()
            return carry

        lax.fori_loop(1, self.count, sent, 0)

    def scratch(self, rows):
        return [
            pltpu.VMEM((rows, 128), F32),
            pltpu.VMEM((self.count, rows, 128), F32),
            pltpu.SemaphoreType.DMA((self.count,)),
            pltpu.SemaphoreType.DMA((self.count,)),
        ]


def rows_to_tile(tile_ref, *rows):
    at = 0
    for row in rows:
        for start in range(0, row.shape[1], 128):
            tile_ref[at : at + 1, :] = row[:, start : start + 128]
            at += 1


def tile_to_row(tile, start, width):
    return jnp.concatenate(
        [tile[at : at + 1] for at in range(start, start + width // 128)], axis=1
    )


def middle_kernel(clip_length, *refs):
    (
        conv_ref, after_ref, cotangent_ref, gains_ref, stats_ref, point_ref, up_ref, down_ref,
    ) = refs[:8]
    (
        out_ref, shaped_grad_ref, stream_ref, rows_ref, totals_ref,
        point_grad_ref, up_grad_ref, down_grad_ref,
    ) = refs[8:16]
    active_conv, normed, active, back, low, low_conv, hidden, sums = refs[16:24]
    stats_buffers, sums_buffers = refs[24:28], refs[28:32]
    count, width = out_ref.shape
    hidden_width = up_ref.shape[1]
    everyone = Everyone()
    tokens = count * everyone.count

    everyone.greet()
    clips = stats_ref.shape[0]
    mean = sum(stats_ref[clip, 0:1, :] for clip in range(clips)) * (1.0 / clips)
    squares = jnp.zeros_like(mean)
    for clip in range(clips):
        apart = stats_ref[clip, 0:1, :] - mean
        squares = squares + stats_ref[clip, 1:2, :] + clip_length * (apart * apart)
    rows_to_tile(stats_buffers[0], mean, squares)
    everyone.send(stats_buffers)
    sums[...] = jnp.zeros_like(sums)
    everyone.receive(stats_buffers)
    tile = combine_stats(count, stats_buffers[1][...])
    mean = tile_to_row(tile, 0, width)
    inverse = lax.rsqrt(tile_to_row(tile, width // 128, width) + epsilon)
    scale, shift = gains_ref[5:6, :], gains_ref[6:7, :]
    gain_second, gain_final = gains_ref[7:8, :], gains_ref[8:9, :]

    def visit(rows):
        unit = (conv_ref[rows, :] - mean) * inverse
        shaped = unit * scale + shift
        active_conv[rows, :] = swish_act(shaped).astype(BF16)
        after_conv = after_ref[rows, :] + product(active_conv[rows, :], point_ref[...])
        unit_second, spread_second = standardize(after_conv)
        normed[rows, :] = (unit_second * gain_second).astype(BF16)
        total = jnp.zeros(after_conv.shape, F32)
        for at in range(0, hidden_width, width):
            cols = slice(at, at + width)
            values = product(normed[rows, :], up_ref[:, cols])
            hidden[:, cols] = values
            active[rows, cols] = swish_act(values).astype(BF16)
            total = total + product(active[rows, cols], down_ref[cols, :])
        unit_last, spread_last = standardize(after_conv + 0.5 * total)
        out_ref[rows, :] = (unit_last * gain_final).astype(BF16)
        grad = cotangent_ref[rows, :].astype(F32)
        sums[1:2, :] = sums[1:2, :] + jnp.sum(grad * unit_last, axis=0, keepdims=True)
        last = standardize_back(grad * gain_final, unit_last, spread_last)
        low[rows, :] = (0.5 * last).astype(BF16)
        total = jnp.zeros(after_conv.shape, F32)
        for at in range(0, hidden_width, width):
            cols = slice(at, at + width)
            grad = product_right(low[rows, :], down_ref[cols, :])
            back[rows, cols] = (grad * swish_slope(hidden[:, cols])).astype(BF16)
            total = total + product_right(back[rows, cols], up_ref[:, cols])
        sums[0:1, :] = sums[0:1, :] + jnp.sum(total * unit_second, axis=0, keepdims=True)
        stream = last + standardize_back(total * gain_second, unit_second, spread_second)
        stream_ref[rows, :] = stream
        low_conv[rows, :] = stream.astype(BF16)
        grad = product_right(low_conv[rows, :], point_ref[...]) * swish_slope(shaped)
        shaped_grad_ref[rows, :] = grad
        sums[2:3, :] = sums[2:3, :] + jnp.sum(grad, axis=0, keepdims=True)
        sums[3:4, :] = sums[3:4, :] + jnp.sum(grad * unit, axis=0, keepdims=True)

    loop_rows(count, visit)
    rows_to_tile(sums_buffers[0], sums[2:3, :], sums[3:4, :])
    everyone.send(sums_buffers)
    point_grad_ref[...] = product_left(active_conv[...], low_conv[...]).astype(BF16)
    for at in range(0, hidden_width, width):
        cols = slice(at, at + width)
        down_grad_ref[cols, :] = product_left(active[:, cols], low[...]).astype(BF16)
        up_grad_ref[:, cols] = product_left(normed[...], back[:, cols]).astype(BF16)
    everyone.receive(sums_buffers)
    tile = combine_sums(sums_buffers[1][...])
    shift_total = tile_to_row(tile, 0, width)
    gain_total = tile_to_row(tile, width // 128, width)
    rows_ref[0:1, :] = mean
    rows_ref[1:2, :] = inverse
    rows_ref[2:3, :] = scale * inverse
    rows_ref[3:4, :] = shift_total * (1.0 / tokens)
    rows_ref[4:5, :] = gain_total * (1.0 / tokens)
    rows_ref[5:7, :] = sums[0:2, :]
    rows_ref[7:8, :] = jnp.zeros_like(mean)
    totals_ref[...] = jnp.zeros_like(totals_ref)
    totals_ref[5:6, :] = gain_total
    totals_ref[6:7, :] = shift_total
    everyone.close(stats_buffers)
    everyone.close(sums_buffers)


def middle(
    conv_flat, after_attend, cotangent, gains, clip_stats, point_full, up_full, down_full,
    clip_length, collective_id,
):
    count, width = after_attend.shape
    hidden_width = up_full.shape[1]
    everyone = Everyone()
    vmem = pl.BlockSpec(memory_space=pltpu.VMEM)
    tile_rows_count = 2 * width // 128
    return pl.pallas_call(
        functools.partial(middle_kernel, clip_length),
        in_specs=[vmem] * 8,
        out_specs=[vmem] * 8,
        out_shape=[
            jax.ShapeDtypeStruct((count, width), BF16),
            jax.ShapeDtypeStruct((count, width), F32),
            jax.ShapeDtypeStruct((count, width), F32),
            jax.ShapeDtypeStruct((8, width), F32),
            jax.ShapeDtypeStruct((16, width), F32),
            jax.ShapeDtypeStruct((width, width), BF16),
            jax.ShapeDtypeStruct((width, hidden_width), BF16),
            jax.ShapeDtypeStruct((hidden_width, width), BF16),
        ],
        scratch_shapes=[
            pltpu.VMEM((count, width), BF16),
            pltpu.VMEM((count, width), BF16),
            pltpu.VMEM((count, hidden_width), BF16),
            pltpu.VMEM((count, hidden_width), BF16),
            pltpu.VMEM((count, width), BF16),
            pltpu.VMEM((count, width), BF16),
            pltpu.VMEM((row_step(count), hidden_width), F32),
            pltpu.VMEM((8, width), F32),
        ]
        + everyone.scratch(tile_rows_count)
        + everyone.scratch(tile_rows_count),
        compiler_params=pltpu.CompilerParams(
            collective_id=collective_id,
            has_side_effects=True,
            vmem_limit_bytes=60 * 1024 * 1024,
        ),
        cost_estimate=pl.CostEstimate(
            flops=15500000000, bytes_accessed=25000000, transcendentals=10000000
        ),
    )(conv_flat, after_attend, cotangent, gains, clip_stats, point_full, up_full, down_full)


def tap_windows(padded_ref, start, rows, visit):
    for shift in range(8):
        window = padded_ref[start + shift : start + shift + rows + 24, :]
        for lift in range(4):
            offset = 8 * lift + shift
            if offset > 0:
                visit(offset, window[8 * lift : 8 * lift + rows])


def fill_padded(padded_ref, values):
    length = values.shape[0]
    edge = jnp.zeros((16, values.shape[1]), F32)
    padded_ref[0:16, :] = edge
    padded_ref[16 : 16 + length, :] = values
    padded_ref[16 + length : 32 + length, :] = edge


def tile_rows(length):
    for rows in (136, 128, 120, 112, 104, 96, 88, 80, 72, 64, 56, 48, 40, 32, 24, 16, 8):
        if length % rows == 0:
            return rows
    return length


def conv_forward_kernel(linear_ref, gate_ref, taps_ref, out_ref, stats_ref, padded_ref):
    length = out_ref.shape[1]
    rows = tile_rows(length)
    fill_padded(padded_ref, linear_ref[0] * jax.nn.sigmoid(gate_ref[0]))
    for start in range(0, length, rows):
        total = [jnp.zeros((rows, out_ref.shape[2]), F32)]

        def visit(offset, window):
            total[0] = total[0] + taps_ref[offset - 1 : offset, :] * window

        tap_windows(padded_ref, start, rows, visit)
        out_ref[0, start : start + rows, :] = total[0]
    values = out_ref[0]
    mean = jnp.sum(values, axis=0, keepdims=True) * (1.0 / length)
    apart = values - mean
    squares = jnp.sum(apart * apart, axis=0, keepdims=True)
    at_row = lax.broadcasted_iota(jnp.int32, stats_ref.shape[1:], 0)
    stats_ref[0] = jnp.where(at_row == 0, mean, jnp.where(at_row == 1, squares, 0.0))


def conv_forward(mixed_clips, taps):
    clip_count, clip_length, width = mixed_clips.shape
    channels = width // 2
    blocks = channels // 128
    piece = pl.BlockSpec((1, clip_length, 128), lambda i, j: (i, 0, j))
    return pl.pallas_call(
        conv_forward_kernel,
        grid=(clip_count, blocks),
        in_specs=[
            piece,
            pl.BlockSpec((1, clip_length, 128), lambda i, j: (i, 0, blocks + j)),
            pl.BlockSpec((taps.shape[0], 128), lambda i, j: (0, j)),
        ],
        out_specs=[piece, pl.BlockSpec((1, 8, 128), lambda i, j: (i, 0, j))],
        out_shape=[
            jax.ShapeDtypeStruct((clip_count, clip_length, channels), F32),
            jax.ShapeDtypeStruct((clip_count, 8, channels), F32),
        ],
        scratch_shapes=[pltpu.VMEM((clip_length + 32, 128), F32)],
        compiler_params=pltpu.CompilerParams(vmem_limit_bytes=32 * 1024 * 1024),
        cost_estimate=pl.CostEstimate(
            flops=80000000, bytes_accessed=8000000, transcendentals=600000
        ),
    )(mixed_clips, mixed_clips, taps)


def conv_backward_kernel(
    linear_ref, gate_ref, grad_ref, conv_ref, rows_ref, taps_ref,
    out_ref, grad_taps_ref, padded_ref, grad_padded_ref, tap_sums_ref,
):
    length = grad_ref.shape[1]
    rows = tile_rows(length)
    block = pl.program_id(1)
    channels = out_ref.shape[2] // 2
    mean, inverse, scale = rows_ref[0:1, :], rows_ref[1:2, :], rows_ref[2:3, :]
    shift_mean, gain_mean = rows_ref[3:4, :], rows_ref[4:5, :]
    unit = (conv_ref[0] - mean) * inverse
    grad_conv = scale * (grad_ref[0] - shift_mean - unit * gain_mean)
    fill_padded(grad_padded_ref, grad_conv)
    fill_padded(padded_ref, linear_ref[0] * jax.nn.sigmoid(gate_ref[0]))
    tap_sums_ref[...] = jnp.zeros_like(tap_sums_ref)
    first = pl.multiple_of(block * 128, 128)
    second = pl.multiple_of(channels + block * 128, 128)
    for start in range(0, length, rows):
        grad_rows = grad_padded_ref[16 + start : 16 + start + rows, :]

        def visit(offset, window):
            product_rows = (grad_rows * window).reshape(rows // 8, 8, window.shape[1])
            tap_sums_ref[offset - 1] = tap_sums_ref[offset - 1] + jnp.sum(product_rows, axis=0)

        tap_windows(padded_ref, start, rows, visit)
        total = [jnp.zeros((rows, 128), F32)]

        def visit_back(offset, window):
            total[0] = total[0] + taps_ref[31 - offset : 32 - offset, :] * window

        tap_windows(grad_padded_ref, start, rows, visit_back)
        grad_gated = total[0]
        gate = jax.nn.sigmoid(gate_ref[0, start : start + rows, :])
        grad_linear = grad_gated * gate
        linear = linear_ref[0, start : start + rows, :]
        out_ref[0, start : start + rows, pl.ds(first, 128)] = grad_linear.astype(BF16)
        out_ref[0, start : start + rows, pl.ds(second, 128)] = (
            grad_linear * linear * (1.0 - gate)
        ).astype(BF16)
    grad_taps_ref[0] = jnp.sum(tap_sums_ref[...], axis=1)


def conv_backward(mixed_clips, grad_clips, conv_clips, rows, taps):
    clip_count, clip_length, width = mixed_clips.shape
    channels = width // 2
    blocks = channels // 128
    piece = pl.BlockSpec((1, clip_length, 128), lambda i, j: (i, 0, j))
    return pl.pallas_call(
        conv_backward_kernel,
        grid=(clip_count, blocks),
        in_specs=[
            piece,
            pl.BlockSpec((1, clip_length, 128), lambda i, j: (i, 0, blocks + j)),
            piece,
            piece,
            pl.BlockSpec((8, 128), lambda i, j: (0, j)),
            pl.BlockSpec((taps.shape[0], 128), lambda i, j: (0, j)),
        ],
        out_specs=[
            pl.BlockSpec((1, clip_length, width), lambda i, j: (i, 0, 0)),
            pl.BlockSpec((1, 32, 128), lambda i, j: (i, 0, j)),
        ],
        out_shape=[
            jax.ShapeDtypeStruct((clip_count, clip_length, width), BF16),
            jax.ShapeDtypeStruct((clip_count, 32, channels), F32),
        ],
        scratch_shapes=[
            pltpu.VMEM((clip_length + 32, 128), F32),
            pltpu.VMEM((clip_length + 32, 128), F32),
            pltpu.VMEM((32, 8, 128), F32),
        ],
        compiler_params=pltpu.CompilerParams(vmem_limit_bytes=32 * 1024 * 1024),
        cost_estimate=pl.CostEstimate(
            flops=160000000, bytes_accessed=14000000, transcendentals=1200000
        ),
    )(mixed_clips, mixed_clips, grad_clips, conv_clips, rows, taps)


LATE_PLAN = [
    (2, 0, 0, 4),
    (2, 1, 4, 8),
    (2, 2, 8, 16),
    (1, 0, 0, 5),
    (1, 1, 5, 11),
    (1, 2, 11, 16),
    (0, 0, 0, 8),
    (0, 1, 8, 14),
    (0, 2, 14, 16),
]
LATE_BACK_PLAN = [
    (3, 0, 0, 4),
    (3, 1, 4, 8),
    (3, 2, 8, 16),
    (2, 0, 0, 5),
    (2, 1, 5, 11),
    (2, 2, 11, 16),
    (0, 0, 0, 4),
    (0, 1, 4, 12),
    (0, 2, 12, 16),
    (1, 0, 0, 16),
]


def body(
    features,
    frame_times,
    cotangent,
    vectors,
    first_up,
    first_down,
    query_key_value,
    place_weight,
    out_weight,
    point_glu,
    depth_taps,
    point_out,
    second_up,
    second_down,
):
    clip_count, clip_length, model_width = features.shape
    row_count = clip_count * clip_length
    row_total = vectors.shape[0]
    tap_total = depth_taps.shape[0]

    small_shard = pack_small([vectors.T, depth_taps.T])
    early_shards = [
        first_up,
        first_down,
        small_shard,
        query_key_value,
        place_weight,
        out_weight,
        point_out,
    ]
    stage = first_stage if first_up.shape[0] % 32 == 0 else first_stage_apart
    first_values, fulls = stage(
        features.reshape(row_count, model_width), frame_times, early_shards, 1
    )
    normed_first, hidden_first, after_first, normed_attend, sine_flat, cos_flat, gains = (
        first_values
    )
    up_one, down_one, _, joint_full, place_full, out_full, point_full = fulls
    joint_rows = product(normed_attend, joint_full)
    joint_clips = joint_rows.reshape(clip_count, clip_length, 3 * model_width)
    attend_parts = attention_inputs(joint_clips, gains, model_width)
    sine_rows = sine_flat.reshape(clip_count, clip_length, -1)
    cosines = cos_flat.reshape(clip_count, clip_length, -1)
    context_clips, probs, late_full = attention_forward(
        attend_parts,
        place_full,
        sine_rows,
        cosines,
        [point_glu, second_up, second_down],
        LATE_PLAN,
        2,
    )
    glu_full = late_full[0]
    context_low = context_clips.reshape(row_count, model_width)
    after_attend = after_first + product(context_low, out_full)
    normed_conv = normalize(after_attend, gains[4]).astype(jnp.bfloat16)
    mixed_rows = product(normed_conv, glu_full).reshape(
        clip_count, clip_length, 2 * model_width
    )
    taps = gains[row_total : row_total + 32]
    conv_clips, clip_stats = conv_forward(mixed_rows, taps)
    conv_flat = conv_clips.reshape(row_count, model_width)
    (
        output,
        grad_shaped,
        grad_conv_out,
        middle_rows,
        batch_grads,
        grad_point_out,
        grad_second_up,
        grad_second_down,
    ) = middle(
        conv_flat,
        after_attend,
        cotangent.reshape(row_count, model_width),
        gains,
        clip_stats,
        point_full,
        late_full[1],
        late_full[2],
        clip_length,
        3,
    )
    grad_mixed_clips, clip_taps = conv_backward(
        mixed_rows,
        grad_shaped.reshape(clip_count, clip_length, model_width),
        conv_clips,
        middle_rows,
        taps,
    )
    grad_mixed_low = grad_mixed_clips.reshape(row_count, 2 * model_width)
    grad_point_glu = product_left(normed_conv, grad_mixed_low)
    grad_extra, grad_conv_gain = normalize_back(
        after_attend, gains[4], product_right(grad_mixed_low, glu_full)
    )
    grad_attend_out = grad_conv_out + grad_extra
    grad_low = grad_attend_out.astype(jnp.bfloat16)
    grad_out_weight = product_left(context_low, grad_low)
    grad_context = (
        product_right(grad_low, out_full)
        .astype(jnp.bfloat16)
        .reshape(clip_count, clip_length, model_width)
    )
    attend_grads, late_sums = attention_backward(
        attend_parts,
        grad_context,
        place_full,
        sine_rows,
        cosines,
        probs,
        [
            array.astype(BF16)
            for array in (grad_point_glu, grad_point_out, grad_second_up, grad_second_down)
        ],
        LATE_BACK_PLAN,
        5,
    )
    grad_query, grad_key, grad_value, grad_bias, grad_place = attend_grads
    attend_low = [
        array.reshape(row_count, model_width) for array in (grad_query, grad_key, grad_value)
    ]
    grad_inputs, early_sums = tail(
        attend_low,
        normed_attend,
        after_first,
        grad_attend_out,
        normed_first,
        features.reshape(row_count, model_width),
        hidden_first,
        gains,
        joint_full,
        up_one,
        down_one,
        [grad_bias, grad_conv_gain[None], middle_rows],
        clip_taps,
        grad_place.astype(BF16),
        grad_out_weight.astype(BF16),
        6,
    )
    shard_cols = vectors.shape[1]
    first_col = lax.axis_index("shard") * shard_cols
    batch_grads = lax.dynamic_slice_in_dim(
        batch_grads[:row_total], first_col, shard_cols, axis=1
    )
    summed = widen(
        [*early_sums[:5], *late_sums, early_sums[5]], batch_grads, tap_total, grad_inputs
    )
    return (
        output.reshape(clip_count, clip_length, model_width),
        summed[11].reshape(clip_count, clip_length, model_width),
        summed[9],
        *summed[:6],
        summed[10],
        *summed[6:9],
    )


def solution(mesh):
    return jax.shard_map(
        body,
        mesh=mesh,
        in_specs=(
            P(("replica", "shard"), None, None),
            P(("replica", "shard"), None),
            P(("replica", "shard"), None, None),
            P(None, "shard"),
            P("shard", None),
            P("shard", None),
            P("shard", None),
            P("shard", None),
            P("shard", None),
            P("shard", None),
            P(None, "shard"),
            P("shard", None),
            P("shard", None),
            P("shard", None),
        ),
        out_specs=(
            P(("replica", "shard"), None, None),
            P(("replica", "shard"), None, None),
            P(None, "shard"),
            P("shard", None),
            P("shard", None),
            P("shard", None),
            P("shard", None),
            P("shard", None),
            P("shard", None),
            P(None, "shard"),
            P("shard", None),
            P("shard", None),
            P("shard", None),
        ),
        check_vma=False,
    )
```
